32 devices in a mesh: rows: 16 (over z, y, x), cols: 2 (over core).
Axes of the slice: x: 2, y: 2, z: 4, core: 2. Of those that a mesh axis runs over, the one named last changes fastest.
Arguments:
- descriptors: bfloat16 [51200, 1024], P('rows', 'cols'), may hold values from -6 to 6
- sparse_points: bfloat16 [4096, 1024], P('cols'), may hold values from -6 to 6
- block_weights: bfloat16 [400], P('rows'), may hold values from 0.29882812 to 3
- block_counts: int32 [16], replicated, may hold values from 1 to 25, as said below
- destinations: int32 [16, 25], replicated, may hold values from 0 to 15, as said below
Outputs:
- projected: float32 [256, 4096], P(None, 'cols')
- remainder: bfloat16 [26624, 4096], P('rows', 'cols')
The draws below stay inside these ranges and needn't reach their ends.
Inputs may be any that keep to these rules, and one draw needn't show every extreme that they name: Live blocks of owner s are slots 0 to block_counts[s] - 1; the counts sum to 208, and some owner holds 25. `destinations`: entries of live slots name the row owner of the block; every row owner receives exactly 13 live blocks, no owner sends more than 2 live block to one row owner, and entries of slots that are not live are not used.
All inputs are finite; a program needn't handle non-finite values.
Results may differ from the reference program's by a relative error of at most 0.0055.
Values may be sent and summed in bfloat16 or wider, within the bound.
No kernel may reach another device: no remote copies, remote signals or barrier semaphores. Data moves between devices by JAX's collectives and lax.ppermute only.
A program may use at most 128 MiB of HBM per device.

```python
import math
import jax
import jax.numpy as jnp
from jax import lax

DESC = 1024
M = 4096
PANEL = 256
BLK = 128
DST_BLK = 13
SRC_BLK = 25
LIVE = 26624
N_ROWS = 16


def draw_plan(key):
    base = jax.random.fold_in(key, 7)
    key_order, key_moves, key_label = jax.random.split(base, 3)
    shuffle = jax.random.permutation(key_order, N_ROWS).astype(jnp.int32)
    half_owners = N_ROWS // 2
    transfers = jax.random.randint(key_moves, (half_owners,), 0, DST_BLK).astype(jnp.int32)
    transfers = transfers.at[0].set(DST_BLK - 1)
    imbalance = jnp.zeros((N_ROWS,), jnp.int32).at[shuffle[0::2]].set(transfers)
    imbalance = imbalance.at[shuffle[1::2]].set(-transfers)
    counts = DST_BLK + imbalance
    first_index = jnp.cumsum(counts) - counts
    slot_ids = jnp.arange(SRC_BLK, dtype=jnp.int32)
    global_index = first_index[:, None] + slot_ids[None, :]
    relabel = jax.random.permutation(key_label, N_ROWS).astype(jnp.int32)
    targets = relabel[global_index % N_ROWS]
    return (counts.astype(jnp.int32), targets.astype(jnp.int32))


def draw_block_counts(key, part):
    return draw_plan(key)[0]


def draw_destinations(key, part):
    return draw_plan(key)[1]


def shard_levels(key, shape, cuts, low, largest):
    loudness = 1.0
    for position, blocks in cuts:
        steps = jax.random.uniform(jax.random.fold_in(jax.random.fold_in(key, 6), position), (blocks,), jnp.float32, low / len(cuts), largest / len(cuts))
        loudness = loudness * jnp.repeat(jnp.exp(steps), shape[position] // blocks).reshape((-1,) + (1,) * (len(shape) - 1 - position))
    return loudness


def scatter_about(stream_key, dims, scale, most, cuts=(), kind=jnp.bfloat16):
    result = jax.random.normal(stream_key, dims, jnp.float32) * scale
    if len(cuts) > 0:
        result = shard_levels(stream_key, dims, cuts, -0.22, 0.18) * result
    return jnp.clip(result, min=-most, max=most).astype(kind)


def setup_inputs(seed: int = 0) -> dict:
    seeds = jax.random.split(jax.random.key(seed), 6)
    descriptors = scatter_about(seeds[0], (N_ROWS * SRC_BLK * BLK, DESC), 1.0, 6.0, ((0, 16), (1, 2)))
    sparse_points = scatter_about(seeds[1], (M, DESC), 1.0, 6.0, ((0, 2),))
    block_weights = jnp.clip(jnp.exp(math.log(3.0) - 2.306499 * jax.random.uniform(seeds[2], (N_ROWS * SRC_BLK,), jnp.float32) ** shard_levels(seeds[2], (N_ROWS * SRC_BLK,), ((0, 16),), -0.2, 0.2)), 0.29882812, 3.0).astype(jnp.bfloat16)
    block_counts = draw_block_counts(jax.random.fold_in(seeds[5], 71), 0)
    destinations = draw_destinations(jax.random.fold_in(seeds[5], 71), 0)
    return dict(descriptors=descriptors, sparse_points=sparse_points, block_weights=block_weights, block_counts=block_counts, destinations=destinations)


EPSILON = 1e-06

def live_order(block_counts, destinations):
    owner_total = destinations.shape[0]
    slot_total = destinations.shape[1]
    slot_ids = jnp.arange(slot_total, dtype=jnp.int32)
    owner_ids = jnp.arange(owner_total, dtype=jnp.int32)
    is_live = slot_ids[None, :] < block_counts[:, None]
    sort_keys = destinations * (owner_total * slot_total) + owner_ids[:, None] * slot_total + slot_ids[None, :]
    sort_keys = jnp.where(is_live, sort_keys, owner_total * owner_total * slot_total + 1)
    return jnp.argsort(sort_keys.reshape(-1))[:owner_total * DST_BLK].astype(jnp.int32)

def reference(descriptors, sparse_points, block_weights, block_counts, destinations):
    arrival_order = live_order(block_counts, destinations)
    blocks = descriptors.reshape(N_ROWS * SRC_BLK, BLK, DESC)
    sparse_sq = lax.optimization_barrier(jnp.mean(sparse_points.astype(jnp.float32) ** 2, axis=1)) + EPSILON

    def one_block(block_index):
        block_rows = blocks[block_index]
        weight = block_weights[block_index].astype(jnp.float32)
        inner = jnp.dot(block_rows.astype(jnp.float32), sparse_points.T.astype(jnp.float32), preferred_element_type=jnp.float32)
        row_sq = lax.optimization_barrier(jnp.mean(block_rows.astype(jnp.float32) ** 2, axis=1)) + EPSILON
        return (weight * inner * inner / (DESC * row_sq[:, None] * sparse_sq[None, :])).astype(jnp.bfloat16)
    kernel = lax.map(one_block, arrival_order).reshape(LIVE, M)
    panel_rows = kernel[:, :PANEL].astype(jnp.float32)
    gram_matrix = jnp.dot(panel_rows.T, panel_rows, precision=lax.Precision.HIGHEST)
    lower_factor = jnp.linalg.cholesky(gram_matrix)
    basis_cols = lax.linalg.triangular_solve(lower_factor, panel_rows.T, left_side=True, lower=True)
    basis_rows = basis_cols.T
    projection = jnp.dot(basis_cols, kernel.astype(jnp.float32), precision=lax.Precision.HIGHEST)
    norm_factor = math.sqrt(LIVE)
    column = jnp.arange(M, dtype=jnp.int32)

    def one_rest(pieces):
        kernel_part, basis_part = pieces
        rest = kernel_part.astype(jnp.float32) - jnp.dot(basis_part, projection, precision=lax.Precision.HIGHEST)
        padded = jnp.pad(basis_part, ((0, 0), (0, M - PANEL))) * norm_factor
        return jnp.where(column[None, :] < PANEL, padded, rest).astype(jnp.bfloat16)
    remainder = lax.map(one_rest, (kernel.reshape(N_ROWS * DST_BLK, BLK, M), basis_rows.reshape(N_ROWS * DST_BLK, BLK, PANEL)))
    return (projection / norm_factor, remainder.reshape(LIVE, M))
```

```python
import functools
import math

import jax
import jax.numpy as jnp
from jax import lax
from jax.experimental import pallas as pl
from jax.experimental.pallas import tpu as pltpu
from jax.sharding import PartitionSpec as P

PANEL = 256
BLK = 128
DST_BLK = 13
EPSILON = 1e-06
VMEM_LIMIT = 56 * 1024 * 1024
HIGH = lax.Precision.HIGHEST
ANY = pl.BlockSpec(memory_space=pl.ANY)
SMEM = pl.BlockSpec(memory_space=pltpu.SMEM)


def params(**kw):
    return pltpu.CompilerParams(vmem_limit_bytes=VMEM_LIMIT, **kw)


def cost(flops, nbytes):
    return pl.CostEstimate(flops=int(flops), bytes_accessed=int(nbytes), transcendentals=0)


def nt(a, b):
    return lax.dot_general(a, b, (((1,), (1,)), ((), ())), preferred_element_type=jnp.float32)


def nn(a, b, precision=None):
    return lax.dot_general(
        a, b, (((1,), (0,)), ((), ())), preferred_element_type=jnp.float32, precision=precision
    )


def pack_kernel(per_pair, me_ref, dest_ref, cnt_ref, desc_ref, out_ref, ctr_ref, sems):
    slots = desc_ref.shape[0]
    owners = ctr_ref.shape[0]
    me = me_ref[0]
    count = cnt_ref[me]

    @pl.loop(0, owners)
    def _(i):
        ctr_ref[i] = 0

    def copy(j, slot):
        return pltpu.make_async_copy(desc_ref.at[j], out_ref.at[slot], sems.at[j])

    @pl.loop(0, slots)
    def _(j):
        @pl.when(j < count)
        def _():
            d = dest_ref[me, j]
            r = ctr_ref[d]
            ctr_ref[d] = r + 1
            copy(j, d * per_pair + r).start()

    @pl.loop(0, slots)
    def _(j):
        @pl.when(j < count)
        def _():
            pltpu.make_async_copy(desc_ref.at[0], out_ref.at[0], sems.at[j]).wait()


def pack(desc_blocks, me, destinations, counts, per_pair):
    slots, blk, feat = desc_blocks.shape
    owners = destinations.shape[0]
    return pl.pallas_call(
        functools.partial(pack_kernel, per_pair),
        out_shape=jax.ShapeDtypeStruct((owners * per_pair, blk, feat), desc_blocks.dtype),
        in_specs=[SMEM, SMEM, SMEM, ANY],
        out_specs=ANY,
        scratch_shapes=[pltpu.SMEM((owners,), jnp.int32), pltpu.SemaphoreType.DMA((slots,))],
        cost_estimate=cost(0, 4 * slots * blk * feat),
        name="pack",
    )(me, destinations, counts, desc_blocks)


def select_kernel(pos_ref, recv_ref, out_ref, sems):
    copies = [
        pltpu.make_async_copy(recv_ref.at[pos_ref[p]], out_ref.at[p], sems.at[p])
        for p in range(DST_BLK)
    ]
    for c in copies:
        c.start()
    for c in copies:
        c.wait()


def select(received, positions):
    _, blk, feat = received.shape
    return pl.pallas_call(
        select_kernel,
        out_shape=jax.ShapeDtypeStruct((DST_BLK, blk, feat), received.dtype),
        in_specs=[SMEM, ANY],
        out_specs=ANY,
        scratch_shapes=[pltpu.SemaphoreType.DMA((DST_BLK,))],
        cost_estimate=cost(0, 4 * DST_BLK * blk * feat),
        name="select",
    )(positions, received)


def share_parts(x):
    groups = lax.axis_size("cols")
    if groups == 2:
        peer = lax.ppermute(x, "cols", [(0, 1), (1, 0)])
        return [x, peer]
    full = lax.all_gather(x, "cols", axis=0, tiled=False)
    return [full[i] for i in range(groups)]


def part_offsets(feat):
    groups = lax.axis_size("cols")
    if groups == 2:
        c = lax.axis_index("cols")
        return jnp.stack([c * feat, (1 - c) * feat]).astype(jnp.int32)
    return jnp.arange(groups, dtype=jnp.int32) * feat


def inner_product(x_parts, rows, off_ref, s_ref):
    feat = x_parts[0].shape[1]
    total = None
    for i, ref in enumerate(x_parts):
        off = pl.multiple_of(off_ref[i], 128)
        term = nt(ref[rows, :], s_ref[:, pl.ds(off, feat)])
        total = term if total is None else total + term
    return total


def row_square(x_parts, rows):
    total = None
    for ref in x_parts:
        x = ref[rows, :].astype(jnp.float32)
        term = jnp.sum(x * x, axis=1, keepdims=True)
        total = term if total is None else total + term
    return total


def source_kernel(nparts, tile, cnt_ref, off_ref, w_ref, *refs):
    parts = refs[:nparts]
    sp_ref, csp_ref, s_ref, cs_ref, gram_ref, g_ref, pt_ref, rs_ref = refs[nparts:]
    width = parts[0].shape[1] * nparts
    rows_all = parts[0].shape[0]
    count = cnt_ref[0]
    step = pl.program_id(0)
    per = tile // BLK
    tiles = rows_all // tile

    @pl.when(step == 0)
    def _():
        gram_ref[...] = jnp.zeros_like(gram_ref)
        for t in range(tiles):
            @pl.when(t * per < count)
            def _():
                for b in range(per):
                    j = t * per + b
                    rows = pl.ds(j * BLK, BLK)
                    sq = row_square(parts, rows) / width + EPSILON
                    w = jnp.where(j < count, w_ref[j], 0.0)
                    rs_ref[rows, :] = w / sq
                rows = pl.ds(t * tile, tile)
                inner = inner_product(parts, rows, off_ref, sp_ref)
                panel = inner * inner * rs_ref[rows, :] * csp_ref[...]
                panel_t = panel.T.astype(jnp.bfloat16)
                pt_ref[t] = panel_t
                gram_ref[...] += nt(panel_t, panel_t)

    g_ref[...] = jnp.zeros_like(g_ref)
    for t in range(tiles):
        @pl.when(t * per < count)
        def _():
            rows = pl.ds(t * tile, tile)
            inner = inner_product(parts, rows, off_ref, s_ref)
            kern = (inner * inner * rs_ref[rows, :] * cs_ref[...]).astype(jnp.bfloat16)
            g_ref[...] += nn(pt_ref[t], kern)


def source_products(parts, offsets, count, weights, sp, csp, s, cs):
    rows, feat = parts[0].shape
    cols, width = s.shape
    blocks = rows // BLK
    per = 5 if blocks % 5 == 0 else 1
    tile = per * BLK
    chunk = min(512, cols)
    once = pl.Buffered(1)
    return pl.pallas_call(
        functools.partial(source_kernel, len(parts), tile),
        grid=(cols // chunk,),
        out_shape=(
            jax.ShapeDtypeStruct((PANEL, PANEL), jnp.float32),
            jax.ShapeDtypeStruct((PANEL, cols), jnp.float32),
        ),
        in_specs=[SMEM, SMEM, SMEM]
        + [pl.BlockSpec((rows, feat), lambda i: (0, 0), pipeline_mode=once)] * len(parts)
        + [
            pl.BlockSpec((PANEL, width), lambda i: (0, 0), pipeline_mode=once),
            pl.BlockSpec((1, PANEL), lambda i: (0, 0), pipeline_mode=once),
            pl.BlockSpec((chunk, width), lambda i: (i, 0)),
            pl.BlockSpec((1, chunk), lambda i: (0, i)),
        ],
        out_specs=(
            pl.BlockSpec((PANEL, PANEL), lambda i: (0, 0)),
            pl.BlockSpec((PANEL, chunk), lambda i: (0, i)),
        ),
        scratch_shapes=[
            pltpu.VMEM((rows // tile, PANEL, tile), jnp.bfloat16),
            pltpu.VMEM((rows, 1), jnp.float32),
        ],
        compiler_params=params(dimension_semantics=("arbitrary",)),
        cost_estimate=cost(
            2 * rows * (width + PANEL) * (cols + PANEL), 2 * rows * width + 2 * cols * width + 4 * PANEL * cols
        ),
        name="source_products",
    )(count, offsets, weights, *parts, sp, csp, s, cs)


def remainder_kernel(nparts, off_ref, w_ref, *refs):
    parts = refs[:nparts]
    sp_ref, csp_ref, s_ref, cs_ref, keep_ref, coef_ref, out_ref, p_ref, rs_ref = refs[nparts:]
    width = parts[0].shape[1] * nparts
    rows_all = parts[0].shape[0]
    step = pl.program_id(0)
    blocks = rows_all // BLK
    bounds = list(range(0, blocks, 4)) + [blocks]
    spans = [pl.ds(a * BLK, (b - a) * BLK) for a, b in zip(bounds, bounds[1:])]

    @pl.when(step == 0)
    def _():
        for j in range(blocks):
            rows = pl.ds(j * BLK, BLK)
            sq = row_square(parts, rows) / width + EPSILON
            rs_ref[rows, :] = w_ref[j] / sq
        for rows in spans:
            inner = inner_product(parts, rows, off_ref, sp_ref)
            panel = inner * inner * rs_ref[rows, :] * csp_ref[...]
            p_ref[rows, :] = panel.astype(jnp.bfloat16)

    coef = coef_ref[...]
    high = coef.astype(jnp.bfloat16)
    low = (coef - high.astype(jnp.float32)).astype(jnp.bfloat16)
    for rows in spans:
        inner = inner_product(parts, rows, off_ref, s_ref)
        kern = (inner * inner * rs_ref[rows, :] * cs_ref[...]).astype(jnp.bfloat16)
        panel = p_ref[rows, :]
        fit = nn(panel, high) + nn(panel, low)
        out_ref[rows, :] = (kern.astype(jnp.float32) * keep_ref[...] - fit).astype(out_ref.dtype)


def remainder_rows(parts, offsets, weights, sp, csp, s, cs, keep, coef):
    rows, feat = parts[0].shape
    cols, width = s.shape
    chunk = min(256, cols)
    once = pl.Buffered(1)
    return pl.pallas_call(
        functools.partial(remainder_kernel, len(parts)),
        grid=(cols // chunk,),
        out_shape=jax.ShapeDtypeStruct((rows, cols), jnp.bfloat16),
        in_specs=[SMEM, SMEM]
        + [pl.BlockSpec((rows, feat), lambda i: (0, 0), pipeline_mode=once)] * len(parts)
        + [
            pl.BlockSpec((PANEL, width), lambda i: (0, 0), pipeline_mode=once),
            pl.BlockSpec((1, PANEL), lambda i: (0, 0), pipeline_mode=once),
            pl.BlockSpec((chunk, width), lambda i: (i, 0)),
            pl.BlockSpec((1, chunk), lambda i: (0, i)),
            pl.BlockSpec((1, chunk), lambda i: (0, i)),
            pl.BlockSpec((PANEL, chunk), lambda i: (0, i)),
        ],
        out_specs=pl.BlockSpec((rows, chunk), lambda i: (0, i)),
        scratch_shapes=[
            pltpu.VMEM((rows, PANEL), jnp.bfloat16),
            pltpu.VMEM((rows, 1), jnp.float32),
        ],
        compiler_params=params(dimension_semantics=("arbitrary",)),
        cost_estimate=cost(
            2 * rows * (width + 2 * PANEL) * cols, 2 * rows * width + 2 * cols * width + 2 * rows * cols
        ),
        name="remainder_rows",
    )(offsets, weights, *parts, sp, csp, s, cs, keep, coef)


def flips(bit, size):
    return [(i, i ^ bit) for i in range(size)]


def butterfly_sum(x, bits):
    size = lax.axis_size("rows")
    me = lax.axis_index("rows")
    for bit in bits:
        half = x.shape[0] // 2
        upper = (me // bit) % 2
        send = lax.dynamic_slice_in_dim(x, (1 - upper) * half, half, 0)
        kept = lax.dynamic_slice_in_dim(x, upper * half, half, 0)
        x = kept + lax.ppermute(send, "rows", flips(bit, size))
    for bit in bits[::-1]:
        upper = (me // bit) % 2
        other = lax.ppermute(x, "rows", flips(bit, size))
        x = jnp.where(
            upper == 0, jnp.concatenate([x, other], 0), jnp.concatenate([other, x], 0)
        )
    return x


def full_sum(x):
    size = lax.axis_size("rows")
    bit = 1
    while bit < size:
        x = x + lax.ppermute(x, "rows", flips(bit, size))
        bit *= 2
    return x


def on_device(descriptors, sparse_points, block_weights, block_counts, destinations):
    owners = lax.axis_size("rows")
    groups = lax.axis_size("cols")
    me = lax.axis_index("rows").astype(jnp.int32)
    group = lax.axis_index("cols").astype(jnp.int32)
    slots = block_weights.shape[0]
    per_pair = -(-slots // owners)
    feat = descriptors.shape[1]
    cols, width = sparse_points.shape
    norm = math.sqrt(owners * DST_BLK * BLK)

    desc_blocks = descriptors.reshape(slots, BLK, feat)
    outgoing = pack(desc_blocks, me[None], destinations, block_counts, per_pair)
    received = lax.all_to_all(outgoing, "rows", split_axis=0, concat_axis=0, tiled=True)

    first = sparse_points[:PANEL]
    if groups == 2:
        moved = lax.ppermute(first, "cols", [(0, 1), (1, 0)])
        panel_points = jnp.where(group == 0, first, moved)
    else:
        panel_points = lax.all_gather(first, "cols", axis=0, tiled=False)[0]

    def column_scale(points):
        sq = jnp.einsum("mf,mf->m", points, points, preferred_element_type=jnp.float32)
        return (1.0 / (width * (sq / width + EPSILON)))[None, :]

    cs = column_scale(sparse_points)
    csp = column_scale(panel_points)
    offsets = part_offsets(feat)

    source_parts = share_parts(descriptors)
    count = lax.dynamic_index_in_dim(block_counts, me, 0)
    weights32 = block_weights.astype(jnp.float32)
    gram_part, g_part = source_products(
        source_parts, offsets, count, weights32, panel_points, csp, sparse_points, cs
    )

    spare = -(-owners * slots // (PANEL * 8)) * 8
    table = lax.dynamic_update_slice(
        jnp.zeros((spare * PANEL,), jnp.float32), weights32, (me * slots,)
    ).reshape(spare, PANEL)
    if groups == 2:
        mine = lax.dynamic_slice_in_dim(gram_part, group * (PANEL // 2), PANEL // 2, 0)
        summed = full_sum(jnp.concatenate([mine, table], 0))
        mine, table = summed[: PANEL // 2], summed[PANEL // 2 :]
        other = lax.ppermute(mine, "cols", [(0, 1), (1, 0)])
        gram = jnp.where(
            group == 0, jnp.concatenate([mine, other], 0), jnp.concatenate([other, mine], 0)
        )
    else:
        summed = full_sum(jnp.concatenate([gram_part, table], 0))
        gram, table = summed[:PANEL], summed[PANEL:]
    all_weights = table.reshape(-1)[: owners * slots]

    lower = jnp.linalg.cholesky(gram)
    inverse = lax.linalg.triangular_solve(
        lower, jnp.eye(PANEL, dtype=jnp.float32), left_side=True, lower=True
    )

    bits = []
    bit = 1
    while bit < owners:
        bits.append(bit)
        bit *= 2
    half = cols // 2
    swapped = [bits[1], bits[0]] + bits[2:]
    g = jnp.concatenate(
        [butterfly_sum(g_part[:, :half], bits), butterfly_sum(g_part[:, half:], swapped)], 1
    )
    projection = nn(inverse, g, HIGH)
    fit = nn(inverse.T, projection, HIGH)
    column = group * cols + jnp.arange(cols, dtype=jnp.int32)
    keep = (column >= PANEL)[None, :]
    basis_map = jnp.pad(inverse.T * (-norm), ((0, 0), (0, cols - PANEL)))
    coef = jnp.where(keep, fit, basis_map)

    slot_ids = jnp.arange(slots, dtype=jnp.int32)
    toward = ((slot_ids[None, :] < block_counts[:, None]) & (destinations == me)).astype(jnp.int32)
    rank = jnp.cumsum(toward, axis=1) - toward
    flat = toward.reshape(-1)
    place = jnp.cumsum(flat) - flat
    where_from = (jnp.arange(owners, dtype=jnp.int32)[:, None] * per_pair + rank).reshape(-1)
    hit = (flat[None, :] == 1) & (place[None, :] == jnp.arange(DST_BLK, dtype=jnp.int32)[:, None])
    positions = jnp.sum(jnp.where(hit, where_from[None, :], 0), axis=1)
    weights_here = jnp.sum(jnp.where(hit, all_weights[None, :], 0.0), axis=1)

    arrived = select(received, positions).reshape(DST_BLK * BLK, feat)
    parts = share_parts(arrived)
    remainder = remainder_rows(
        parts,
        offsets,
        weights_here,
        panel_points,
        csp,
        sparse_points,
        cs,
        keep.astype(jnp.float32),
        coef,
    )
    return (projection / norm, remainder)


def solution(mesh):
    return jax.shard_map(
        on_device,
        mesh=mesh,
        in_specs=(P("rows", "cols"), P("cols", None), P("rows"), P(), P()),
        out_specs=(P(None, "cols"), P("rows", "cols")),
        check_vma=False,
    )
```

```python
import functools
import math

import jax
import jax.numpy as jnp
from jax import lax
from jax.experimental import pallas as pl
from jax.experimental.pallas import tpu as pltpu
from jax.sharding import PartitionSpec as P

PANEL = 256
BLK = 128
DST_BLK = 13
EPSILON = 1e-06
VMEM_LIMIT = 56 * 1024 * 1024
HIGH = lax.Precision.HIGHEST
ANY = pl.BlockSpec(memory_space=pl.ANY)
VMEM = pl.BlockSpec(memory_space=pltpu.VMEM)
SMEM = pl.BlockSpec(memory_space=pltpu.SMEM)


def params(**kw):
    return pltpu.CompilerParams(vmem_limit_bytes=VMEM_LIMIT, **kw)


def cost(flops, nbytes):
    return pl.CostEstimate(flops=int(flops), bytes_accessed=int(nbytes), transcendentals=0)


def dot(a, b, ca, cb, precision=None):
    return lax.dot_general(
        a, b, (((ca,), (cb,)), ((), ())), preferred_element_type=jnp.float32, precision=precision
    )


def nt(a, b, precision=None):
    return dot(a, b, 1, 1, precision)


def nn(a, b, precision=None):
    return dot(a, b, 1, 0, precision)


def tn(a, b, precision=None):
    return dot(a, b, 0, 0, precision)


def split(x):
    high = x.astype(jnp.bfloat16)
    return high, (x - high.astype(jnp.float32)).astype(jnp.bfloat16)


def pack_kernel(per_pair, me_ref, dest_ref, cnt_ref, desc_ref, out_ref, ctr_ref, sems):
    slots = desc_ref.shape[0]
    owners = ctr_ref.shape[0]
    me = me_ref[0]
    count = cnt_ref[me]

    @pl.loop(0, owners)
    def _(i):
        ctr_ref[i] = 0

    @pl.loop(0, slots)
    def _(j):
        @pl.when(j < count)
        def _():
            d = dest_ref[me, j]
            r = ctr_ref[d]
            ctr_ref[d] = r + 1
            slot = d * per_pair + r
            pltpu.make_async_copy(desc_ref.at[j], out_ref.at[slot], sems.at[j]).start()

    @pl.loop(0, slots)
    def _(j):
        @pl.when(j < count)
        def _():
            pltpu.make_async_copy(desc_ref.at[0], out_ref.at[0], sems.at[j]).wait()


def pack(desc_blocks, me, destinations, counts, per_pair):
    slots, blk, feat = desc_blocks.shape
    owners = destinations.shape[0]
    return pl.pallas_call(
        functools.partial(pack_kernel, per_pair),
        out_shape=jax.ShapeDtypeStruct((owners * per_pair, blk, feat), desc_blocks.dtype),
        in_specs=[SMEM, SMEM, SMEM, VMEM],
        out_specs=ANY,
        scratch_shapes=[pltpu.SMEM((owners,), jnp.int32), pltpu.SemaphoreType.DMA((slots,))],
        compiler_params=params(),
        cost_estimate=cost(0, 4 * slots * blk * feat),
        name="pack",
    )(me, destinations, counts, desc_blocks)


def select_kernel(pos_ref, recv_ref, out_ref, sems):
    copies = [
        pltpu.make_async_copy(recv_ref.at[pos_ref[p]], out_ref.at[p], sems.at[p])
        for p in range(DST_BLK)
    ]
    for c in copies:
        c.start()
    for c in copies:
        c.wait()


def select(received, positions):
    _, blk, feat = received.shape
    return pl.pallas_call(
        select_kernel,
        out_shape=jax.ShapeDtypeStruct((DST_BLK, blk, feat), received.dtype),
        in_specs=[SMEM, ANY],
        out_specs=VMEM,
        scratch_shapes=[pltpu.SemaphoreType.DMA((DST_BLK,))],
        compiler_params=params(),
        cost_estimate=cost(0, 4 * DST_BLK * blk * feat),
        name="select",
    )(positions, received)


def small_factor(a):
    n = a.shape[0]
    row = lax.broadcasted_iota(jnp.int32, (n, 1), 0)
    eye = lax.broadcasted_iota(jnp.int32, (n, n), 0) == lax.broadcasted_iota(jnp.int32, (n, n), 1)
    m = jnp.concatenate([a, eye.astype(jnp.float32)], axis=1)
    out = []
    for j in range(0, n, 2):
        r0 = m[j : j + 1, :]
        r1 = m[j + 1 : j + 2, :]
        p = r0[:, j : j + 1]
        q = r0[:, j + 1 : j + 2]
        s = r1[:, j + 1 : j + 2]
        det = p * s - q * q
        out.append(r0[:, n:] * lax.rsqrt(p))
        out.append((r1[:, n:] - (q / p) * r0[:, n:]) * lax.rsqrt(det / p))
        if j + 2 < n:
            inv = 1.0 / det
            g0 = (s * r0 - q * r1) * inv
            g1 = (p * r1 - q * r0) * inv
            c0 = jnp.where(row > j + 1, m[:, j : j + 1], 0.0)
            c1 = jnp.where(row > j + 1, m[:, j + 1 : j + 2], 0.0)
            m = m - c0 * g0 - c1 * g1
    return out


def factor_kernel(leaf, gram_ref, x_ref, a_ref):
    n = gram_ref.shape[0]
    a_ref[...] = gram_ref[...]
    x_ref[...] = jnp.zeros_like(x_ref)
    for k in range(0, n, leaf):
        e = k + leaf
        for i, r in enumerate(small_factor(a_ref[k:e, k:e])):
            x_ref[k + i : k + i + 1, k:e] = r
        xk = x_ref[k:e, k:e]
        if e < n:
            t = nn(xk, a_ref[k:e, e:], HIGH)
            a_ref[k:e, e:] = t
            a_ref[e:, e:] -= tn(t, t, HIGH)
        if k > 0:
            x_ref[k:e, :k] = -nn(xk, tn(a_ref[:k, k:e], x_ref[:k, :k], HIGH), HIGH)


def factor(gram):
    n = gram.shape[0]
    return pl.pallas_call(
        functools.partial(factor_kernel, 64),
        out_shape=jax.ShapeDtypeStruct((n, n), jnp.float32),
        scratch_shapes=[pltpu.VMEM((n, n), jnp.float32)],
        compiler_params=params(),
        cost_estimate=cost(2e10, 8 * n * n),
        name="factor",
    )(gram)


def share_parts(x):
    groups = lax.axis_size("cols")
    if groups == 2:
        peer = lax.ppermute(x, "cols", [(0, 1), (1, 0)])
        return [x, peer]
    full = lax.all_gather(x, "cols", axis=0, tiled=False)
    return [full[i] for i in range(groups)]


def part_offsets(feat):
    groups = lax.axis_size("cols")
    if groups == 2:
        c = lax.axis_index("cols")
        return jnp.stack([c * feat, (1 - c) * feat]).astype(jnp.int32)
    return jnp.arange(groups, dtype=jnp.int32) * feat


def joined(parts, off_ref, x_ref):
    feat = parts[0].shape[1]
    for i, ref in enumerate(parts):
        x_ref[:, pl.ds(pl.multiple_of(off_ref[i], 128), feat)] = ref[...]


def row_scale(x, weight):
    x = x.astype(jnp.float32)
    return weight / (jnp.sum(x * x, axis=1, keepdims=True) / x.shape[1] + EPSILON)


def panel_kernel(nparts, cnt_ref, off_ref, w_ref, *refs):
    parts = refs[:nparts]
    sp_ref, csp_ref, gram_ref, x_ref, pw_ref = refs[nparts:]
    tile = x_ref.shape[0]
    per = tile // BLK
    count = cnt_ref[0]
    step = pl.program_id(0)

    @pl.when(step == 0)
    def _():
        gram_ref[...] = jnp.zeros_like(gram_ref)

    @pl.when(step * per < count)
    def _():
        joined(parts, off_ref, x_ref)
        scales = []
        for b in range(per):
            j = step * per + b
            w = jnp.where(j < count, w_ref[j], 0.0)
            scales.append(row_scale(x_ref[b * BLK : (b + 1) * BLK, :], w))
        scale = jnp.concatenate(scales, axis=0)
        inner = nt(x_ref[...], sp_ref[...])
        panel = (inner * inner * scale * csp_ref[...]).astype(jnp.bfloat16)
        gram_ref[...] += tn(panel, panel)
        pw_ref[...] = (panel.astype(jnp.float32) * scale).astype(jnp.bfloat16)

    @pl.when(step * per >= count)
    def _():
        pw_ref[...] = jnp.zeros_like(pw_ref)


def panel_products(parts, offsets, count, weights, sp, csp):
    rows, feat = parts[0].shape
    width = sp.shape[1]
    blocks = rows // BLK
    per = 5 if blocks % 5 == 0 else 1
    tile = per * BLK
    return pl.pallas_call(
        functools.partial(panel_kernel, len(parts)),
        grid=(rows // tile,),
        out_shape=(
            jax.ShapeDtypeStruct((PANEL, PANEL), jnp.float32),
            jax.ShapeDtypeStruct((rows, width), jnp.bfloat16),
            jax.ShapeDtypeStruct((rows, PANEL), jnp.bfloat16),
        ),
        in_specs=[SMEM, SMEM, SMEM]
        + [pl.BlockSpec((tile, feat), lambda i: (i, 0))] * len(parts)
        + [pl.BlockSpec((PANEL, width), lambda i: (0, 0)), pl.BlockSpec((1, PANEL), lambda i: (0, 0))],
        out_specs=(
            pl.BlockSpec((PANEL, PANEL), lambda i: (0, 0)),
            pl.BlockSpec((tile, width), lambda i: (i, 0)),
            pl.BlockSpec((tile, PANEL), lambda i: (i, 0)),
        ),
        compiler_params=params(dimension_semantics=("arbitrary",)),
        cost_estimate=cost(2 * rows * PANEL * (width + PANEL), 4 * rows * width),
        name="panel_products",
    )(count, offsets, weights, *parts, sp, csp)


def column_kernel(tile, cnt_ref, x_ref, pw_ref, s_ref, g_ref):
    rows, width = x_ref.shape
    count = cnt_ref[0]
    per = tile // BLK
    s = s_ref[...]
    g_ref[...] = jnp.zeros_like(g_ref)
    for t in range(rows // tile):
        @pl.when(t * per < count)
        def _():
            inner = nt(s, x_ref[t * tile : (t + 1) * tile, :])
            square = (inner * inner).astype(jnp.bfloat16)
            g_ref[...] += nn(square, pw_ref[t * tile : (t + 1) * tile, :])

    wide = s.astype(jnp.float32)
    norm = jnp.sum(wide * wide, axis=1, keepdims=True) / width + EPSILON
    g_ref[...] = g_ref[...] / (width * norm)


def column_products(x, pw, count, s, start, size):
    rows, width = x.shape
    blocks = rows // BLK
    per = 5 if blocks % 5 == 0 else 1
    chunk = min(512, size)
    first = start // chunk
    once = pl.Buffered(1)
    return pl.pallas_call(
        functools.partial(column_kernel, per * BLK),
        grid=(size // chunk,),
        out_shape=jax.ShapeDtypeStruct((size, PANEL), jnp.float32),
        in_specs=[
            SMEM,
            pl.BlockSpec((rows, width), lambda i: (0, 0), pipeline_mode=once),
            pl.BlockSpec((rows, PANEL), lambda i: (0, 0), pipeline_mode=once),
            pl.BlockSpec((chunk, width), lambda i: (first + i, 0)),
        ],
        out_specs=pl.BlockSpec((chunk, PANEL), lambda i: (i, 0)),
        compiler_params=params(dimension_semantics=("arbitrary",)),
        cost_estimate=cost(2 * rows * (width + PANEL) * size, 2 * rows * width),
        name="column_products",
    )(count, x, pw, s)


def remainder_kernel(nparts, norm, off_ref, w_ref, group_ref, *refs):
    parts = refs[:nparts]
    sp_ref, csp_ref, s_ref, cs_ref, inv_ref, rt_ref, out_ref, proj_ref, x_ref, p_ref, rs_ref = refs[nparts:]
    rows_all, width = x_ref.shape
    chunk = s_ref.shape[0]
    step = pl.program_id(0)
    blocks = rows_all // BLK
    bounds = list(range(0, blocks, 4)) + [blocks]
    spans = [(a * BLK, b * BLK) for a, b in zip(bounds, bounds[1:])]

    @pl.when(step == 0)
    def _():
        joined(parts, off_ref, x_ref)
        for j in range(blocks):
            scale = row_scale(x_ref[j * BLK : (j + 1) * BLK, :], w_ref[j])
            rs_ref[j * BLK : (j + 1) * BLK, :] = jnp.broadcast_to(scale, (BLK, 128))
        for a, b in spans:
            inner = nt(x_ref[a:b, :], sp_ref[...])
            scale = jnp.concatenate([rs_ref[a:b, :]] * (PANEL // 128), axis=1)
            p_ref[a:b, :] = (inner * inner * scale * csp_ref[...]).astype(jnp.bfloat16)

    inv_high, inv_low = split(inv_ref[...])
    rt = rt_ref[...]
    coef = (nn(rt, inv_high) + nn(rt, inv_low)).astype(jnp.bfloat16)
    proj_ref[...] = rt.astype(jnp.float32).T * (1.0 / norm)
    for a, b in spans:
        inner = nt(x_ref[a:b, :], s_ref[...])
        scale = jnp.concatenate([rs_ref[a:b, :]] * (chunk // 128), axis=1)
        kern = (inner * inner * scale * cs_ref[...]).astype(jnp.bfloat16)
        fit = nt(p_ref[a:b, :], coef)
        out_ref[a:b, :] = (kern.astype(jnp.float32) - fit).astype(out_ref.dtype)

    @pl.when((step == 0) & (group_ref[0] == 0))
    def _():
        for a, b in spans:
            panel = p_ref[a:b, :]
            basis = nt(panel, inv_high) + nt(panel, inv_low)
            out_ref[a:b, :PANEL] = (basis * norm).astype(out_ref.dtype)


def remainder_rows(parts, offsets, weights, group, sp, csp, s, cs, inverse, rt, norm):
    rows, feat = parts[0].shape
    cols, width = s.shape
    chunk = min(512, cols)
    once = pl.Buffered(1)
    return pl.pallas_call(
        functools.partial(remainder_kernel, len(parts), norm),
        grid=(cols // chunk,),
        out_shape=(
            jax.ShapeDtypeStruct((rows, cols), jnp.bfloat16),
            jax.ShapeDtypeStruct((PANEL, cols), jnp.float32),
        ),
        in_specs=[SMEM, SMEM, SMEM]
        + [pl.BlockSpec((rows, feat), lambda i: (0, 0), pipeline_mode=once)] * len(parts)
        + [
            pl.BlockSpec((PANEL, width), lambda i: (0, 0), pipeline_mode=once),
            pl.BlockSpec((1, PANEL), lambda i: (0, 0), pipeline_mode=once),
            pl.BlockSpec((chunk, width), lambda i: (i, 0)),
            pl.BlockSpec((1, chunk), lambda i: (0, i)),
            pl.BlockSpec((PANEL, PANEL), lambda i: (0, 0), pipeline_mode=once),
            pl.BlockSpec((chunk, PANEL), lambda i: (i, 0)),
        ],
        out_specs=(
            pl.BlockSpec((rows, chunk), lambda i: (0, i)),
            pl.BlockSpec((PANEL, chunk), lambda i: (0, i)),
        ),
        scratch_shapes=[
            pltpu.VMEM((rows, width), jnp.bfloat16),
            pltpu.VMEM((rows, PANEL), jnp.bfloat16),
            pltpu.VMEM((rows, 128), jnp.float32),
        ],
        compiler_params=params(dimension_semantics=("arbitrary",)),
        cost_estimate=cost(
            2 * rows * (width + 2 * PANEL) * cols, 2 * rows * width + 2 * cols * width + 2 * rows * cols
        ),
        name="remainder_rows",
    )(offsets, weights, group, *parts, sp, csp, s, cs, inverse, rt)


def flips(bit, size):
    return [(i, i ^ bit) for i in range(size)]


def scatter_sum(x, bits):
    size = lax.axis_size("rows")
    me = lax.axis_index("rows")
    for bit in bits:
        half = x.shape[0] // 2
        upper = (me // bit) % 2
        send = lax.dynamic_slice_in_dim(x, (1 - upper) * half, half, 0)
        kept = lax.dynamic_slice_in_dim(x, upper * half, half, 0)
        x = kept + lax.ppermute(send, "rows", flips(bit, size))
    return x


def gather_back(x, bits):
    size = lax.axis_size("rows")
    me = lax.axis_index("rows")
    for bit in bits[::-1]:
        upper = (me // bit) % 2
        other = lax.ppermute(x, "rows", flips(bit, size))
        x = jnp.where(
            upper == 0, jnp.concatenate([x, other], 0), jnp.concatenate([other, x], 0)
        )
    return x


def full_sum(x, bits):
    size = lax.axis_size("rows")
    for i in range(0, len(bits), 2):
        pair = bits[i : i + 2]
        if len(pair) == 1:
            x = x + lax.ppermute(x, "rows", flips(pair[0], size))
        else:
            a, b = pair
            xa = lax.ppermute(x, "rows", flips(a, size))
            xb = lax.ppermute(x, "rows", flips(b, size))
            xab = lax.ppermute(x, "rows", flips(a + b, size))
            x = (x + xa) + (xb + xab)
    return x


def on_device(descriptors, sparse_points, block_weights, block_counts, destinations):
    owners = lax.axis_size("rows")
    groups = lax.axis_size("cols")
    me = lax.axis_index("rows").astype(jnp.int32)
    group = lax.axis_index("cols").astype(jnp.int32)
    slots = block_weights.shape[0]
    per_pair = -(-slots // owners)
    feat = descriptors.shape[1]
    cols, width = sparse_points.shape
    norm = math.sqrt(owners * DST_BLK * BLK)
    bits = [1 << i for i in range(owners.bit_length() - 1)]
    swapped = [bits[1], bits[0]] + bits[2:]

    source_parts = share_parts(descriptors)
    desc_blocks = descriptors.reshape(slots, BLK, feat)
    outgoing = pack(desc_blocks, me[None], destinations, block_counts, per_pair)
    received = lax.all_to_all(outgoing, "rows", split_axis=0, concat_axis=0, tiled=True)

    first = sparse_points[:PANEL]
    if groups == 2:
        moved = lax.ppermute(first, "cols", [(0, 1), (1, 0)])
        panel_points = jnp.where(group == 0, first, moved)
    else:
        panel_points = lax.all_gather(first, "cols", axis=0, tiled=False)[0]

    def column_scale(points):
        sq = jnp.einsum("mf,mf->m", points, points, preferred_element_type=jnp.float32)
        return (1.0 / (width * (sq / width + EPSILON)))[None, :]

    cs = column_scale(sparse_points)
    csp = column_scale(panel_points)
    offsets = part_offsets(feat)

    count = lax.dynamic_index_in_dim(block_counts, me, 0)
    weights32 = block_weights.astype(jnp.float32)
    gram_part, x_source, pw = panel_products(
        source_parts, offsets, count, weights32, panel_points, csp
    )

    spare = -(-owners * slots // (PANEL * 8)) * 8
    table = lax.dynamic_update_slice(
        jnp.zeros((spare * PANEL,), jnp.float32), weights32, (me * slots,)
    ).reshape(spare, PANEL)
    if groups == 2:
        mine = lax.dynamic_slice_in_dim(gram_part, group * (PANEL // 2), PANEL // 2, 0)
        summed = full_sum(jnp.concatenate([mine, table], 0), bits)
        mine, table = summed[: PANEL // 2], summed[PANEL // 2 :]
        other = lax.ppermute(mine, "cols", [(0, 1), (1, 0)])
        gram = jnp.where(
            group == 0, jnp.concatenate([mine, other], 0), jnp.concatenate([other, mine], 0)
        )
    else:
        summed = full_sum(jnp.concatenate([gram_part, table], 0), bits)
        gram, table = summed[:PANEL], summed[PANEL:]
    all_weights = table.reshape(-1)[: owners * slots]
    inverse = factor(gram)

    half = cols // 2
    low = scatter_sum(column_products(x_source, pw, count, sparse_points, 0, half), bits)
    high = scatter_sum(column_products(x_source, pw, count, sparse_points, half, half), swapped)
    own = low.shape[0]
    solved = nt(jnp.concatenate([low, high], 0), inverse, HIGH).astype(jnp.bfloat16)
    rt = jnp.concatenate(
        [gather_back(solved[:own], bits), gather_back(solved[own:], swapped)], 0
    )

    slot_ids = jnp.arange(slots, dtype=jnp.int32)
    toward = ((slot_ids[None, :] < block_counts[:, None]) & (destinations == me)).astype(jnp.int32)
    rank = jnp.cumsum(toward, axis=1) - toward
    flat = toward.reshape(-1)
    place = jnp.cumsum(flat) - flat
    where_from = (jnp.arange(owners, dtype=jnp.int32)[:, None] * per_pair + rank).reshape(-1)
    hit = (flat[None, :] == 1) & (place[None, :] == jnp.arange(DST_BLK, dtype=jnp.int32)[:, None])
    positions = jnp.sum(jnp.where(hit, where_from[None, :], 0), axis=1)
    weights_here = jnp.sum(jnp.where(hit, all_weights[None, :], 0.0), axis=1)

    arrived = select(received, positions).reshape(DST_BLK * BLK, feat)
    remainder, projected = remainder_rows(
        share_parts(arrived),
        offsets,
        weights_here,
        group[None],
        panel_points,
        csp,
        sparse_points,
        cs,
        inverse,
        rt,
        norm,
    )
    return (projected, remainder)


def solution(mesh):
    return jax.shard_map(
        on_device,
        mesh=mesh,
        in_specs=(P("rows", "cols"), P("cols", None), P("rows"), P(), P()),
        out_specs=(P(None, "cols"), P("rows", "cols")),
        check_vma=False,
    )
```

```python
import functools
import math

import jax
import jax.numpy as jnp
from jax import lax
from jax.experimental import pallas as pl
from jax.experimental.pallas import tpu as pltpu
from jax.sharding import PartitionSpec as P

PANEL = 256
BLK = 128
DST_BLK = 13
EPSILON = 1e-06
VMEM_LIMIT = 56 * 1024 * 1024
HIGH = lax.Precision.HIGHEST
ANY = pl.BlockSpec(memory_space=pl.ANY)
VMEM = pl.BlockSpec(memory_space=pltpu.VMEM)
SMEM = pl.BlockSpec(memory_space=pltpu.SMEM)


def params(**kw):
    return pltpu.CompilerParams(vmem_limit_bytes=VMEM_LIMIT, **kw)


def cost(flops, nbytes):
    return pl.CostEstimate(flops=int(flops), bytes_accessed=int(nbytes), transcendentals=0)


def dot(a, b, ca, cb, precision=None):
    return lax.dot_general(
        a, b, (((ca,), (cb,)), ((), ())), preferred_element_type=jnp.float32, precision=precision
    )


def nt(a, b, precision=None):
    return dot(a, b, 1, 1, precision)


def nn(a, b, precision=None):
    return dot(a, b, 1, 0, precision)


def tn(a, b, precision=None):
    return dot(a, b, 0, 0, precision)


def split(x):
    high = x.astype(jnp.bfloat16)
    return high, (x - high.astype(jnp.float32)).astype(jnp.bfloat16)


def pack_kernel(per_pair, me_ref, dest_ref, cnt_ref, desc_ref, out_ref, ctr_ref, sems):
    slots = desc_ref.shape[0]
    owners = ctr_ref.shape[0]
    me = me_ref[0]
    count = cnt_ref[me]

    @pl.loop(0, owners)
    def _(i):
        ctr_ref[i] = 0

    @pl.loop(0, slots)
    def _(j):
        @pl.when(j < count)
        def _():
            d = dest_ref[me, j]
            r = ctr_ref[d]
            ctr_ref[d] = r + 1
            slot = d * per_pair + r
            pltpu.make_async_copy(desc_ref.at[j], out_ref.at[slot], sems.at[j]).start()

    @pl.loop(0, slots)
    def _(j):
        @pl.when(j < count)
        def _():
            pltpu.make_async_copy(desc_ref.at[0], out_ref.at[0], sems.at[j]).wait()


def pack(desc_blocks, me, destinations, counts, per_pair):
    slots, blk, feat = desc_blocks.shape
    owners = destinations.shape[0]
    return pl.pallas_call(
        functools.partial(pack_kernel, per_pair),
        out_shape=jax.ShapeDtypeStruct((owners * per_pair, blk, feat), desc_blocks.dtype),
        in_specs=[SMEM, SMEM, SMEM, VMEM],
        out_specs=ANY,
        scratch_shapes=[pltpu.SMEM((owners,), jnp.int32), pltpu.SemaphoreType.DMA((slots,))],
        compiler_params=params(),
        cost_estimate=cost(0, 4 * slots * blk * feat),
        name="pack",
    )(me, destinations, counts, desc_blocks)


def select_kernel(pos_ref, recv_ref, out_ref, sems):
    copies = [
        pltpu.make_async_copy(recv_ref.at[pos_ref[p]], out_ref.at[p], sems.at[p])
        for p in range(DST_BLK)
    ]
    for c in copies:
        c.start()
    for c in copies:
        c.wait()


def select(received, positions):
    _, blk, feat = received.shape
    return pl.pallas_call(
        select_kernel,
        out_shape=jax.ShapeDtypeStruct((DST_BLK, blk, feat), received.dtype),
        in_specs=[SMEM, ANY],
        out_specs=VMEM,
        scratch_shapes=[pltpu.SemaphoreType.DMA((DST_BLK,))],
        compiler_params=params(),
        cost_estimate=cost(0, 4 * DST_BLK * blk * feat),
        name="select",
    )(positions, received)


def small_factor(a):
    n = a.shape[0]
    row = lax.broadcasted_iota(jnp.int32, (n, 1), 0)
    eye = lax.broadcasted_iota(jnp.int32, (n, n), 0) == lax.broadcasted_iota(jnp.int32, (n, n), 1)
    m = jnp.concatenate([a, eye.astype(jnp.float32)], axis=1)
    out = []
    for j in range(0, n, 2):
        r0 = m[j : j + 1, :]
        r1 = m[j + 1 : j + 2, :]
        p = r0[:, j : j + 1]
        q = r0[:, j + 1 : j + 2]
        s = r1[:, j + 1 : j + 2]
        det = p * s - q * q
        out.append(r0[:, n:] * lax.rsqrt(p))
        out.append((r1[:, n:] - (q / p) * r0[:, n:]) * lax.rsqrt(det / p))
        if j + 2 < n:
            inv = 1.0 / det
            g0 = (s * r0 - q * r1) * inv
            g1 = (p * r1 - q * r0) * inv
            c0 = jnp.where(row > j + 1, m[:, j : j + 1], 0.0)
            c1 = jnp.where(row > j + 1, m[:, j + 1 : j + 2], 0.0)
            m = m - c0 * g0 - c1 * g1
    return out


def factor_kernel(leaf, gram_ref, x_ref, a_ref):
    n = gram_ref.shape[0]
    a_ref[...] = gram_ref[...]
    x_ref[...] = jnp.zeros_like(x_ref)
    for k in range(0, n, leaf):
        e = k + leaf
        for i, r in enumerate(small_factor(a_ref[k:e, k:e])):
            x_ref[k + i : k + i + 1, k:e] = r
        xk = x_ref[k:e, k:e]
        if e < n:
            t = nn(xk, a_ref[k:e, e:], HIGH)
            a_ref[k:e, e:] = t
            a_ref[e:, e:] -= tn(t, t, HIGH)
        if k > 0:
            x_ref[k:e, :k] = -nn(xk, tn(a_ref[:k, k:e], x_ref[:k, :k], HIGH), HIGH)


def factor(gram):
    n = gram.shape[0]
    return pl.pallas_call(
        functools.partial(factor_kernel, 64),
        out_shape=jax.ShapeDtypeStruct((n, n), jnp.float32),
        scratch_shapes=[pltpu.VMEM((n, n), jnp.float32)],
        compiler_params=params(),
        cost_estimate=cost(2e10, 8 * n * n),
        name="factor",
    )(gram)


def share_parts(x):
    groups = lax.axis_size("cols")
    if groups == 2:
        peer = lax.ppermute(x, "cols", [(0, 1), (1, 0)])
        return [x, peer]
    full = lax.all_gather(x, "cols", axis=0, tiled=False)
    return [full[i] for i in range(groups)]


def part_offsets(feat):
    groups = lax.axis_size("cols")
    if groups == 2:
        c = lax.axis_index("cols")
        return jnp.stack([c * feat, (1 - c) * feat]).astype(jnp.int32)
    return jnp.arange(groups, dtype=jnp.int32) * feat


def join_copies(parts, off_ref, x_ref, sems, spans):
    feat = parts[0].shape[1]
    return [
        [
            pltpu.make_async_copy(
                ref.at[pl.ds(start, size)],
                x_ref.at[pl.ds(start, size), pl.ds(pl.multiple_of(off_ref[i], 128), feat)],
                sems.at[t, i],
            )
            for i, ref in enumerate(parts)
        ]
        for t, (start, size) in enumerate(spans)
    ]


def row_scale(x, weight):
    x = x.astype(jnp.float32)
    return weight / (jnp.sum(x * x, axis=1, keepdims=True) / x.shape[1] + EPSILON)


def column_scale(s):
    s = s.astype(jnp.float32)
    width = s.shape[1]
    scale = 1.0 / (width * (jnp.sum(s * s, axis=1, keepdims=True) / width + EPSILON))
    return jnp.broadcast_to(scale, (s.shape[0], 128)).T[:1, :]


def row_tiles(rows):
    blocks = rows // BLK
    per = 5 if blocks % 5 == 0 else 1
    return per, [(i * BLK, per * BLK) for i in range(0, blocks, per)]


def panel_kernel(nparts, cnt_ref, off_ref, w_ref, *refs):
    parts = refs[:nparts]
    sp_ref, gram_ref, pw_ref, x_ref, sems = refs[nparts:]
    per, tiles = row_tiles(x_ref.shape[0])
    count = cnt_ref[0]
    copies = join_copies(parts, off_ref, x_ref, sems, tiles)
    for group in copies:
        for c in group:
            c.start()
    gram_ref[...] = jnp.zeros_like(gram_ref)
    pw_ref[...] = jnp.zeros_like(pw_ref)
    points = column_scale(sp_ref[...])
    for t, (start, size) in enumerate(tiles):
        for c in copies[t]:
            c.wait()

        @pl.when(t * per < count)
        def _():
            scales = []
            for b in range(per):
                j = t * per + b
                w = jnp.where(j < count, w_ref[j], 0.0)
                scales.append(row_scale(x_ref[j * BLK : (j + 1) * BLK, :], w))
            scale = jnp.concatenate(scales, axis=0)
            inner = nt(x_ref[start : start + size, :], sp_ref[...])
            panel = (inner * inner * scale * points).astype(jnp.bfloat16)
            gram_ref[...] += tn(panel, panel)
            pw_ref[start : start + size, :] = (panel.astype(jnp.float32) * scale).astype(
                jnp.bfloat16
            )


def panel_products(parts, offsets, count, weights, sp):
    rows, feat = parts[0].shape
    width = sp.shape[1]
    tiles = len(row_tiles(rows)[1])
    return pl.pallas_call(
        functools.partial(panel_kernel, len(parts)),
        out_shape=(
            jax.ShapeDtypeStruct((PANEL, PANEL), jnp.float32),
            jax.ShapeDtypeStruct((rows, PANEL), jnp.bfloat16),
        ),
        in_specs=[SMEM, SMEM, SMEM] + [ANY] * len(parts) + [VMEM],
        out_specs=(VMEM, VMEM),
        scratch_shapes=[
            pltpu.VMEM((rows, width), jnp.bfloat16),
            pltpu.SemaphoreType.DMA((tiles, len(parts))),
        ],
        compiler_params=params(),
        cost_estimate=cost(2 * rows * PANEL * (width + PANEL), 2 * rows * width),
        name="panel_products",
    )(count, offsets, weights, *parts, sp)


def column_kernel(nparts, off_ref, *refs):
    parts = refs[:nparts]
    pw_ref, s_ref, g_ref, x_ref, sems = refs[nparts:]
    width = x_ref.shape[1]

    @pl.when(pl.program_id(0) == 0)
    def _():
        copies = join_copies(parts, off_ref, x_ref, sems, row_tiles(x_ref.shape[0])[1])
        for group in copies:
            for c in group:
                c.start()
        for group in copies:
            for c in group:
                c.wait()

    s = s_ref[...]
    inner = nt(s, x_ref[...])
    products = nn((inner * inner).astype(jnp.bfloat16), pw_ref[...])
    wide = s.astype(jnp.float32)
    square = jnp.sum(wide * wide, axis=1, keepdims=True) / width + EPSILON
    g_ref[...] = products / (width * square)


def column_products(parts, offsets, pw, s, start, size):
    rows, feat = parts[0].shape
    width = s.shape[1]
    chunk = min(512, size)
    first = start // chunk
    tiles = len(row_tiles(rows)[1])
    once = pl.Buffered(1)
    return pl.pallas_call(
        functools.partial(column_kernel, len(parts)),
        grid=(size // chunk,),
        out_shape=jax.ShapeDtypeStruct((size, PANEL), jnp.float32),
        in_specs=[SMEM]
        + [ANY] * len(parts)
        + [
            pl.BlockSpec((rows, PANEL), lambda i: (0, 0), pipeline_mode=once),
            pl.BlockSpec((chunk, width), lambda i: (first + i, 0)),
        ],
        out_specs=pl.BlockSpec((chunk, PANEL), lambda i: (i, 0)),
        scratch_shapes=[
            pltpu.VMEM((rows, width), jnp.bfloat16),
            pltpu.SemaphoreType.DMA((tiles, len(parts))),
        ],
        compiler_params=params(dimension_semantics=("arbitrary",)),
        cost_estimate=cost(2 * rows * (width + PANEL) * size, 2 * rows * width),
        name="column_products",
    )(offsets, *parts, pw, s)


def remainder_kernel(nparts, norm, quarter_ref, off_ref, w_ref, group_ref, *refs):
    parts = refs[:nparts]
    sp_ref, s_ref, inv_ref, rt_ref, out_ref, proj_ref, x_ref, p_ref, rs_ref, sems = refs[nparts:]
    rows_all, width = x_ref.shape
    chunk = s_ref.shape[0]
    step = pl.program_id(0)
    blocks = rows_all // BLK
    bounds = list(range(0, blocks, 7)) + [blocks]
    spans = [(a * BLK, b * BLK) for a, b in zip(bounds, bounds[1:])]

    @pl.when(step == 0)
    def _():
        copies = join_copies(parts, off_ref, x_ref, sems, [(a, b - a) for a, b in spans])
        for group in copies:
            for c in group:
                c.start()
        points = column_scale(sp_ref[...])
        for (a, b), group in zip(spans, copies):
            for c in group:
                c.wait()
            for j in range(a // BLK, b // BLK):
                scale = row_scale(x_ref[j * BLK : (j + 1) * BLK, :], w_ref[j])
                rs_ref[j * BLK : (j + 1) * BLK, :] = jnp.broadcast_to(scale, (BLK, 128))
            inner = nt(x_ref[a:b, :], sp_ref[...])
            scale = jnp.concatenate([rs_ref[a:b, :]] * (PANEL // 128), axis=1)
            p_ref[a:b, :] = (inner * inner * scale * points).astype(jnp.bfloat16)

    inv_high, inv_low = split(inv_ref[...])
    rt = rt_ref[0]
    coef = (nn(rt, inv_high) + nn(rt, inv_low)).astype(jnp.bfloat16)
    proj_ref[...] = rt.astype(jnp.float32).T * (1.0 / norm)
    columns = column_scale(s_ref[...])
    for a, b in spans:
        inner = nt(x_ref[a:b, :], s_ref[...])
        scale = jnp.concatenate([rs_ref[a:b, :]] * (chunk // 128), axis=1)
        kern = (inner * inner * scale * columns).astype(jnp.bfloat16)
        fit = nt(p_ref[a:b, :], coef)
        out_ref[a:b, :] = (kern.astype(jnp.float32) - fit).astype(out_ref.dtype)

    for i in range(-(-PANEL // chunk)):
        part = min(chunk, PANEL)

        @pl.when((step == i) & (group_ref[0] == 0))
        def _():
            for a, b in spans:
                panel = p_ref[a:b, :]
                rows = slice(i * part, (i + 1) * part)
                basis = nt(panel, inv_high[rows, :]) + nt(panel, inv_low[rows, :])
                out_ref[a:b, :part] = (basis * norm).astype(out_ref.dtype)


def remainder_rows(parts, offsets, weights, group, quarter, sp, s, inverse, rt, norm):
    rows, feat = parts[0].shape
    cols, width = s.shape
    chunk = rt.shape[1]
    once = pl.Buffered(1)
    spec = pltpu.PrefetchScalarGridSpec(
        num_scalar_prefetch=1,
        grid=(cols // chunk,),
        in_specs=[SMEM, SMEM, SMEM]
        + [ANY] * len(parts)
        + [
            pl.BlockSpec((PANEL, width), lambda i, q: (0, 0), pipeline_mode=once),
            pl.BlockSpec((chunk, width), lambda i, q: (i, 0)),
            pl.BlockSpec((PANEL, PANEL), lambda i, q: (0, 0), pipeline_mode=once),
            pl.BlockSpec((1, chunk, PANEL), lambda i, q: (i ^ q[0], 0, 0)),
        ],
        out_specs=(
            pl.BlockSpec((rows, chunk), lambda i, q: (0, i)),
            pl.BlockSpec((PANEL, chunk), lambda i, q: (0, i)),
        ),
        scratch_shapes=[
            pltpu.VMEM((rows, width), jnp.bfloat16),
            pltpu.VMEM((rows, PANEL), jnp.bfloat16),
            pltpu.VMEM((rows, 128), jnp.float32),
            pltpu.SemaphoreType.DMA((2, len(parts))),
        ],
    )
    return pl.pallas_call(
        functools.partial(remainder_kernel, len(parts), norm),
        grid_spec=spec,
        out_shape=(
            jax.ShapeDtypeStruct((rows, cols), jnp.bfloat16),
            jax.ShapeDtypeStruct((PANEL, cols), jnp.float32),
        ),
        compiler_params=params(dimension_semantics=("arbitrary",)),
        cost_estimate=cost(
            2 * rows * (width + 2 * PANEL) * cols, 2 * rows * width + 2 * cols * width + 2 * rows * cols
        ),
        name="remainder_rows",
    )(quarter, offsets, weights, group, *parts, sp, s, inverse, rt)


def flips(bit, size):
    return [(i, i ^ bit) for i in range(size)]


def quarter_of(pair):
    me = lax.axis_index("rows").astype(jnp.int32)
    return (me // pair[0]) % 2 + 2 * ((me // pair[1]) % 2)


def trade(x, pair, k):
    bit = pair[0] * (k & 1) + pair[1] * (k >> 1)
    return lax.ppermute(x, "rows", flips(bit, lax.axis_size("rows")))


def scatter_sum(x, pair):
    n = x.shape[0] // 4
    q = quarter_of(pair)
    pieces = [lax.dynamic_slice_in_dim(x, (q ^ k) * n, n, 0) for k in range(4)]
    got = [pieces[0]] + [trade(pieces[k], pair, k) for k in range(1, 4)]
    return (got[0] + got[1]) + (got[2] + got[3])


def gather_pieces(x, pair):
    return [x] + [trade(x, pair, k) for k in range(1, 4)]


def gather_back(x, pair):
    n = x.shape[0]
    q = quarter_of(pair)
    pieces = gather_pieces(x, pair)
    return jnp.concatenate(
        [lax.select_n(q ^ i, *pieces) for i in range(4)], 0
    )


def pair_sum(x, pair):
    got = gather_pieces(x, pair)
    return (got[0] + got[1]) + (got[2] + got[3])


def on_device(descriptors, sparse_points, block_weights, block_counts, destinations):
    owners = lax.axis_size("rows")
    groups = lax.axis_size("cols")
    me = lax.axis_index("rows").astype(jnp.int32)
    group = lax.axis_index("cols").astype(jnp.int32)
    slots = block_weights.shape[0]
    per_pair = -(-slots // owners)
    feat = descriptors.shape[1]
    cols, width = sparse_points.shape
    norm = math.sqrt(owners * DST_BLK * BLK)
    pairs = [(1 << i, 2 << i) for i in range(0, owners.bit_length() - 1, 2)]

    first = sparse_points[:PANEL]
    source_parts = share_parts(descriptors)
    if groups == 2:
        moved = lax.ppermute(first, "cols", [(0, 1), (1, 0)])
        panel_points = jnp.where(group == 0, first, moved)
    else:
        panel_points = lax.all_gather(first, "cols", axis=0, tiled=False)[0]
    desc_blocks = descriptors.reshape(slots, BLK, feat)
    outgoing = pack(desc_blocks, me[None], destinations, block_counts, per_pair)
    received = lax.all_to_all(outgoing, "rows", split_axis=0, concat_axis=0, tiled=True)

    offsets = part_offsets(feat)
    count = lax.dynamic_index_in_dim(block_counts, me, 0)
    weights32 = block_weights.astype(jnp.float32)
    gram_part, pw = panel_products(source_parts, offsets, count, weights32, panel_points)
    half = cols // 2
    low = column_products(source_parts, offsets, pw, sparse_points, 0, half)

    spare = -(-owners * slots // (PANEL * 8)) * 8
    table = lax.dynamic_update_slice(
        jnp.zeros((spare * PANEL,), jnp.float32), weights32, (me * slots,)
    ).reshape(spare, PANEL)
    if groups == 2:
        gram_part = lax.dynamic_slice_in_dim(gram_part, group * (PANEL // 2), PANEL // 2, 0)
    summed = pair_sum(jnp.concatenate([gram_part, table], 0), pairs[0])
    pw, summed = lax.optimization_barrier((pw, summed))
    high = column_products(source_parts, offsets, pw, sparse_points, half, half)
    for pair in pairs[1:]:
        summed = pair_sum(summed, pair)
    gram, table = summed[:-spare], summed[-spare:]
    if groups == 2:
        other = lax.ppermute(gram, "cols", [(0, 1), (1, 0)])
        gram = jnp.where(
            group == 0, jnp.concatenate([gram, other], 0), jnp.concatenate([other, gram], 0)
        )
    all_weights = table.reshape(-1)[: owners * slots]
    inverse = factor(gram)

    g = jnp.concatenate([low, high], 0)
    for pair in pairs:
        g = scatter_sum(g, pair)
    rt = nt(g, inverse, HIGH).astype(jnp.bfloat16)
    for pair in pairs[:0:-1]:
        rt = gather_back(rt, pair)
    slot_ids = jnp.arange(slots, dtype=jnp.int32)
    toward = ((slot_ids[None, :] < block_counts[:, None]) & (destinations == me)).astype(jnp.int32)
    rank = jnp.cumsum(toward, axis=1) - toward
    flat = toward.reshape(-1)
    place = jnp.cumsum(flat) - flat
    where_from = (jnp.arange(owners, dtype=jnp.int32)[:, None] * per_pair + rank).reshape(-1)
    hit = (flat[None, :] == 1) & (place[None, :] == jnp.arange(DST_BLK, dtype=jnp.int32)[:, None])
    positions = jnp.sum(jnp.where(hit, where_from[None, :], 0), axis=1)
    weights_here = jnp.sum(jnp.where(hit, all_weights[None, :], 0.0), axis=1)

    rt, positions = lax.optimization_barrier((rt, positions))
    rt = jnp.stack(gather_pieces(rt, pairs[0]))
    arrived = select(received, positions).reshape(DST_BLK * BLK, feat)
    remainder, projected = remainder_rows(
        share_parts(arrived),
        offsets,
        weights_here,
        group[None],
        quarter_of(pairs[0])[None],
        panel_points,
        sparse_points,
        inverse,
        rt,
        norm,
    )
    return (projected, remainder)


def solution(mesh):
    return jax.shard_map(
        on_device,
        mesh=mesh,
        in_specs=(P("rows", "cols"), P("cols", None), P("rows"), P(), P()),
        out_specs=(P(None, "cols"), P("rows", "cols")),
        check_vma=False,
    )
```

```python
import functools
import math

import jax
import jax.numpy as jnp
from jax import lax
from jax.experimental import pallas as pl
from jax.experimental.pallas import tpu as pltpu
from jax.sharding import PartitionSpec as P

PANEL = 256
BLK = 128
DST_BLK = 13
EPSILON = 1e-06
VMEM_LIMIT = 56 * 1024 * 1024
HIGH = lax.Precision.HIGHEST
ANY = pl.BlockSpec(memory_space=pl.ANY)
VMEM = pl.BlockSpec(memory_space=pltpu.VMEM)
SMEM = pl.BlockSpec(memory_space=pltpu.SMEM)


def params(**kw):
    return pltpu.CompilerParams(vmem_limit_bytes=VMEM_LIMIT, **kw)


def cost(flops, nbytes):
    return pl.CostEstimate(flops=int(flops), bytes_accessed=int(nbytes), transcendentals=0)


def dot(a, b, ca, cb, precision=None):
    return lax.dot_general(
        a, b, (((ca,), (cb,)), ((), ())), preferred_element_type=jnp.float32, precision=precision
    )


def nt(a, b, precision=None):
    return dot(a, b, 1, 1, precision)


def nn(a, b, precision=None):
    return dot(a, b, 1, 0, precision)


def tn(a, b, precision=None):
    return dot(a, b, 0, 0, precision)


def split(x):
    high = x.astype(jnp.bfloat16)
    return high, (x - high.astype(jnp.float32)).astype(jnp.bfloat16)


HEAD = 64


def block_copies(rank, whole_ref, outer, first_ref, last_ref, sems):
    if rank == 0:
        pairs = [(whole_ref, first_ref.at[outer, pl.ds(0, BLK)])]
    else:
        pairs = [
            (whole_ref.at[pl.ds(0, HEAD)], first_ref.at[outer, pl.ds(BLK, HEAD)]),
            (whole_ref.at[pl.ds(HEAD, BLK - HEAD)], last_ref.at[outer]),
        ]
    return [(a, b, sems.at[i]) for i, (a, b) in enumerate(pairs)]


def pack_kernel(per_pair, me_ref, dest_ref, cnt_ref, desc_ref, *refs):
    out_refs, (ctr_ref, rank_ref, sems) = refs[:per_pair], refs[per_pair:]
    slots = desc_ref.shape[0]
    owners = ctr_ref.shape[0]
    me = me_ref[0]
    count = cnt_ref[me]

    def copies(j, d, rank):
        moves = block_copies(rank, desc_ref.at[j], d, out_refs[0], out_refs[-1], sems.at[j])
        return [pltpu.make_async_copy(a, b, sem) for a, b, sem in moves]

    @pl.loop(0, owners)
    def _(i):
        ctr_ref[i] = 0

    @pl.loop(0, slots)
    def _(j):
        @pl.when(j < count)
        def _():
            d = dest_ref[me, j]
            rank = ctr_ref[d]
            ctr_ref[d] = rank + 1
            rank_ref[j] = rank
            for r in range(per_pair):
                @pl.when(rank == r)
                def _():
                    for c in copies(j, d, r):
                        c.start()

    @pl.loop(0, slots)
    def _(j):
        @pl.when(j < count)
        def _():
            for r in range(per_pair):
                @pl.when(rank_ref[j] == r)
                def _():
                    for c in copies(j, 0, r):
                        c.wait()


def pack(desc_blocks, me, destinations, counts, per_pair):
    slots, blk, feat = desc_blocks.shape
    owners = destinations.shape[0]
    heights = [blk] if per_pair == 1 else [blk + HEAD, blk - HEAD]
    return pl.pallas_call(
        functools.partial(pack_kernel, per_pair),
        out_shape=[
            jax.ShapeDtypeStruct((owners, h, feat), desc_blocks.dtype) for h in heights
        ],
        in_specs=[SMEM, SMEM, SMEM, VMEM],
        out_specs=[ANY] * per_pair,
        scratch_shapes=[
            pltpu.SMEM((owners,), jnp.int32),
            pltpu.SMEM((slots,), jnp.int32),
            pltpu.SemaphoreType.DMA((slots, 2)),
        ],
        compiler_params=params(),
        cost_estimate=cost(0, 4 * slots * blk * feat),
        name="pack",
    )(me, destinations, counts, desc_blocks)


def select_kernel(per_pair, pos_ref, *refs):
    recv_refs, (out_ref, sems) = refs[:per_pair], refs[per_pair:]

    def copies(p, rank):
        owner = pos_ref[p] // per_pair
        moves = block_copies(rank, out_ref.at[p], owner, recv_refs[0], recv_refs[-1], sems.at[p])
        return [pltpu.make_async_copy(b, a, sem) for a, b, sem in moves]

    for act in ("start", "wait"):
        for p in range(DST_BLK):
            for r in range(per_pair):
                @pl.when(pos_ref[p] % per_pair == r)
                def _():
                    for c in copies(p, r):
                        getattr(c, act)()


def select(received, positions):
    feat = received[0].shape[-1]
    return pl.pallas_call(
        functools.partial(select_kernel, len(received)),
        out_shape=jax.ShapeDtypeStruct((DST_BLK, BLK, feat), received[0].dtype),
        in_specs=[SMEM] + [ANY] * len(received),
        out_specs=VMEM,
        scratch_shapes=[pltpu.SemaphoreType.DMA((DST_BLK, 2))],
        compiler_params=params(),
        cost_estimate=cost(0, 4 * DST_BLK * BLK * feat),
        name="select",
    )(positions, *received)


def small_factor(a):
    n = a.shape[0]
    row = lax.broadcasted_iota(jnp.int32, (n, 1), 0)
    eye = lax.broadcasted_iota(jnp.int32, (n, n), 0) == lax.broadcasted_iota(jnp.int32, (n, n), 1)
    m = jnp.concatenate([a, eye.astype(jnp.float32)], axis=1)
    out = []
    for j in range(0, n, 2):
        r0 = m[j : j + 1, :]
        r1 = m[j + 1 : j + 2, :]
        p = r0[:, j : j + 1]
        q = r0[:, j + 1 : j + 2]
        s = r1[:, j + 1 : j + 2]
        det = p * s - q * q
        out.append(r0[:, n:] * lax.rsqrt(p))
        out.append((r1[:, n:] - (q / p) * r0[:, n:]) * lax.rsqrt(det / p))
        if j + 2 < n:
            inv = 1.0 / det
            g0 = (s * r0 - q * r1) * inv
            g1 = (p * r1 - q * r0) * inv
            c0 = jnp.where(row > j + 1, m[:, j : j + 1], 0.0)
            c1 = jnp.where(row > j + 1, m[:, j + 1 : j + 2], 0.0)
            m = m - c0 * g0 - c1 * g1
    return out


def factor_kernel(leaf, gram_ref, x_ref, a_ref):
    n = gram_ref.shape[0]
    a_ref[...] = gram_ref[...]
    x_ref[...] = jnp.zeros_like(x_ref)
    for k in range(0, n, leaf):
        e = k + leaf
        for i, r in enumerate(small_factor(a_ref[k:e, k:e])):
            x_ref[k + i : k + i + 1, k:e] = r
        xk = x_ref[k:e, k:e]
        if e < n:
            t = nn(xk, a_ref[k:e, e:], HIGH)
            a_ref[k:e, e:] = t
            a_ref[e:, e:] -= tn(t, t, HIGH)
        if k > 0:
            x_ref[k:e, :k] = -nn(xk, tn(a_ref[:k, k:e], x_ref[:k, :k], HIGH), HIGH)


def factor(gram):
    n = gram.shape[0]
    return pl.pallas_call(
        functools.partial(factor_kernel, 64),
        out_shape=jax.ShapeDtypeStruct((n, n), jnp.float32),
        scratch_shapes=[pltpu.VMEM((n, n), jnp.float32)],
        compiler_params=params(),
        cost_estimate=cost(2e10, 8 * n * n),
        name="factor",
    )(gram)


def share_parts(x):
    groups = lax.axis_size("cols")
    if groups == 2:
        peer = lax.ppermute(x, "cols", [(0, 1), (1, 0)])
        return [x, peer]
    full = lax.all_gather(x, "cols", axis=0, tiled=False)
    return [full[i] for i in range(groups)]


def part_offsets(feat):
    groups = lax.axis_size("cols")
    if groups == 2:
        c = lax.axis_index("cols")
        return jnp.stack([c * feat, (1 - c) * feat]).astype(jnp.int32)
    return jnp.arange(groups, dtype=jnp.int32) * feat


def join_copies(parts, off_ref, x_ref, sems, spans):
    feat = parts[0].shape[1]
    return [
        [
            pltpu.make_async_copy(
                ref.at[pl.ds(start, size)],
                x_ref.at[pl.ds(start, size), pl.ds(pl.multiple_of(off_ref[i], 128), feat)],
                sems.at[t, i],
            )
            for i, ref in enumerate(parts)
        ]
        for t, (start, size) in enumerate(spans)
    ]


def row_scale(x, weight):
    x = x.astype(jnp.float32)
    return weight / (jnp.sum(x * x, axis=1, keepdims=True) / x.shape[1] + EPSILON)


def column_scale(s):
    s = s.astype(jnp.float32)
    width = s.shape[1]
    scale = 1.0 / (width * (jnp.sum(s * s, axis=1, keepdims=True) / width + EPSILON))
    return jnp.broadcast_to(scale, (s.shape[0], 128)).T[:1, :]


def row_tiles(rows):
    blocks = rows // BLK
    per = 5 if blocks % 5 == 0 else 1
    return per, [(i * BLK, per * BLK) for i in range(0, blocks, per)]


def panel_kernel(nparts, cnt_ref, off_ref, w_ref, *refs):
    parts = refs[:nparts]
    sp_ref, gram_ref, pw_ref, x_ref, sems = refs[nparts:]
    per, tiles = row_tiles(x_ref.shape[0])
    count = cnt_ref[0]
    copies = join_copies(parts, off_ref, x_ref, sems, tiles)
    for group in copies:
        for c in group:
            c.start()
    gram_ref[...] = jnp.zeros_like(gram_ref)
    pw_ref[...] = jnp.zeros_like(pw_ref)
    points = column_scale(sp_ref[...])
    for t, (start, size) in enumerate(tiles):
        for c in copies[t]:
            c.wait()

        @pl.when(t * per < count)
        def _():
            scales = []
            for b in range(per):
                j = t * per + b
                w = jnp.where(j < count, w_ref[j], 0.0)
                scales.append(row_scale(x_ref[j * BLK : (j + 1) * BLK, :], w))
            scale = jnp.concatenate(scales, axis=0)
            inner = nt(x_ref[start : start + size, :], sp_ref[...])
            panel = (inner * inner * scale * points).astype(jnp.bfloat16)
            gram_ref[...] += tn(panel, panel)
            pw_ref[start : start + size, :] = (panel.astype(jnp.float32) * scale).astype(
                jnp.bfloat16
            )


def panel_products(parts, offsets, count, weights, sp):
    rows, feat = parts[0].shape
    width = sp.shape[1]
    tiles = len(row_tiles(rows)[1])
    return pl.pallas_call(
        functools.partial(panel_kernel, len(parts)),
        out_shape=(
            jax.ShapeDtypeStruct((PANEL, PANEL), jnp.float32),
            jax.ShapeDtypeStruct((rows, PANEL), jnp.bfloat16),
        ),
        in_specs=[SMEM, SMEM, SMEM] + [ANY] * len(parts) + [VMEM],
        out_specs=(VMEM, VMEM),
        scratch_shapes=[
            pltpu.VMEM((rows, width), jnp.bfloat16),
            pltpu.SemaphoreType.DMA((tiles, len(parts))),
        ],
        compiler_params=params(),
        cost_estimate=cost(2 * rows * PANEL * (width + PANEL), 2 * rows * width),
        name="panel_products",
    )(count, offsets, weights, *parts, sp)


def column_kernel(nparts, off_ref, *refs):
    parts = refs[:nparts]
    pw_ref, s_ref, g_ref, x_ref, sems = refs[nparts:]
    width = x_ref.shape[1]

    @pl.when(pl.program_id(0) == 0)
    def _():
        copies = join_copies(parts, off_ref, x_ref, sems, row_tiles(x_ref.shape[0])[1])
        for group in copies:
            for c in group:
                c.start()
        for group in copies:
            for c in group:
                c.wait()

    s = s_ref[...]
    inner = nt(s, x_ref[...])
    products = nn((inner * inner).astype(jnp.bfloat16), pw_ref[...])
    wide = s.astype(jnp.float32)
    square = jnp.sum(wide * wide, axis=1, keepdims=True) / width + EPSILON
    g_ref[...] = products / (width * square)


def column_products(parts, offsets, pw, s):
    rows, feat = parts[0].shape
    size, width = s.shape
    chunk = min(512, size)
    tiles = len(row_tiles(rows)[1])
    once = pl.Buffered(1)
    return pl.pallas_call(
        functools.partial(column_kernel, len(parts)),
        grid=(size // chunk,),
        out_shape=jax.ShapeDtypeStruct((size, PANEL), jnp.float32),
        in_specs=[SMEM]
        + [ANY] * len(parts)
        + [
            pl.BlockSpec((rows, PANEL), lambda i: (0, 0), pipeline_mode=once),
            pl.BlockSpec((chunk, width), lambda i: (i, 0)),
        ],
        out_specs=pl.BlockSpec((chunk, PANEL), lambda i: (i, 0)),
        scratch_shapes=[
            pltpu.VMEM((rows, width), jnp.bfloat16),
            pltpu.SemaphoreType.DMA((tiles, len(parts))),
        ],
        compiler_params=params(dimension_semantics=("arbitrary",)),
        cost_estimate=cost(2 * rows * (width + PANEL) * size, 2 * rows * width),
        name="column_products",
    )(offsets, *parts, pw, s)


def remainder_kernel(nparts, norm, quarter_ref, off_ref, w_ref, group_ref, *refs):
    parts = refs[:nparts]
    sp_ref, s_ref, inv_ref, rt_ref, out_ref, proj_ref, x_ref, p_ref, rs_ref, sems = refs[nparts:]
    rows_all, width = x_ref.shape
    chunk = s_ref.shape[0]
    step = pl.program_id(0)
    blocks = rows_all // BLK
    bounds = list(range(0, blocks, 7)) + [blocks]
    spans = [(a * BLK, b * BLK) for a, b in zip(bounds, bounds[1:])]

    @pl.when(step == 0)
    def _():
        copies = join_copies(parts, off_ref, x_ref, sems, [(a, b - a) for a, b in spans])
        for group in copies:
            for c in group:
                c.start()
        points = column_scale(sp_ref[...])
        for (a, b), group in zip(spans, copies):
            for c in group:
                c.wait()
            for j in range(a // BLK, b // BLK):
                scale = row_scale(x_ref[j * BLK : (j + 1) * BLK, :], w_ref[j])
                rs_ref[j * BLK : (j + 1) * BLK, :] = jnp.broadcast_to(scale, (BLK, 128))
            inner = nt(x_ref[a:b, :], sp_ref[...])
            scale = jnp.concatenate([rs_ref[a:b, :]] * (PANEL // 128), axis=1)
            p_ref[a:b, :] = (inner * inner * scale * points).astype(jnp.bfloat16)

    inv_high, inv_low = split(inv_ref[...])
    rt = rt_ref[0]
    coef = (nn(rt, inv_high) + nn(rt, inv_low)).astype(jnp.bfloat16)
    proj_ref[...] = rt.astype(jnp.float32).T * (1.0 / norm)
    columns = column_scale(s_ref[...])
    for a, b in spans:
        inner = nt(x_ref[a:b, :], s_ref[...])
        scale = jnp.concatenate([rs_ref[a:b, :]] * (chunk // 128), axis=1)
        kern = (inner * inner * scale * columns).astype(jnp.bfloat16)
        fit = nt(p_ref[a:b, :], coef)
        out_ref[a:b, :] = (kern.astype(jnp.float32) - fit).astype(out_ref.dtype)

    for i in range(-(-PANEL // chunk)):
        part = min(chunk, PANEL)

        @pl.when((step == i) & (group_ref[0] == 0))
        def _():
            for a, b in spans:
                panel = p_ref[a:b, :]
                rows = slice(i * part, (i + 1) * part)
                basis = nt(panel, inv_high[rows, :]) + nt(panel, inv_low[rows, :])
                out_ref[a:b, :part] = (basis * norm).astype(out_ref.dtype)


def remainder_rows(parts, offsets, weights, group, quarter, sp, s, inverse, rt, norm):
    rows, feat = parts[0].shape
    cols, width = s.shape
    chunk = rt.shape[1]
    once = pl.Buffered(1)
    spec = pltpu.PrefetchScalarGridSpec(
        num_scalar_prefetch=1,
        grid=(cols // chunk,),
        in_specs=[SMEM, SMEM, SMEM]
        + [ANY] * len(parts)
        + [
            pl.BlockSpec((PANEL, width), lambda i, q: (0, 0), pipeline_mode=once),
            pl.BlockSpec((chunk, width), lambda i, q: (i, 0)),
            pl.BlockSpec((PANEL, PANEL), lambda i, q: (0, 0), pipeline_mode=once),
            pl.BlockSpec((1, chunk, PANEL), lambda i, q: (i ^ q[0], 0, 0)),
        ],
        out_specs=(
            pl.BlockSpec((rows, chunk), lambda i, q: (0, i)),
            pl.BlockSpec((PANEL, chunk), lambda i, q: (0, i)),
        ),
        scratch_shapes=[
            pltpu.VMEM((rows, width), jnp.bfloat16),
            pltpu.VMEM((rows, PANEL), jnp.bfloat16),
            pltpu.VMEM((rows, 128), jnp.float32),
            pltpu.SemaphoreType.DMA((2, len(parts))),
        ],
    )
    return pl.pallas_call(
        functools.partial(remainder_kernel, len(parts), norm),
        grid_spec=spec,
        out_shape=(
            jax.ShapeDtypeStruct((rows, cols), jnp.bfloat16),
            jax.ShapeDtypeStruct((PANEL, cols), jnp.float32),
        ),
        compiler_params=params(dimension_semantics=("arbitrary",)),
        cost_estimate=cost(
            2 * rows * (width + 2 * PANEL) * cols, 2 * rows * width + 2 * cols * width + 2 * rows * cols
        ),
        name="remainder_rows",
    )(quarter, offsets, weights, group, *parts, sp, s, inverse, rt)


def flips(bit, size):
    return [(i, i ^ bit) for i in range(size)]


def quarter_of(pair):
    me = lax.axis_index("rows").astype(jnp.int32)
    return (me // pair[0]) % 2 + 2 * ((me // pair[1]) % 2)


def trade(x, pair, k):
    bit = pair[0] * (k & 1) + pair[1] * (k >> 1)
    return lax.ppermute(x, "rows", flips(bit, lax.axis_size("rows")))


def scatter_sum(x, pair):
    n = x.shape[0] // 4
    q = quarter_of(pair)
    pieces = [lax.dynamic_slice_in_dim(x, (q ^ k) * n, n, 0) for k in range(4)]
    got = [pieces[0]] + [trade(pieces[k], pair, k) for k in range(1, 4)]
    return (got[0] + got[1]) + (got[2] + got[3])


def halve_sum(x, bit):
    half = x.shape[0] // 2
    upper = (lax.axis_index("rows") // bit) % 2
    send = lax.dynamic_slice_in_dim(x, (1 - upper) * half, half, 0)
    kept = lax.dynamic_slice_in_dim(x, upper * half, half, 0)
    return kept + lax.ppermute(send, "rows", flips(bit, lax.axis_size("rows")))


def gather_pieces(x, pair):
    return [x] + [trade(x, pair, k) for k in range(1, 4)]


def gather_back(x, pair):
    n = x.shape[0]
    q = quarter_of(pair)
    pieces = gather_pieces(x, pair)
    return jnp.concatenate(
        [lax.select_n(q ^ i, *pieces) for i in range(4)], 0
    )


def pair_sum(x, pair):
    got = gather_pieces(x, pair)
    return (got[0] + got[1]) + (got[2] + got[3])


def on_device(descriptors, sparse_points, block_weights, block_counts, destinations):
    owners = lax.axis_size("rows")
    groups = lax.axis_size("cols")
    me = lax.axis_index("rows").astype(jnp.int32)
    group = lax.axis_index("cols").astype(jnp.int32)
    slots = block_weights.shape[0]
    per_pair = -(-slots // owners)
    feat = descriptors.shape[1]
    cols, width = sparse_points.shape
    norm = math.sqrt(owners * DST_BLK * BLK)
    near = (1, 2)
    far = [1 << i for i in range(2, owners.bit_length() - 1)]

    first = sparse_points[:PANEL]
    source_parts = share_parts(descriptors)
    if groups == 2:
        moved = lax.ppermute(first, "cols", [(0, 1), (1, 0)])
        panel_points = jnp.where(group == 0, first, moved)
    else:
        panel_points = lax.all_gather(first, "cols", axis=0, tiled=False)[0]
    desc_blocks = descriptors.reshape(slots, BLK, feat)
    outgoing = pack(desc_blocks, me[None], destinations, block_counts, per_pair)
    received = [lax.all_to_all(outgoing[0], "rows", split_axis=0, concat_axis=0, tiled=True)]

    offsets = part_offsets(feat)
    count = lax.dynamic_index_in_dim(block_counts, me, 0)
    weights32 = block_weights.astype(jnp.float32)
    gram_part, pw = panel_products(source_parts, offsets, count, weights32, panel_points)
    spare = -(-owners * slots // (PANEL * 8)) * 8
    table = lax.dynamic_update_slice(
        jnp.zeros((spare * PANEL,), jnp.float32), weights32, (me * slots,)
    ).reshape(spare, PANEL)
    if groups == 2:
        gram_part = lax.dynamic_slice_in_dim(gram_part, group * (PANEL // 2), PANEL // 2, 0)
    summed = pair_sum(jnp.concatenate([gram_part, table], 0), near)
    for bit in far:
        summed = summed + lax.ppermute(summed, "rows", flips(bit, owners))
    gram, table = summed[:-spare], summed[-spare:]
    if groups == 2:
        other = lax.ppermute(gram, "cols", [(0, 1), (1, 0)])
        gram = jnp.where(
            group == 0, jnp.concatenate([gram, other], 0), jnp.concatenate([other, gram], 0)
        )
    all_weights = table.reshape(-1)[: owners * slots]
    inverse = factor(gram)

    g = scatter_sum(column_products(source_parts, offsets, pw, sparse_points), near)
    for bit in far:
        g = halve_sum(g, bit)
    if per_pair > 1:
        g, last = lax.optimization_barrier((g, outgoing[1]))
        received.append(lax.all_to_all(last, "rows", split_axis=0, concat_axis=0, tiled=True))
    rt = nt(g, inverse, HIGH).astype(jnp.bfloat16)
    for i in range(len(far) - 1, 0, -2):
        rt = gather_back(rt, (far[i], far[i - 1]))

    slot_ids = jnp.arange(slots, dtype=jnp.int32)
    toward = ((slot_ids[None, :] < block_counts[:, None]) & (destinations == me)).astype(jnp.int32)
    rank = jnp.cumsum(toward, axis=1) - toward
    flat = toward.reshape(-1)
    place = jnp.cumsum(flat) - flat
    where_from = (jnp.arange(owners, dtype=jnp.int32)[:, None] * per_pair + rank).reshape(-1)
    hit = (flat[None, :] == 1) & (place[None, :] == jnp.arange(DST_BLK, dtype=jnp.int32)[:, None])
    positions = jnp.sum(jnp.where(hit, where_from[None, :], 0), axis=1)
    weights_here = jnp.sum(jnp.where(hit, all_weights[None, :], 0.0), axis=1)

    rt, positions = lax.optimization_barrier((rt, positions))
    rt = jnp.stack(gather_pieces(rt, near))
    arrived = select(received, positions).reshape(DST_BLK * BLK, feat)
    remainder, projected = remainder_rows(
        share_parts(arrived),
        offsets,
        weights_here,
        group[None],
        quarter_of(near)[None],
        panel_points,
        sparse_points,
        inverse,
        rt,
        norm,
    )
    return (projected, remainder)


def solution(mesh):
    return jax.shard_map(
        on_device,
        mesh=mesh,
        in_specs=(P("rows", "cols"), P("cols", None), P("rows"), P(), P()),
        out_specs=(P(None, "cols"), P("rows", "cols")),
        check_vma=False,
    )
```

```python
import functools
import math

import jax
import jax.numpy as jnp
from jax import lax
from jax.experimental import pallas as pl
from jax.experimental.pallas import tpu as pltpu
from jax.sharding import PartitionSpec as P

PANEL = 256
BLK = 128
DST_BLK = 13
EPSILON = 1e-06
VMEM_LIMIT = 56 * 1024 * 1024
HIGH = lax.Precision.HIGHEST
ANY = pl.BlockSpec(memory_space=pl.ANY)
VMEM = pl.BlockSpec(memory_space=pltpu.VMEM)
SMEM = pl.BlockSpec(memory_space=pltpu.SMEM)


def params(**kw):
    return pltpu.CompilerParams(vmem_limit_bytes=VMEM_LIMIT, **kw)


def cost(flops, nbytes):
    return pl.CostEstimate(flops=int(flops), bytes_accessed=int(nbytes), transcendentals=0)


def dot(a, b, ca, cb, precision=None):
    return lax.dot_general(
        a, b, (((ca,), (cb,)), ((), ())), preferred_element_type=jnp.float32, precision=precision
    )


def nt(a, b, precision=None):
    return dot(a, b, 1, 1, precision)


def nn(a, b, precision=None):
    return dot(a, b, 1, 0, precision)


def tn(a, b, precision=None):
    return dot(a, b, 0, 0, precision)


def split(x):
    high = x.astype(jnp.bfloat16)
    return high, (x - high.astype(jnp.float32)).astype(jnp.bfloat16)


HEAD = 64


def block_copies(rank, whole_ref, outer, first_ref, last_ref, sems):
    if rank == 0:
        pairs = [(whole_ref, first_ref.at[outer, pl.ds(0, BLK)])]
    else:
        pairs = [
            (whole_ref.at[pl.ds(0, HEAD)], first_ref.at[outer, pl.ds(BLK, HEAD)]),
            (whole_ref.at[pl.ds(HEAD, BLK - HEAD)], last_ref.at[outer]),
        ]
    return [(a, b, sems.at[i]) for i, (a, b) in enumerate(pairs)]


def pack_kernel(per_pair, dest_ref, cnt_ref, desc_ref, *refs):
    out_refs, (ctr_ref, rank_ref, sems) = refs[:per_pair], refs[per_pair:]
    slots = desc_ref.shape[0]
    owners = ctr_ref.shape[0]
    me = lax.axis_index("rows")
    count = cnt_ref[me]

    def copies(j, d, rank):
        moves = block_copies(rank, desc_ref.at[j], d, out_refs[0], out_refs[-1], sems.at[j])
        return [pltpu.make_async_copy(a, b, sem) for a, b, sem in moves]

    @pl.loop(0, owners)
    def _(i):
        ctr_ref[i] = 0

    @pl.loop(0, slots)
    def _(j):
        @pl.when(j < count)
        def _():
            d = dest_ref[me, j]
            rank = ctr_ref[d]
            ctr_ref[d] = rank + 1
            rank_ref[j] = rank
            for r in range(per_pair):
                @pl.when(rank == r)
                def _():
                    for c in copies(j, d, r):
                        c.start()

    @pl.loop(0, slots)
    def _(j):
        @pl.when(j < count)
        def _():
            for r in range(per_pair):
                @pl.when(rank_ref[j] == r)
                def _():
                    for c in copies(j, 0, r):
                        c.wait()


def pack(desc_blocks, destinations, counts, per_pair):
    slots, blk, feat = desc_blocks.shape
    owners = destinations.shape[0]
    heights = [blk] if per_pair == 1 else [blk + HEAD, blk - HEAD]
    return pl.pallas_call(
        functools.partial(pack_kernel, per_pair),
        out_shape=[
            jax.ShapeDtypeStruct((owners, h, feat), desc_blocks.dtype) for h in heights
        ],
        in_specs=[SMEM, SMEM, VMEM],
        out_specs=[ANY] * per_pair,
        scratch_shapes=[
            pltpu.SMEM((owners,), jnp.int32),
            pltpu.SMEM((slots,), jnp.int32),
            pltpu.SemaphoreType.DMA((slots, 2)),
        ],
        compiler_params=params(),
        cost_estimate=cost(0, 4 * slots * blk * feat),
        name="pack",
    )(destinations, counts, desc_blocks)


def select_kernel(per_pair, pos_ref, *refs):
    recv_refs, (out_ref, sems) = refs[:per_pair], refs[per_pair:]

    def copies(p, rank):
        owner = pos_ref[p] // per_pair
        moves = block_copies(rank, out_ref.at[p], owner, recv_refs[0], recv_refs[-1], sems.at[p])
        return [pltpu.make_async_copy(b, a, sem) for a, b, sem in moves]

    for act in ("start", "wait"):
        for p in range(DST_BLK):
            for r in range(per_pair):
                @pl.when(pos_ref[p] % per_pair == r)
                def _():
                    for c in copies(p, r):
                        getattr(c, act)()


def select(received, positions):
    feat = received[0].shape[-1]
    return pl.pallas_call(
        functools.partial(select_kernel, len(received)),
        out_shape=jax.ShapeDtypeStruct((DST_BLK, BLK, feat), received[0].dtype),
        in_specs=[SMEM] + [ANY] * len(received),
        out_specs=VMEM,
        scratch_shapes=[pltpu.SemaphoreType.DMA((DST_BLK, 2))],
        compiler_params=params(),
        cost_estimate=cost(0, 4 * DST_BLK * BLK * feat),
        name="select",
    )(positions, *received)


def small_factor(a):
    n = a.shape[0]
    row = lax.broadcasted_iota(jnp.int32, (n, 1), 0)
    eye = lax.broadcasted_iota(jnp.int32, (n, n), 0) == lax.broadcasted_iota(jnp.int32, (n, n), 1)
    m = jnp.concatenate([a, eye.astype(jnp.float32)], axis=1)
    out = []
    for j in range(0, n, 2):
        r0 = m[j : j + 1, :]
        r1 = m[j + 1 : j + 2, :]
        p = r0[:, j : j + 1]
        q = r0[:, j + 1 : j + 2]
        s = r1[:, j + 1 : j + 2]
        det = p * s - q * q
        out.append(r0[:, n:] * lax.rsqrt(p))
        out.append((r1[:, n:] - (q / p) * r0[:, n:]) * lax.rsqrt(det / p))
        if j + 2 < n:
            inv = 1.0 / det
            g0 = (s * r0 - q * r1) * inv
            g1 = (p * r1 - q * r0) * inv
            c0 = jnp.where(row > j + 1, m[:, j : j + 1], 0.0)
            c1 = jnp.where(row > j + 1, m[:, j + 1 : j + 2], 0.0)
            m = m - c0 * g0 - c1 * g1
    return out


def factor_kernel(leaf, gram_ref, x_ref, a_ref):
    n = gram_ref.shape[0]
    a_ref[...] = gram_ref[...]
    x_ref[...] = jnp.zeros_like(x_ref)
    for k in range(0, n, leaf):
        e = k + leaf
        for i, r in enumerate(small_factor(a_ref[k:e, k:e])):
            x_ref[k + i : k + i + 1, k:e] = r
        xk = x_ref[k:e, k:e]
        if e < n:
            t = nn(xk, a_ref[k:e, e:], HIGH)
            a_ref[k:e, e:] = t
            a_ref[e:, e:] -= tn(t, t, HIGH)
        if k > 0:
            x_ref[k:e, :k] = -nn(xk, tn(a_ref[:k, k:e], x_ref[:k, :k], HIGH), HIGH)


def factor(gram):
    n = gram.shape[0]
    return pl.pallas_call(
        functools.partial(factor_kernel, 64),
        out_shape=jax.ShapeDtypeStruct((n, n), jnp.float32),
        scratch_shapes=[pltpu.VMEM((n, n), jnp.float32)],
        compiler_params=params(),
        cost_estimate=cost(2e10, 8 * n * n),
        name="factor",
    )(gram)


def share_parts(x):
    groups = lax.axis_size("cols")
    if groups == 2:
        peer = lax.ppermute(x, "cols", [(0, 1), (1, 0)])
        return [x, peer]
    full = lax.all_gather(x, "cols", axis=0, tiled=False)
    return [full[i] for i in range(groups)]


def part_offset(i, feat):
    if lax.axis_size("cols") == 2:
        c = lax.axis_index("cols")
        return (c if i == 0 else 1 - c) * feat
    return i * feat


def join_copies(parts, x_ref, sems, spans):
    feat = parts[0].shape[1]
    return [
        [
            pltpu.make_async_copy(
                ref.at[pl.ds(start, size)],
                x_ref.at[pl.ds(start, size), pl.ds(pl.multiple_of(part_offset(i, feat), 128), feat)],
                sems.at[t, i],
            )
            for i, ref in enumerate(parts)
        ]
        for t, (start, size) in enumerate(spans)
    ]


def row_scale(x, weight):
    x = x.astype(jnp.float32)
    return weight / (jnp.sum(x * x, axis=1, keepdims=True) / x.shape[1] + EPSILON)


def column_scale(s):
    s = s.astype(jnp.float32)
    width = s.shape[1]
    scale = 1.0 / (width * (jnp.sum(s * s, axis=1, keepdims=True) / width + EPSILON))
    return jnp.broadcast_to(scale, (s.shape[0], 128)).T[:1, :]


def row_tiles(rows):
    blocks = rows // BLK
    per = 5 if blocks % 5 == 0 else 1
    return per, [(i * BLK, per * BLK) for i in range(0, blocks, per)]


def panel_kernel(nparts, cnt_ref, w_ref, *refs):
    parts = refs[:nparts]
    s_ref, moved_ref, gram_ref, pw_ref, sp_ref, x_ref, sems, sp_sem = refs[nparts:]
    per, tiles = row_tiles(x_ref.shape[0])
    count = cnt_ref[lax.axis_index("rows")]
    group = lax.axis_index("cols")
    own = pltpu.make_async_copy(s_ref.at[pl.ds(0, PANEL)], sp_ref, sp_sem)
    other = pltpu.make_async_copy(moved_ref, sp_ref, sp_sem)

    @pl.when(group == 0)
    def _():
        own.start()

    @pl.when(group != 0)
    def _():
        other.start()

    copies = join_copies(parts, x_ref, sems, tiles)
    for moves in copies:
        for c in moves:
            c.start()
    gram_ref[...] = jnp.zeros_like(gram_ref)
    pw_ref[...] = jnp.zeros_like(pw_ref)

    @pl.when(group == 0)
    def _():
        own.wait()

    @pl.when(group != 0)
    def _():
        other.wait()

    points = column_scale(sp_ref[...])
    for t, (start, size) in enumerate(tiles):
        for c in copies[t]:
            c.wait()

        @pl.when(t * per < count)
        def _():
            scales = []
            for b in range(per):
                j = t * per + b
                w = jnp.where(j < count, w_ref[j], 0.0)
                scales.append(row_scale(x_ref[j * BLK : (j + 1) * BLK, :], w))
            scale = jnp.concatenate(scales, axis=0)
            inner = nt(x_ref[start : start + size, :], sp_ref[...])
            panel = (inner * inner * scale * points).astype(jnp.bfloat16)
            gram_ref[...] += tn(panel, panel)
            pw_ref[start : start + size, :] = (panel.astype(jnp.float32) * scale).astype(
                jnp.bfloat16
            )


def panel_products(parts, counts, weights, s, moved):
    rows, feat = parts[0].shape
    width = s.shape[1]
    tiles = len(row_tiles(rows)[1])
    return pl.pallas_call(
        functools.partial(panel_kernel, len(parts)),
        out_shape=(
            jax.ShapeDtypeStruct((PANEL, PANEL), jnp.float32),
            jax.ShapeDtypeStruct((rows, PANEL), jnp.bfloat16),
            jax.ShapeDtypeStruct((PANEL, width), jnp.bfloat16),
        ),
        in_specs=[SMEM, SMEM] + [ANY] * (len(parts) + 2),
        out_specs=(VMEM, VMEM, VMEM),
        scratch_shapes=[
            pltpu.VMEM((rows, width), jnp.bfloat16),
            pltpu.SemaphoreType.DMA((tiles, len(parts))),
            pltpu.SemaphoreType.DMA,
        ],
        compiler_params=params(),
        cost_estimate=cost(2 * rows * PANEL * (width + PANEL), 2 * rows * width),
        name="panel_products",
    )(counts, weights, *parts, s, moved)


def column_kernel(nparts, *refs):
    parts = refs[:nparts]
    pw_ref, s_ref, g_ref, x_ref, sems = refs[nparts:]
    width = x_ref.shape[1]

    @pl.when(pl.program_id(0) == 0)
    def _():
        copies = join_copies(parts, x_ref, sems, row_tiles(x_ref.shape[0])[1])
        for group in copies:
            for c in group:
                c.start()
        for group in copies:
            for c in group:
                c.wait()

    s = s_ref[...]
    inner = nt(s, x_ref[...])
    products = nn((inner * inner).astype(jnp.bfloat16), pw_ref[...])
    wide = s.astype(jnp.float32)
    square = jnp.sum(wide * wide, axis=1, keepdims=True) / width + EPSILON
    g_ref[...] = products / (width * square)


def column_products(parts, pw, s):
    rows, feat = parts[0].shape
    size, width = s.shape
    chunk = min(512, size)
    tiles = len(row_tiles(rows)[1])
    once = pl.Buffered(1)
    return pl.pallas_call(
        functools.partial(column_kernel, len(parts)),
        grid=(size // chunk,),
        out_shape=jax.ShapeDtypeStruct((size, PANEL), jnp.float32),
        in_specs=[ANY] * len(parts)
        + [
            pl.BlockSpec((rows, PANEL), lambda i: (0, 0), pipeline_mode=once),
            pl.BlockSpec((chunk, width), lambda i: (i, 0)),
        ],
        out_specs=pl.BlockSpec((chunk, PANEL), lambda i: (i, 0)),
        scratch_shapes=[
            pltpu.VMEM((rows, width), jnp.bfloat16),
            pltpu.SemaphoreType.DMA((tiles, len(parts))),
        ],
        compiler_params=params(dimension_semantics=("arbitrary",)),
        cost_estimate=cost(2 * rows * (width + PANEL) * size, 2 * rows * width),
        name="column_products",
    )(*parts, pw, s)


def rows_kernel(nparts, w_ref, *refs):
    parts = refs[:nparts]
    sp_ref, s_ref, kern_ref, p_ref, x_ref, rs_ref, sems = refs[nparts:]
    rows_all = x_ref.shape[0]
    chunk = s_ref.shape[0]
    blocks = rows_all // BLK
    bounds = list(range(0, blocks, 7)) + [blocks]
    spans = [(a * BLK, b * BLK) for a, b in zip(bounds, bounds[1:])]

    @pl.when(pl.program_id(0) == 0)
    def _():
        copies = join_copies(parts, x_ref, sems, [(a, b - a) for a, b in spans])
        for moves in copies:
            for c in moves:
                c.start()
        points = column_scale(sp_ref[...])
        for (a, b), moves in zip(spans, copies):
            for c in moves:
                c.wait()
            for j in range(a // BLK, b // BLK):
                scale = row_scale(x_ref[j * BLK : (j + 1) * BLK, :], w_ref[j])
                rs_ref[j * BLK : (j + 1) * BLK, :] = jnp.broadcast_to(scale, (BLK, 128))
            inner = nt(x_ref[a:b, :], sp_ref[...])
            scale = jnp.concatenate([rs_ref[a:b, :]] * (PANEL // 128), axis=1)
            p_ref[a:b, :] = (inner * inner * scale * points).astype(jnp.bfloat16)

    columns = column_scale(s_ref[...])
    for a, b in spans:
        inner = nt(x_ref[a:b, :], s_ref[...])
        scale = jnp.concatenate([rs_ref[a:b, :]] * (chunk // 128), axis=1)
        kern_ref[a:b, :] = (inner * inner * scale * columns).astype(jnp.bfloat16)


def kernel_rows(parts, weights, sp, s):
    rows, feat = parts[0].shape
    cols, width = s.shape
    chunk = min(512, cols)
    once = pl.Buffered(1)
    return pl.pallas_call(
        functools.partial(rows_kernel, len(parts)),
        grid=(cols // chunk,),
        out_shape=(
            jax.ShapeDtypeStruct((rows, cols), jnp.bfloat16),
            jax.ShapeDtypeStruct((rows, PANEL), jnp.bfloat16),
        ),
        in_specs=[SMEM]
        + [ANY] * len(parts)
        + [
            pl.BlockSpec((PANEL, width), lambda i: (0, 0), pipeline_mode=once),
            pl.BlockSpec((chunk, width), lambda i: (i, 0)),
        ],
        out_specs=(
            pl.BlockSpec((rows, chunk), lambda i: (0, i)),
            pl.BlockSpec((rows, PANEL), lambda i: (0, 0)),
        ),
        scratch_shapes=[
            pltpu.VMEM((rows, width), jnp.bfloat16),
            pltpu.VMEM((rows, 128), jnp.float32),
            pltpu.SemaphoreType.DMA((2, len(parts))),
        ],
        compiler_params=params(dimension_semantics=("arbitrary",)),
        cost_estimate=cost(
            2 * rows * width * (cols + PANEL), 2 * rows * width + 2 * cols * width + 2 * rows * cols
        ),
        name="kernel_rows",
    )(weights, *parts, sp, s)


def remainder_kernel(norm, quarter_ref, kern_ref, p_ref, inv_ref, rt_ref, out_ref, proj_ref):
    chunk = kern_ref.shape[1]
    step = pl.program_id(0)
    inv_high, inv_low = split(inv_ref[...])
    rt = rt_ref[0]
    coef = (nn(rt, inv_high) + nn(rt, inv_low)).astype(jnp.bfloat16)
    proj_ref[...] = rt.astype(jnp.float32).T * (1.0 / norm)
    fit = nt(p_ref[...], coef)
    out_ref[...] = (kern_ref[...].astype(jnp.float32) - fit).astype(out_ref.dtype)

    part = min(chunk, PANEL)
    for i in range(PANEL // part):
        @pl.when((step == i) & (lax.axis_index("cols") == 0))
        def _():
            panel = p_ref[...]
            rows = slice(i * part, (i + 1) * part)
            basis = nt(panel, inv_high[rows, :]) + nt(panel, inv_low[rows, :])
            out_ref[:, :part] = (basis * norm).astype(out_ref.dtype)


def remainder_rows(kern, panel, quarter, inverse, rt, norm):
    rows, cols = kern.shape
    chunk = rt.shape[1]
    once = pl.Buffered(1)
    spec = pltpu.PrefetchScalarGridSpec(
        num_scalar_prefetch=1,
        grid=(cols // chunk,),
        in_specs=[
            pl.BlockSpec((rows, chunk), lambda i, q: (0, i)),
            pl.BlockSpec((rows, PANEL), lambda i, q: (0, 0), pipeline_mode=once),
            pl.BlockSpec((PANEL, PANEL), lambda i, q: (0, 0), pipeline_mode=once),
            pl.BlockSpec((1, chunk, PANEL), lambda i, q: (i ^ q[0], 0, 0)),
        ],
        out_specs=(
            pl.BlockSpec((rows, chunk), lambda i, q: (0, i)),
            pl.BlockSpec((PANEL, chunk), lambda i, q: (0, i)),
        ),
    )
    return pl.pallas_call(
        functools.partial(remainder_kernel, norm),
        grid_spec=spec,
        out_shape=(
            jax.ShapeDtypeStruct((rows, cols), jnp.bfloat16),
            jax.ShapeDtypeStruct((PANEL, cols), jnp.float32),
        ),
        compiler_params=params(dimension_semantics=("arbitrary",)),
        cost_estimate=cost(2 * rows * PANEL * cols, 4 * rows * cols),
        name="remainder_rows",
    )(quarter, kern, panel, inverse, rt)


def flips(bit, size):
    return [(i, i ^ bit) for i in range(size)]


def quarter_of(pair):
    me = lax.axis_index("rows").astype(jnp.int32)
    return (me // pair[0]) % 2 + 2 * ((me // pair[1]) % 2)


def trade(x, pair, k):
    bit = pair[0] * (k & 1) + pair[1] * (k >> 1)
    return lax.ppermute(x, "rows", flips(bit, lax.axis_size("rows")))


def scatter_sum(x, pair):
    n = x.shape[0] // 4
    q = quarter_of(pair)
    pieces = [lax.dynamic_slice_in_dim(x, (q ^ k) * n, n, 0) for k in range(4)]
    got = [pieces[0]] + [trade(pieces[k], pair, k) for k in range(1, 4)]
    return (got[0] + got[1]) + (got[2] + got[3])


def gather_pieces(x, pair):
    return [x] + [trade(x, pair, k) for k in range(1, 4)]


def gather_back(x, pair):
    n = x.shape[0]
    q = quarter_of(pair)
    pieces = gather_pieces(x, pair)
    return jnp.concatenate(
        [lax.select_n(q ^ i, *pieces) for i in range(4)], 0
    )


def pair_sum(x, pair):
    got = gather_pieces(x, pair)
    return (got[0] + got[1]) + (got[2] + got[3])


def on_device(descriptors, sparse_points, block_weights, block_counts, destinations):
    owners = lax.axis_size("rows")
    groups = lax.axis_size("cols")
    me = lax.axis_index("rows").astype(jnp.int32)
    group = lax.axis_index("cols").astype(jnp.int32)
    slots = block_weights.shape[0]
    per_pair = -(-slots // owners)
    feat = descriptors.shape[1]
    cols, width = sparse_points.shape
    norm = math.sqrt(owners * DST_BLK * BLK)
    pairs = [(1 << i, 2 << i) for i in range(0, owners.bit_length() - 1, 2)]

    first = sparse_points[:PANEL]
    source_parts = share_parts(descriptors)
    if groups == 2:
        moved = lax.ppermute(first, "cols", [(0, 1), (1, 0)])
    else:
        moved = lax.all_gather(first, "cols", axis=0, tiled=False)[0]
    desc_blocks = descriptors.reshape(slots, BLK, feat)
    outgoing = pack(desc_blocks, destinations, block_counts, per_pair)
    received = [lax.all_to_all(outgoing[0], "rows", split_axis=0, concat_axis=0, tiled=True)]

    weights32 = block_weights.astype(jnp.float32)
    gram_part, pw, panel_points = panel_products(
        source_parts, block_counts, weights32, sparse_points, moved
    )
    g = column_products(source_parts, pw, sparse_points)

    spare = -(-owners * slots // (PANEL * 8)) * 8
    table = lax.dynamic_update_slice(
        jnp.zeros((spare * PANEL,), jnp.float32), weights32, (me * slots,)
    ).reshape(spare, PANEL)
    if groups == 2:
        gram_part = lax.dynamic_slice_in_dim(gram_part, group * (PANEL // 2), PANEL // 2, 0)
    summed = pair_sum(jnp.concatenate([gram_part, table], 0), pairs[0])
    summed, g = lax.optimization_barrier((summed, g))
    for pair in pairs[1:]:
        summed = pair_sum(summed, pair)
    gram, table = summed[:-spare], summed[-spare:]
    if groups == 2:
        other = lax.ppermute(gram, "cols", [(0, 1), (1, 0)])
        gram = jnp.where(
            group == 0, jnp.concatenate([gram, other], 0), jnp.concatenate([other, gram], 0)
        )
    all_weights = table.reshape(-1)[: owners * slots]

    g = scatter_sum(g, pairs[0])
    if per_pair > 1:
        g, gram, last = lax.optimization_barrier((g, gram, outgoing[1]))
    for pair in pairs[1:]:
        g = scatter_sum(g, pair)
    if per_pair > 1:
        received.append(lax.all_to_all(last, "rows", split_axis=0, concat_axis=0, tiled=True))
    inverse = factor(gram)
    rt = nt(g, inverse, HIGH).astype(jnp.bfloat16)
    for pair in pairs[:0:-1]:
        rt = gather_back(rt, pair)

    slot_ids = jnp.arange(slots, dtype=jnp.int32)
    toward = ((slot_ids[None, :] < block_counts[:, None]) & (destinations == me)).astype(jnp.int32)
    rank = jnp.cumsum(toward, axis=1) - toward
    flat = toward.reshape(-1)
    place = jnp.cumsum(flat) - flat
    where_from = (jnp.arange(owners, dtype=jnp.int32)[:, None] * per_pair + rank).reshape(-1)
    hit = (flat[None, :] == 1) & (place[None, :] == jnp.arange(DST_BLK, dtype=jnp.int32)[:, None])
    positions = jnp.sum(jnp.where(hit, where_from[None, :], 0), axis=1)
    weights_here = jnp.sum(jnp.where(hit, all_weights[None, :], 0.0), axis=1)

    rt, positions = lax.optimization_barrier((rt, positions))
    arrived = select(received, positions).reshape(DST_BLK * BLK, feat)
    kern, panel = kernel_rows(share_parts(arrived), weights_here, panel_points, sparse_points)
    pieces = gather_pieces(rt, pairs[0])
    kern, *pieces = lax.optimization_barrier((kern, *pieces))
    rt = jnp.stack(pieces)
    remainder, projected = remainder_rows(
        kern, panel, quarter_of(pairs[0])[None], inverse, rt, norm
    )
    return (projected, remainder)


def solution(mesh):
    return jax.shard_map(
        on_device,
        mesh=mesh,
        in_specs=(P("rows", "cols"), P("cols", None), P("rows"), P(), P()),
        out_specs=(P(None, "cols"), P("rows", "cols")),
        check_vma=False,
    )
```

```python
import functools
import math

import jax
import jax.numpy as jnp
from jax import lax
from jax.experimental import pallas as pl
from jax.experimental.pallas import tpu as pltpu
from jax.sharding import PartitionSpec as P

PANEL = 256
BLK = 128
DST_BLK = 13
EPSILON = 1e-06
VMEM_LIMIT = 56 * 1024 * 1024
HIGH = lax.Precision.HIGHEST
ANY = pl.BlockSpec(memory_space=pl.ANY)
VMEM = pl.BlockSpec(memory_space=pltpu.VMEM)
SMEM = pl.BlockSpec(memory_space=pltpu.SMEM)


def params(**kw):
    return pltpu.CompilerParams(vmem_limit_bytes=VMEM_LIMIT, **kw)


def cost(flops, nbytes):
    return pl.CostEstimate(flops=int(flops), bytes_accessed=int(nbytes), transcendentals=0)


def dot(a, b, ca, cb, precision=None):
    return lax.dot_general(
        a, b, (((ca,), (cb,)), ((), ())), preferred_element_type=jnp.float32, precision=precision
    )


def nt(a, b, precision=None):
    return dot(a, b, 1, 1, precision)


def nn(a, b, precision=None):
    return dot(a, b, 1, 0, precision)


def tn(a, b, precision=None):
    return dot(a, b, 0, 0, precision)


def split(x):
    high = x.astype(jnp.bfloat16)
    return high, (x - high.astype(jnp.float32)).astype(jnp.bfloat16)


def pack_kernel(per_pair, dest_ref, cnt_ref, desc_ref, *refs):
    out_refs, (ctr_ref, sems) = refs[:per_pair], refs[per_pair:]
    slots = desc_ref.shape[0]
    owners = ctr_ref.shape[0]
    me = lax.axis_index("rows")
    count = cnt_ref[me]

    def copy(j, d, rank):
        return pltpu.make_async_copy(desc_ref.at[j], out_refs[rank].at[d], sems.at[j])

    @pl.loop(0, owners)
    def _(i):
        ctr_ref[i] = 0

    @pl.loop(0, slots)
    def _(j):
        @pl.when(j < count)
        def _():
            d = dest_ref[me, j]
            rank = ctr_ref[d]
            ctr_ref[d] = rank + 1
            for r in range(per_pair):
                @pl.when(rank == r)
                def _():
                    copy(j, d, r).start()

    @pl.loop(0, slots)
    def _(j):
        @pl.when(j < count)
        def _():
            pltpu.make_async_copy(desc_ref.at[0], out_refs[0].at[0], sems.at[j]).wait()


def pack(desc_blocks, destinations, counts, per_pair):
    slots, blk, feat = desc_blocks.shape
    owners = destinations.shape[0]
    return pl.pallas_call(
        functools.partial(pack_kernel, per_pair),
        out_shape=[jax.ShapeDtypeStruct((owners, blk, feat), desc_blocks.dtype)] * per_pair,
        in_specs=[SMEM, SMEM, VMEM],
        out_specs=[ANY] * per_pair,
        scratch_shapes=[
            pltpu.SMEM((owners,), jnp.int32),
            pltpu.SemaphoreType.DMA((slots,)),
        ],
        compiler_params=params(),
        cost_estimate=cost(0, 4 * slots * blk * feat),
        name="pack",
    )(destinations, counts, desc_blocks)


def select_kernel(per_pair, pos_ref, *refs):
    recv_refs, (out_ref, sems) = refs[:per_pair], refs[per_pair:]

    def copy(p, rank):
        owner = pos_ref[p] // per_pair
        return pltpu.make_async_copy(recv_refs[rank].at[owner], out_ref.at[p], sems.at[p])

    for p in range(DST_BLK):
        for r in range(per_pair):
            @pl.when(pos_ref[p] % per_pair == r)
            def _():
                copy(p, r).start()

    for p in range(DST_BLK):
        pltpu.make_async_copy(recv_refs[0].at[0], out_ref.at[p], sems.at[p]).wait()


def select(received, positions):
    feat = received[0].shape[-1]
    return pl.pallas_call(
        functools.partial(select_kernel, len(received)),
        out_shape=jax.ShapeDtypeStruct((DST_BLK, BLK, feat), received[0].dtype),
        in_specs=[SMEM] + [ANY] * len(received),
        out_specs=VMEM,
        scratch_shapes=[pltpu.SemaphoreType.DMA((DST_BLK,))],
        compiler_params=params(),
        cost_estimate=cost(0, 4 * DST_BLK * BLK * feat),
        name="select",
    )(positions, *received)


def small_factor(a):
    n = a.shape[0]
    row = lax.broadcasted_iota(jnp.int32, (n, 1), 0)
    eye = lax.broadcasted_iota(jnp.int32, (n, n), 0) == lax.broadcasted_iota(jnp.int32, (n, n), 1)
    m = jnp.concatenate([a, eye.astype(jnp.float32)], axis=1)
    out = []
    for j in range(0, n, 2):
        r0 = m[j : j + 1, :]
        r1 = m[j + 1 : j + 2, :]
        p = r0[:, j : j + 1]
        q = r0[:, j + 1 : j + 2]
        s = r1[:, j + 1 : j + 2]
        det = p * s - q * q
        out.append(r0[:, n:] * lax.rsqrt(p))
        out.append((r1[:, n:] - (q / p) * r0[:, n:]) * lax.rsqrt(det / p))
        if j + 2 < n:
            inv = 1.0 / det
            g0 = (s * r0 - q * r1) * inv
            g1 = (p * r1 - q * r0) * inv
            c0 = jnp.where(row > j + 1, m[:, j : j + 1], 0.0)
            c1 = jnp.where(row > j + 1, m[:, j + 1 : j + 2], 0.0)
            m = m - c0 * g0 - c1 * g1
    return out


def factor_kernel(leaf, gram_ref, x_ref, a_ref):
    n = gram_ref.shape[0]
    a_ref[...] = gram_ref[...]
    x_ref[...] = jnp.zeros_like(x_ref)
    for k in range(0, n, leaf):
        e = k + leaf
        for i, r in enumerate(small_factor(a_ref[k:e, k:e])):
            x_ref[k + i : k + i + 1, k:e] = r
        xk = x_ref[k:e, k:e]
        if e < n:
            t = nn(xk, a_ref[k:e, e:], HIGH)
            a_ref[k:e, e:] = t
            a_ref[e:, e:] -= tn(t, t, HIGH)
        if k > 0:
            x_ref[k:e, :k] = -nn(xk, tn(a_ref[:k, k:e], x_ref[:k, :k], HIGH), HIGH)


def factor(gram):
    n = gram.shape[0]
    return pl.pallas_call(
        functools.partial(factor_kernel, 64),
        out_shape=jax.ShapeDtypeStruct((n, n), jnp.float32),
        scratch_shapes=[pltpu.VMEM((n, n), jnp.float32)],
        compiler_params=params(),
        cost_estimate=cost(2e10, 8 * n * n),
        name="factor",
    )(gram)


def share_parts(x):
    groups = lax.axis_size("cols")
    if groups == 2:
        peer = lax.ppermute(x, "cols", [(0, 1), (1, 0)])
        return [x, peer]
    full = lax.all_gather(x, "cols", axis=0, tiled=False)
    return [full[i] for i in range(groups)]


def part_offset(i, feat):
    if lax.axis_size("cols") == 2:
        c = lax.axis_index("cols")
        return (c if i == 0 else 1 - c) * feat
    return i * feat


def join_copies(parts, x_ref, sems, spans):
    feat = parts[0].shape[1]
    return [
        [
            pltpu.make_async_copy(
                ref.at[pl.ds(start, size)],
                x_ref.at[pl.ds(start, size), pl.ds(pl.multiple_of(part_offset(i, feat), 128), feat)],
                sems.at[t, i],
            )
            for i, ref in enumerate(parts)
        ]
        for t, (start, size) in enumerate(spans)
    ]


def row_scale(x, weight):
    x = x.astype(jnp.float32)
    return weight / (jnp.sum(x * x, axis=1, keepdims=True) / x.shape[1] + EPSILON)


def column_scale(s):
    s = s.astype(jnp.float32)
    width = s.shape[1]
    scale = 1.0 / (width * (jnp.sum(s * s, axis=1, keepdims=True) / width + EPSILON))
    return jnp.broadcast_to(scale, (s.shape[0], 128)).T[:1, :]


def row_tiles(rows):
    blocks = rows // BLK
    per = 5 if blocks % 5 == 0 else 1
    return per, [(i * BLK, per * BLK) for i in range(0, blocks, per)]


def panel_kernel(nparts, cnt_ref, w_ref, *refs):
    parts = refs[:nparts]
    s_ref, moved_ref, gram_ref, pw_ref, sp_ref, x_ref, sems, sp_sem = refs[nparts:]
    per, tiles = row_tiles(x_ref.shape[0])
    count = cnt_ref[lax.axis_index("rows")]
    group = lax.axis_index("cols")
    own = pltpu.make_async_copy(s_ref.at[pl.ds(0, PANEL)], sp_ref, sp_sem)
    other = pltpu.make_async_copy(moved_ref, sp_ref, sp_sem)

    @pl.when(group == 0)
    def _():
        own.start()

    @pl.when(group != 0)
    def _():
        other.start()

    copies = join_copies(parts, x_ref, sems, tiles)
    for moves in copies:
        for c in moves:
            c.start()
    gram_ref[...] = jnp.zeros_like(gram_ref)
    pw_ref[...] = jnp.zeros_like(pw_ref)

    @pl.when(group == 0)
    def _():
        own.wait()

    @pl.when(group != 0)
    def _():
        other.wait()

    points = column_scale(sp_ref[...])
    for t, (start, size) in enumerate(tiles):
        for c in copies[t]:
            c.wait()

        @pl.when(t * per < count)
        def _():
            scales = []
            for b in range(per):
                j = t * per + b
                w = jnp.where(j < count, w_ref[j], 0.0)
                scales.append(row_scale(x_ref[j * BLK : (j + 1) * BLK, :], w))
            scale = jnp.concatenate(scales, axis=0)
            inner = nt(x_ref[start : start + size, :], sp_ref[...])
            panel = (inner * inner * scale * points).astype(jnp.bfloat16)
            gram_ref[...] += tn(panel, panel)
            pw_ref[start : start + size, :] = (panel.astype(jnp.float32) * scale).astype(
                jnp.bfloat16
            )


def panel_products(parts, counts, weights, s, moved):
    rows, feat = parts[0].shape
    width = s.shape[1]
    tiles = len(row_tiles(rows)[1])
    return pl.pallas_call(
        functools.partial(panel_kernel, len(parts)),
        out_shape=(
            jax.ShapeDtypeStruct((PANEL, PANEL), jnp.float32),
            jax.ShapeDtypeStruct((rows, PANEL), jnp.bfloat16),
            jax.ShapeDtypeStruct((PANEL, width), jnp.bfloat16),
        ),
        in_specs=[SMEM, SMEM] + [ANY] * (len(parts) + 2),
        out_specs=(VMEM, VMEM, VMEM),
        scratch_shapes=[
            pltpu.VMEM((rows, width), jnp.bfloat16),
            pltpu.SemaphoreType.DMA((tiles, len(parts))),
            pltpu.SemaphoreType.DMA,
        ],
        compiler_params=params(),
        cost_estimate=cost(2 * rows * PANEL * (width + PANEL), 2 * rows * width),
        name="panel_products",
    )(counts, weights, *parts, s, moved)


def column_kernel(nparts, *refs):
    parts = refs[:nparts]
    pw_ref, s_ref, g_ref, x_ref, sems = refs[nparts:]
    width = x_ref.shape[1]

    @pl.when(pl.program_id(0) == 0)
    def _():
        copies = join_copies(parts, x_ref, sems, row_tiles(x_ref.shape[0])[1])
        for group in copies:
            for c in group:
                c.start()
        for group in copies:
            for c in group:
                c.wait()

    s = s_ref[...]
    inner = nt(s, x_ref[...])
    products = nn((inner * inner).astype(jnp.bfloat16), pw_ref[...])
    wide = s.astype(jnp.float32)
    square = jnp.sum(wide * wide, axis=1, keepdims=True) / width + EPSILON
    g_ref[...] = products / (width * square)


def column_products(parts, pw, s):
    rows, feat = parts[0].shape
    size, width = s.shape
    chunk = min(512, size)
    tiles = len(row_tiles(rows)[1])
    once = pl.Buffered(1)
    return pl.pallas_call(
        functools.partial(column_kernel, len(parts)),
        grid=(size // chunk,),
        out_shape=jax.ShapeDtypeStruct((size, PANEL), jnp.float32),
        in_specs=[ANY] * len(parts)
        + [
            pl.BlockSpec((rows, PANEL), lambda i: (0, 0), pipeline_mode=once),
            pl.BlockSpec((chunk, width), lambda i: (i, 0)),
        ],
        out_specs=pl.BlockSpec((chunk, PANEL), lambda i: (i, 0)),
        scratch_shapes=[
            pltpu.VMEM((rows, width), jnp.bfloat16),
            pltpu.SemaphoreType.DMA((tiles, len(parts))),
        ],
        compiler_params=params(dimension_semantics=("arbitrary",)),
        cost_estimate=cost(2 * rows * (width + PANEL) * size, 2 * rows * width),
        name="column_products",
    )(*parts, pw, s)


def rows_kernel(nparts, w_ref, *refs):
    parts = refs[:nparts]
    sp_ref, s_ref, kern_ref, p_ref, x_ref, rs_ref, sems = refs[nparts:]
    rows_all = x_ref.shape[0]
    chunk = s_ref.shape[0]
    blocks = rows_all // BLK
    bounds = list(range(0, blocks, 7)) + [blocks]
    spans = [(a * BLK, b * BLK) for a, b in zip(bounds, bounds[1:])]

    @pl.when(pl.program_id(0) == 0)
    def _():
        copies = join_copies(parts, x_ref, sems, [(a, b - a) for a, b in spans])
        for moves in copies:
            for c in moves:
                c.start()
        points = column_scale(sp_ref[...])
        for (a, b), moves in zip(spans, copies):
            for c in moves:
                c.wait()
            for j in range(a // BLK, b // BLK):
                scale = row_scale(x_ref[j * BLK : (j + 1) * BLK, :], w_ref[j])
                rs_ref[j * BLK : (j + 1) * BLK, :] = jnp.broadcast_to(scale, (BLK, 128))
            inner = nt(x_ref[a:b, :], sp_ref[...])
            scale = jnp.concatenate([rs_ref[a:b, :]] * (PANEL // 128), axis=1)
            p_ref[a:b, :] = (inner * inner * scale * points).astype(jnp.bfloat16)

    columns = column_scale(s_ref[...])
    for a, b in spans:
        inner = nt(x_ref[a:b, :], s_ref[...])
        scale = jnp.concatenate([rs_ref[a:b, :]] * (chunk // 128), axis=1)
        kern_ref[a:b, :] = (inner * inner * scale * columns).astype(jnp.bfloat16)


def kernel_rows(parts, weights, sp, s):
    rows, feat = parts[0].shape
    cols, width = s.shape
    chunk = min(512, cols)
    once = pl.Buffered(1)
    return pl.pallas_call(
        functools.partial(rows_kernel, len(parts)),
        grid=(cols // chunk,),
        out_shape=(
            jax.ShapeDtypeStruct((rows, cols), jnp.bfloat16),
            jax.ShapeDtypeStruct((rows, PANEL), jnp.bfloat16),
        ),
        in_specs=[SMEM]
        + [ANY] * len(parts)
        + [
            pl.BlockSpec((PANEL, width), lambda i: (0, 0), pipeline_mode=once),
            pl.BlockSpec((chunk, width), lambda i: (i, 0)),
        ],
        out_specs=(
            pl.BlockSpec((rows, chunk), lambda i: (0, i)),
            pl.BlockSpec((rows, PANEL), lambda i: (0, 0)),
        ),
        scratch_shapes=[
            pltpu.VMEM((rows, width), jnp.bfloat16),
            pltpu.VMEM((rows, 128), jnp.float32),
            pltpu.SemaphoreType.DMA((2, len(parts))),
        ],
        compiler_params=params(dimension_semantics=("arbitrary",)),
        cost_estimate=cost(
            2 * rows * width * (cols + PANEL), 2 * rows * width + 2 * cols * width + 2 * rows * cols
        ),
        name="kernel_rows",
    )(weights, *parts, sp, s)


def remainder_kernel(norm, quarter_ref, kern_ref, p_ref, inv_ref, rt_ref, out_ref, proj_ref):
    chunk = kern_ref.shape[1]
    step = pl.program_id(0)
    inv_high, inv_low = split(inv_ref[...])
    rt = rt_ref[0]
    coef = (nn(rt, inv_high) + nn(rt, inv_low)).astype(jnp.bfloat16)
    proj_ref[...] = rt.astype(jnp.float32).T * (1.0 / norm)
    fit = nt(p_ref[...], coef)
    out_ref[...] = (kern_ref[...].astype(jnp.float32) - fit).astype(out_ref.dtype)

    part = min(chunk, PANEL)
    for i in range(PANEL // part):
        @pl.when((step == i) & (lax.axis_index("cols") == 0))
        def _():
            panel = p_ref[...]
            rows = slice(i * part, (i + 1) * part)
            basis = nt(panel, inv_high[rows, :]) + nt(panel, inv_low[rows, :])
            out_ref[:, :part] = (basis * norm).astype(out_ref.dtype)


def remainder_rows(kern, panel, quarter, inverse, rt, norm):
    rows, cols = kern.shape
    chunk = rt.shape[1]
    once = pl.Buffered(1)
    spec = pltpu.PrefetchScalarGridSpec(
        num_scalar_prefetch=1,
        grid=(cols // chunk,),
        in_specs=[
            pl.BlockSpec((rows, chunk), lambda i, q: (0, i)),
            pl.BlockSpec((rows, PANEL), lambda i, q: (0, 0), pipeline_mode=once),
            pl.BlockSpec((PANEL, PANEL), lambda i, q: (0, 0), pipeline_mode=once),
            pl.BlockSpec((1, chunk, PANEL), lambda i, q: (i ^ q[0], 0, 0)),
        ],
        out_specs=(
            pl.BlockSpec((rows, chunk), lambda i, q: (0, i)),
            pl.BlockSpec((PANEL, chunk), lambda i, q: (0, i)),
        ),
    )
    return pl.pallas_call(
        functools.partial(remainder_kernel, norm),
        grid_spec=spec,
        out_shape=(
            jax.ShapeDtypeStruct((rows, cols), jnp.bfloat16),
            jax.ShapeDtypeStruct((PANEL, cols), jnp.float32),
        ),
        compiler_params=params(dimension_semantics=("arbitrary",)),
        cost_estimate=cost(2 * rows * PANEL * cols, 4 * rows * cols),
        name="remainder_rows",
    )(quarter, kern, panel, inverse, rt)


def flips(bit, size):
    return [(i, i ^ bit) for i in range(size)]


def quarter_of(pair):
    me = lax.axis_index("rows").astype(jnp.int32)
    return (me // pair[0]) % 2 + 2 * ((me // pair[1]) % 2)


def trade(x, pair, k):
    bit = pair[0] * (k & 1) + pair[1] * (k >> 1)
    return lax.ppermute(x, "rows", flips(bit, lax.axis_size("rows")))


def scatter_sum(x, pair):
    n = x.shape[0] // 4
    q = quarter_of(pair)
    pieces = [lax.dynamic_slice_in_dim(x, (q ^ k) * n, n, 0) for k in range(4)]
    got = [pieces[0]] + [trade(pieces[k], pair, k) for k in range(1, 4)]
    return (got[0] + got[1]) + (got[2] + got[3])


def gather_pieces(x, pair):
    return [x] + [trade(x, pair, k) for k in range(1, 4)]


def gather_back(x, pair):
    n = x.shape[0]
    q = quarter_of(pair)
    pieces = gather_pieces(x, pair)
    return jnp.concatenate(
        [lax.select_n(q ^ i, *pieces) for i in range(4)], 0
    )


def pair_sum(x, pair):
    got = gather_pieces(x, pair)
    return (got[0] + got[1]) + (got[2] + got[3])


def on_device(descriptors, sparse_points, block_weights, block_counts, destinations):
    owners = lax.axis_size("rows")
    groups = lax.axis_size("cols")
    me = lax.axis_index("rows").astype(jnp.int32)
    group = lax.axis_index("cols").astype(jnp.int32)
    slots = block_weights.shape[0]
    per_pair = -(-slots // owners)
    feat = descriptors.shape[1]
    cols, width = sparse_points.shape
    norm = math.sqrt(owners * DST_BLK * BLK)
    pairs = [(1 << i, 2 << i) for i in range(0, owners.bit_length() - 1, 2)]

    first = sparse_points[:PANEL]
    source_parts = share_parts(descriptors)
    if groups == 2:
        moved = lax.ppermute(first, "cols", [(0, 1), (1, 0)])
    else:
        moved = lax.all_gather(first, "cols", axis=0, tiled=False)[0]
    desc_blocks = descriptors.reshape(slots, BLK, feat)
    outgoing = pack(desc_blocks, destinations, block_counts, per_pair)
    received = [lax.all_to_all(outgoing[0], "rows", split_axis=0, concat_axis=0, tiled=True)]

    weights32 = block_weights.astype(jnp.float32)
    gram_part, pw, panel_points = panel_products(
        source_parts, block_counts, weights32, sparse_points, moved
    )
    g = column_products(source_parts, pw, sparse_points)

    spare = -(-owners * slots // (PANEL * 8)) * 8
    table = lax.dynamic_update_slice(
        jnp.zeros((spare * PANEL,), jnp.float32), weights32, (me * slots,)
    ).reshape(spare, PANEL)
    if groups == 2:
        gram_part = lax.dynamic_slice_in_dim(gram_part, group * (PANEL // 2), PANEL // 2, 0)
    summed = pair_sum(jnp.concatenate([gram_part, table], 0), pairs[0])
    summed, g = lax.optimization_barrier((summed, g))
    for pair in pairs[1:]:
        summed = pair_sum(summed, pair)
    gram, table = summed[:-spare], summed[-spare:]
    if groups == 2:
        other = lax.ppermute(gram, "cols", [(0, 1), (1, 0)])
        gram = jnp.where(
            group == 0, jnp.concatenate([gram, other], 0), jnp.concatenate([other, gram], 0)
        )
    all_weights = table.reshape(-1)[: owners * slots]

    g = scatter_sum(g, pairs[0])
    if per_pair > 1:
        g, gram, last = lax.optimization_barrier((g, gram, outgoing[1]))
    for pair in pairs[1:]:
        g = scatter_sum(g, pair)
    if per_pair > 1:
        received.append(lax.all_to_all(last, "rows", split_axis=0, concat_axis=0, tiled=True))
    inverse = factor(gram)
    rt = nt(g, inverse, HIGH).astype(jnp.bfloat16)
    for pair in pairs[:0:-1]:
        rt = gather_back(rt, pair)

    slot_ids = jnp.arange(slots, dtype=jnp.int32)
    toward = ((slot_ids[None, :] < block_counts[:, None]) & (destinations == me)).astype(jnp.int32)
    rank = jnp.cumsum(toward, axis=1) - toward
    flat = toward.reshape(-1)
    place = jnp.cumsum(flat) - flat
    where_from = (jnp.arange(owners, dtype=jnp.int32)[:, None] * per_pair + rank).reshape(-1)
    hit = (flat[None, :] == 1) & (place[None, :] == jnp.arange(DST_BLK, dtype=jnp.int32)[:, None])
    positions = jnp.sum(jnp.where(hit, where_from[None, :], 0), axis=1)
    weights_here = jnp.sum(jnp.where(hit, all_weights[None, :], 0.0), axis=1)

    rt, positions = lax.optimization_barrier((rt, positions))
    arrived = select(received, positions).reshape(DST_BLK * BLK, feat)
    kern, panel = kernel_rows(share_parts(arrived), weights_here, panel_points, sparse_points)
    pieces = gather_pieces(rt, pairs[0])
    kern, *pieces = lax.optimization_barrier((kern, *pieces))
    rt = jnp.stack(pieces)
    remainder, projected = remainder_rows(
        kern, panel, quarter_of(pairs[0])[None], inverse, rt, norm
    )
    return (projected, remainder)


def solution(mesh):
    return jax.shard_map(
        on_device,
        mesh=mesh,
        in_specs=(P("rows", "cols"), P("cols", None), P("rows"), P(), P()),
        out_specs=(P(None, "cols"), P("rows", "cols")),
        check_vma=False,
    )
```

```python
import functools
import math

import jax
import jax.numpy as jnp
from jax import lax
from jax.experimental import pallas as pl
from jax.experimental.pallas import tpu as pltpu
from jax.sharding import PartitionSpec as P

PANEL = 256
BLK = 128
DST_BLK = 13
EPSILON = 1e-06
VMEM_LIMIT = 56 * 1024 * 1024
HIGH = lax.Precision.HIGHEST
ANY = pl.BlockSpec(memory_space=pl.ANY)
VMEM = pl.BlockSpec(memory_space=pltpu.VMEM)
SMEM = pl.BlockSpec(memory_space=pltpu.SMEM)


def params(**kw):
    return pltpu.CompilerParams(vmem_limit_bytes=VMEM_LIMIT, **kw)


def cost(flops, nbytes):
    return pl.CostEstimate(flops=int(flops), bytes_accessed=int(nbytes), transcendentals=0)


def dot(a, b, ca, cb, precision=None):
    return lax.dot_general(
        a, b, (((ca,), (cb,)), ((), ())), preferred_element_type=jnp.float32, precision=precision
    )


def nt(a, b, precision=None):
    return dot(a, b, 1, 1, precision)


def nn(a, b, precision=None):
    return dot(a, b, 1, 0, precision)


def tn(a, b, precision=None):
    return dot(a, b, 0, 0, precision)


def split(x):
    high = x.astype(jnp.bfloat16)
    return high, (x - high.astype(jnp.float32)).astype(jnp.bfloat16)


HEAD = 48


def block_copies(rank, whole_ref, outer, first_ref, last_ref, sems):
    if rank == 0:
        pairs = [(whole_ref, first_ref.at[outer, pl.ds(0, BLK)])]
    else:
        pairs = [
            (whole_ref.at[pl.ds(0, HEAD)], first_ref.at[outer, pl.ds(BLK, HEAD)]),
            (whole_ref.at[pl.ds(HEAD, BLK - HEAD)], last_ref.at[outer]),
        ]
    return [(a, b, sems.at[i]) for i, (a, b) in enumerate(pairs)]


def pack_kernel(per_pair, dest_ref, cnt_ref, desc_ref, *refs):
    out_refs, (ctr_ref, rank_ref, sems) = refs[:per_pair], refs[per_pair:]
    slots = desc_ref.shape[0]
    owners = ctr_ref.shape[0]
    me = lax.axis_index("rows")
    count = cnt_ref[me]

    def copies(j, d, rank):
        moves = block_copies(rank, desc_ref.at[j], d, out_refs[0], out_refs[-1], sems.at[j])
        return [pltpu.make_async_copy(a, b, sem) for a, b, sem in moves]

    @pl.loop(0, owners)
    def _(i):
        ctr_ref[i] = 0

    @pl.loop(0, slots)
    def _(j):
        @pl.when(j < count)
        def _():
            d = dest_ref[me, j]
            rank = ctr_ref[d]
            ctr_ref[d] = rank + 1
            rank_ref[j] = rank
            for r in range(per_pair):
                @pl.when(rank == r)
                def _():
                    for c in copies(j, d, r):
                        c.start()

    @pl.loop(0, slots)
    def _(j):
        @pl.when(j < count)
        def _():
            for r in range(per_pair):
                @pl.when(rank_ref[j] == r)
                def _():
                    for c in copies(j, 0, r):
                        c.wait()


def pack(desc_blocks, destinations, counts, per_pair):
    slots, blk, feat = desc_blocks.shape
    owners = destinations.shape[0]
    heights = [blk] if per_pair == 1 else [blk + HEAD, blk - HEAD]
    return pl.pallas_call(
        functools.partial(pack_kernel, per_pair),
        out_shape=[
            jax.ShapeDtypeStruct((owners, h, feat), desc_blocks.dtype) for h in heights
        ],
        in_specs=[SMEM, SMEM, VMEM],
        out_specs=[ANY] * per_pair,
        scratch_shapes=[
            pltpu.SMEM((owners,), jnp.int32),
            pltpu.SMEM((slots,), jnp.int32),
            pltpu.SemaphoreType.DMA((slots, 2)),
        ],
        compiler_params=params(),
        cost_estimate=cost(0, 4 * slots * blk * feat),
        name="pack",
    )(destinations, counts, desc_blocks)


def select_kernel(rows, owner_ref, *refs):
    recv_refs, (out_ref, sems) = refs[: len(rows)], refs[len(rows) :]
    copies = []
    for p in range(out_ref.shape[0]):
        at = 0
        for i, (start, size) in enumerate(rows):
            src = recv_refs[i].at[owner_ref[p], pl.ds(start, size)]
            copies.append(pltpu.make_async_copy(src, out_ref.at[p, pl.ds(at, size)], sems.at[p, i]))
            at += size
    for c in copies:
        c.start()
    for c in copies:
        c.wait()


def select(received, rows, from_owner):
    feat = received[0].shape[-1]
    count = from_owner.shape[0]
    return pl.pallas_call(
        functools.partial(select_kernel, rows),
        out_shape=jax.ShapeDtypeStruct((count, BLK, feat), received[0].dtype),
        in_specs=[SMEM] + [ANY] * len(rows),
        out_specs=VMEM,
        scratch_shapes=[pltpu.SemaphoreType.DMA((count, len(rows)))],
        compiler_params=params(),
        cost_estimate=cost(0, 4 * count * BLK * feat),
        name="select",
    )(from_owner, *received)


def small_factor(a):
    n = a.shape[0]
    row = lax.broadcasted_iota(jnp.int32, (n, 1), 0)
    eye = lax.broadcasted_iota(jnp.int32, (n, n), 0) == lax.broadcasted_iota(jnp.int32, (n, n), 1)
    m = jnp.concatenate([a, eye.astype(jnp.float32)], axis=1)
    out = []
    for j in range(0, n, 2):
        r0 = m[j : j + 1, :]
        r1 = m[j + 1 : j + 2, :]
        p = r0[:, j : j + 1]
        q = r0[:, j + 1 : j + 2]
        s = r1[:, j + 1 : j + 2]
        det = p * s - q * q
        out.append(r0[:, n:] * lax.rsqrt(p))
        out.append((r1[:, n:] - (q / p) * r0[:, n:]) * lax.rsqrt(det / p))
        if j + 2 < n:
            inv = 1.0 / det
            g0 = (s * r0 - q * r1) * inv
            g1 = (p * r1 - q * r0) * inv
            c0 = jnp.where(row > j + 1, m[:, j : j + 1], 0.0)
            c1 = jnp.where(row > j + 1, m[:, j + 1 : j + 2], 0.0)
            m = m - c0 * g0 - c1 * g1
    return out


def factor_kernel(leaf, gram_ref, x_ref, a_ref):
    n = gram_ref.shape[0]
    a_ref[...] = gram_ref[...]
    x_ref[...] = jnp.zeros_like(x_ref)
    for k in range(0, n, leaf):
        e = k + leaf
        for i, r in enumerate(small_factor(a_ref[k:e, k:e])):
            x_ref[k + i : k + i + 1, k:e] = r
        xk = x_ref[k:e, k:e]
        if e < n:
            t = nn(xk, a_ref[k:e, e:], HIGH)
            a_ref[k:e, e:] = t
            a_ref[e:, e:] -= tn(t, t, HIGH)
        if k > 0:
            x_ref[k:e, :k] = -nn(xk, tn(a_ref[:k, k:e], x_ref[:k, :k], HIGH), HIGH)


def factor(gram):
    n = gram.shape[0]
    return pl.pallas_call(
        functools.partial(factor_kernel, 64),
        out_shape=jax.ShapeDtypeStruct((n, n), jnp.float32),
        scratch_shapes=[pltpu.VMEM((n, n), jnp.float32)],
        compiler_params=params(),
        cost_estimate=cost(4 * n * n * n, 8 * n * n),
        name="factor",
    )(gram)


def share_parts(x):
    groups = lax.axis_size("cols")
    if groups == 2:
        peer = lax.ppermute(x, "cols", [(0, 1), (1, 0)])
        return [x, peer]
    full = lax.all_gather(x, "cols", axis=0, tiled=False)
    return [full[i] for i in range(groups)]


def part_offset(i, feat):
    if lax.axis_size("cols") == 2:
        c = lax.axis_index("cols")
        return (c if i == 0 else 1 - c) * feat
    return i * feat


def join_copies(parts, x_ref, sems, spans):
    feat = parts[0].shape[1]
    return [
        [
            pltpu.make_async_copy(
                ref.at[pl.ds(start, size)],
                x_ref.at[pl.ds(start, size), pl.ds(pl.multiple_of(part_offset(i, feat), 128), feat)],
                sems.at[t, i],
            )
            for i, ref in enumerate(parts)
        ]
        for t, (start, size) in enumerate(spans)
    ]


def row_scale(x, weight):
    x = x.astype(jnp.float32)
    return weight / (jnp.sum(x * x, axis=1, keepdims=True) / x.shape[1] + EPSILON)


def column_scale(s):
    s = s.astype(jnp.float32)
    width = s.shape[1]
    scale = 1.0 / (width * (jnp.sum(s * s, axis=1, keepdims=True) / width + EPSILON))
    return jnp.broadcast_to(scale, (s.shape[0], 128)).T[:1, :]


def row_tiles(rows):
    blocks = rows // BLK
    per = 5 if blocks % 5 == 0 else 1
    return per, [(i * BLK, per * BLK) for i in range(0, blocks, per)]


def panel_kernel(nparts, cnt_ref, w_ref, *refs):
    parts = refs[:nparts]
    s_ref, moved_ref, gram_ref, pw_ref, sp_ref, x_ref, sems, sp_sem = refs[nparts:]
    per, tiles = row_tiles(x_ref.shape[0])
    count = cnt_ref[lax.axis_index("rows")]
    group = lax.axis_index("cols")
    own = pltpu.make_async_copy(s_ref.at[pl.ds(0, PANEL)], sp_ref, sp_sem)
    other = pltpu.make_async_copy(moved_ref, sp_ref, sp_sem)

    @pl.when(group == 0)
    def _():
        own.start()

    @pl.when(group != 0)
    def _():
        other.start()

    copies = join_copies(parts, x_ref, sems, tiles)
    for moves in copies:
        for c in moves:
            c.start()
    gram_ref[...] = jnp.zeros_like(gram_ref)
    pw_ref[...] = jnp.zeros_like(pw_ref)

    @pl.when(group == 0)
    def _():
        own.wait()

    @pl.when(group != 0)
    def _():
        other.wait()

    points = column_scale(sp_ref[...])
    for t, (start, size) in enumerate(tiles):
        for c in copies[t]:
            c.wait()

        @pl.when(t * per < count)
        def _():
            scales = []
            for b in range(per):
                j = t * per + b
                w = jnp.where(j < count, w_ref[j], 0.0)
                scales.append(row_scale(x_ref[j * BLK : (j + 1) * BLK, :], w))
            scale = jnp.concatenate(scales, axis=0)
            inner = nt(x_ref[start : start + size, :], sp_ref[...])
            panel = (inner * inner * scale * points).astype(jnp.bfloat16)
            gram_ref[...] += tn(panel, panel)
            pw_ref[start : start + size, :] = (panel.astype(jnp.float32) * scale).astype(
                jnp.bfloat16
            )


def panel_products(parts, counts, weights, s, moved):
    rows, feat = parts[0].shape
    width = s.shape[1]
    tiles = len(row_tiles(rows)[1])
    return pl.pallas_call(
        functools.partial(panel_kernel, len(parts)),
        out_shape=(
            jax.ShapeDtypeStruct((PANEL, PANEL), jnp.float32),
            jax.ShapeDtypeStruct((rows, PANEL), jnp.bfloat16),
            jax.ShapeDtypeStruct((PANEL, width), jnp.bfloat16),
        ),
        in_specs=[SMEM, SMEM] + [ANY] * (len(parts) + 2),
        out_specs=(VMEM, VMEM, VMEM),
        scratch_shapes=[
            pltpu.VMEM((rows, width), jnp.bfloat16),
            pltpu.SemaphoreType.DMA((tiles, len(parts))),
            pltpu.SemaphoreType.DMA,
        ],
        compiler_params=params(),
        cost_estimate=cost(2 * rows * PANEL * (width + PANEL), 2 * rows * width),
        name="panel_products",
    )(counts, weights, *parts, s, moved)


def column_kernel(nparts, *refs):
    parts = refs[:nparts]
    pw_ref, s_ref, g_ref, x_ref, sems = refs[nparts:]
    width = x_ref.shape[1]

    @pl.when(pl.program_id(0) == 0)
    def _():
        copies = join_copies(parts, x_ref, sems, row_tiles(x_ref.shape[0])[1])
        for group in copies:
            for c in group:
                c.start()
        for group in copies:
            for c in group:
                c.wait()

    s = s_ref[...]
    inner = nt(s, x_ref[...])
    products = nn((inner * inner).astype(jnp.bfloat16), pw_ref[...])
    wide = s.astype(jnp.float32)
    square = jnp.sum(wide * wide, axis=1, keepdims=True) / width + EPSILON
    g_ref[...] = products / (width * square)


def column_products(parts, pw, s):
    rows, feat = parts[0].shape
    size, width = s.shape
    chunk = min(512, size)
    tiles = len(row_tiles(rows)[1])
    once = pl.Buffered(1)
    return pl.pallas_call(
        functools.partial(column_kernel, len(parts)),
        grid=(size // chunk,),
        out_shape=jax.ShapeDtypeStruct((size, PANEL), jnp.float32),
        in_specs=[ANY] * len(parts)
        + [
            pl.BlockSpec((rows, PANEL), lambda i: (0, 0), pipeline_mode=once),
            pl.BlockSpec((chunk, width), lambda i: (i, 0)),
        ],
        out_specs=pl.BlockSpec((chunk, PANEL), lambda i: (i, 0)),
        scratch_shapes=[
            pltpu.VMEM((rows, width), jnp.bfloat16),
            pltpu.SemaphoreType.DMA((tiles, len(parts))),
        ],
        compiler_params=params(dimension_semantics=("arbitrary",)),
        cost_estimate=cost(2 * rows * (width + PANEL) * size, 2 * rows * width),
        name="column_products",
    )(*parts, pw, s)


def rows_kernel(nparts, w_ref, *refs):
    parts = refs[:nparts]
    sp_ref, s_ref, kern_ref, p_ref, cs_ref, csp_ref, x_ref, rs_ref, sems = refs[nparts:]
    rows_all = x_ref.shape[0]
    chunk = s_ref.shape[0]
    blocks = rows_all // BLK
    bounds = list(range(0, blocks, 7)) + [blocks]
    spans = [(a * BLK, b * BLK) for a, b in zip(bounds, bounds[1:])]

    @pl.when(pl.program_id(0) == 0)
    def _():
        copies = join_copies(parts, x_ref, sems, [(a, b - a) for a, b in spans])
        for moves in copies:
            for c in moves:
                c.start()
        points = column_scale(sp_ref[...])
        csp_ref[...] = points
        for (a, b), moves in zip(spans, copies):
            for c in moves:
                c.wait()
            for j in range(a // BLK, b // BLK):
                scale = row_scale(x_ref[j * BLK : (j + 1) * BLK, :], w_ref[j])
                rs_ref[j * BLK : (j + 1) * BLK, :] = jnp.broadcast_to(scale, (BLK, 128))
            inner = nt(x_ref[a:b, :], sp_ref[...])
            scale = jnp.concatenate([rs_ref[a:b, :]] * (PANEL // 128), axis=1)
            p_ref[a:b, :] = (inner * inner * scale * points).astype(jnp.bfloat16)

    columns = column_scale(s_ref[...])
    cs_ref[...] = columns
    for a, b in spans:
        inner = nt(x_ref[a:b, :], s_ref[...])
        scale = jnp.concatenate([rs_ref[a:b, :]] * (chunk // 128), axis=1)
        kern_ref[a:b, :] = (inner * inner * scale * columns).astype(jnp.bfloat16)


def kernel_rows(parts, weights, sp, s):
    rows, feat = parts[0].shape
    cols, width = s.shape
    chunk = min(512, cols)
    once = pl.Buffered(1)
    return pl.pallas_call(
        functools.partial(rows_kernel, len(parts)),
        grid=(cols // chunk,),
        out_shape=(
            jax.ShapeDtypeStruct((rows, cols), jnp.bfloat16),
            jax.ShapeDtypeStruct((rows, PANEL), jnp.bfloat16),
            jax.ShapeDtypeStruct((1, cols), jnp.float32),
            jax.ShapeDtypeStruct((1, PANEL), jnp.float32),
        ),
        in_specs=[SMEM]
        + [ANY] * len(parts)
        + [
            pl.BlockSpec((PANEL, width), lambda i: (0, 0), pipeline_mode=once),
            pl.BlockSpec((chunk, width), lambda i: (i, 0)),
        ],
        out_specs=(
            pl.BlockSpec((rows, chunk), lambda i: (0, i)),
            pl.BlockSpec((rows, PANEL), lambda i: (0, 0)),
            pl.BlockSpec((1, chunk), lambda i: (0, i)),
            pl.BlockSpec((1, PANEL), lambda i: (0, 0)),
        ),
        scratch_shapes=[
            pltpu.VMEM((rows, width), jnp.bfloat16),
            pltpu.VMEM((rows, 128), jnp.float32),
            pltpu.SemaphoreType.DMA((2, len(parts))),
        ],
        compiler_params=params(dimension_semantics=("arbitrary",)),
        cost_estimate=cost(
            2 * rows * width * (cols + PANEL), 2 * rows * width + 2 * cols * width + 2 * rows * cols
        ),
        name="kernel_rows",
    )(weights, *parts, sp, s)


def seconds_kernel(nparts, place_ref, num_ref, w_ref, *refs):
    parts = refs[:nparts]
    sp_ref, csp_ref, s_ref, cs_ref = refs[nparts : nparts + 4]
    kern_ref, p_ref, x_ref, kbuf_ref, pbuf_ref, sems, out_sems = refs[nparts + 6 :]
    rows_all = x_ref.shape[0]
    blocks = rows_all // BLK
    num = num_ref[0]
    spans = [(a, min(2, blocks - a)) for a in range(0, blocks, 2)]
    copies = join_copies(parts, x_ref, sems, [(a * BLK, n * BLK) for a, n in spans])
    for moves in copies:
        for c in moves:
            c.start()

    def puts(j):
        rows = pl.ds(j * BLK, BLK)
        dst = pl.ds(pl.multiple_of(place_ref[j] * BLK, BLK), BLK)
        return [
            pltpu.make_async_copy(kbuf_ref.at[rows], kern_ref.at[dst], out_sems.at[j, 0]),
            pltpu.make_async_copy(pbuf_ref.at[rows], p_ref.at[dst], out_sems.at[j, 1]),
        ]

    for t, (first, n) in enumerate(spans):
        for c in copies[t]:
            c.wait()

        @pl.when(first < num)
        def _():
            a, b = first * BLK, (first + n) * BLK
            scale = jnp.concatenate(
                [row_scale(x_ref[j * BLK : (j + 1) * BLK, :], w_ref[j]) for j in range(first, first + n)],
                axis=0,
            )
            inner = nt(x_ref[a:b, :], sp_ref[...])
            pbuf_ref[a:b, :] = (inner * inner * scale * csp_ref[...]).astype(jnp.bfloat16)
            inner = nt(x_ref[a:b, :], s_ref[...])
            kbuf_ref[a:b, :] = (inner * inner * scale * cs_ref[...]).astype(jnp.bfloat16)

        for j in range(first, first + n):
            @pl.when(j < num)
            def _():
                for c in puts(j):
                    c.start()

    for j in range(blocks):
        @pl.when(j < num)
        def _():
            for c in puts(j):
                c.wait()


def second_rows(parts, places, num, weights, sp, csp, s, cs, kern, panel):
    rows, feat = parts[0].shape
    cols, width = s.shape
    n = len(parts)
    return pl.pallas_call(
        functools.partial(seconds_kernel, n),
        out_shape=(
            jax.ShapeDtypeStruct(kern.shape, kern.dtype),
            jax.ShapeDtypeStruct(panel.shape, panel.dtype),
        ),
        in_specs=[SMEM] * 3 + [ANY] * n + [VMEM] * 4 + [ANY, ANY],
        out_specs=(ANY, ANY),
        input_output_aliases={n + 7: 0, n + 8: 1},
        scratch_shapes=[
            pltpu.VMEM((rows, width), jnp.bfloat16),
            pltpu.VMEM((rows, cols), jnp.bfloat16),
            pltpu.VMEM((rows, PANEL), jnp.bfloat16),
            pltpu.SemaphoreType.DMA((-(-rows // (2 * BLK)), n)),
            pltpu.SemaphoreType.DMA((rows // BLK, 2)),
        ],
        compiler_params=params(),
        cost_estimate=cost(2 * rows * width * (cols + PANEL), 2 * cols * width),
        name="second_rows",
    )(places, num, weights, *parts, sp, csp, s, cs, kern, panel)


def remainder_kernel(norm, quarter_ref, kern_ref, p_ref, inv_ref, rt_ref, out_ref, proj_ref):
    chunk = kern_ref.shape[1]
    step = pl.program_id(0)
    inv_high, inv_low = split(inv_ref[...])
    rt = rt_ref[0]
    coef = (nn(rt, inv_high) + nn(rt, inv_low)).astype(jnp.bfloat16)
    proj_ref[...] = rt.astype(jnp.float32).T * (1.0 / norm)
    fit = nt(p_ref[...], coef)
    out_ref[...] = (kern_ref[...].astype(jnp.float32) - fit).astype(out_ref.dtype)

    part = min(chunk, PANEL)
    for i in range(PANEL // part):
        @pl.when((step == i) & (lax.axis_index("cols") == 0))
        def _():
            panel = p_ref[...]
            rows = slice(i * part, (i + 1) * part)
            basis = nt(panel, inv_high[rows, :]) + nt(panel, inv_low[rows, :])
            out_ref[:, :part] = (basis * norm).astype(out_ref.dtype)


def remainder_rows(kern, panel, quarter, inverse, rt, norm):
    rows, cols = kern.shape
    chunk = rt.shape[1]
    once = pl.Buffered(1)
    spec = pltpu.PrefetchScalarGridSpec(
        num_scalar_prefetch=1,
        grid=(cols // chunk,),
        in_specs=[
            pl.BlockSpec((rows, chunk), lambda i, q: (0, i)),
            pl.BlockSpec((rows, PANEL), lambda i, q: (0, 0), pipeline_mode=once),
            pl.BlockSpec((PANEL, PANEL), lambda i, q: (0, 0), pipeline_mode=once),
            pl.BlockSpec((1, chunk, PANEL), lambda i, q: (i ^ q[0], 0, 0)),
        ],
        out_specs=(
            pl.BlockSpec((rows, chunk), lambda i, q: (0, i)),
            pl.BlockSpec((PANEL, chunk), lambda i, q: (0, i)),
        ),
    )
    return pl.pallas_call(
        functools.partial(remainder_kernel, norm),
        grid_spec=spec,
        out_shape=(
            jax.ShapeDtypeStruct((rows, cols), jnp.bfloat16),
            jax.ShapeDtypeStruct((PANEL, cols), jnp.float32),
        ),
        compiler_params=params(dimension_semantics=("arbitrary",)),
        cost_estimate=cost(2 * rows * PANEL * cols, 4 * rows * cols),
        name="remainder_rows",
    )(quarter, kern, panel, inverse, rt)


def flips(bit, size):
    return [(i, i ^ bit) for i in range(size)]


def quarter_of(pair):
    me = lax.axis_index("rows").astype(jnp.int32)
    return (me // pair[0]) % 2 + 2 * ((me // pair[1]) % 2)


def trade(x, pair, k):
    bit = pair[0] * (k & 1) + pair[1] * (k >> 1)
    return lax.ppermute(x, "rows", flips(bit, lax.axis_size("rows")))


def quarters(x, pair):
    n = x.shape[0] // 4
    q = quarter_of(pair)
    return [lax.dynamic_slice_in_dim(x, (q ^ k) * n, n, 0) for k in range(4)]


def quarter_sum(pieces, pair):
    got = [pieces[0]] + [trade(pieces[k], pair, k) for k in range(1, 4)]
    return (got[0] + got[1]) + (got[2] + got[3])


def gather_pieces(x, pair):
    return [x] + [trade(x, pair, k) for k in range(1, 4)]


def gather_back(x, pair):
    q = quarter_of(pair)
    pieces = gather_pieces(x, pair)
    return jnp.concatenate([lax.select_n(q ^ i, *pieces) for i in range(4)], 0)


def pair_sum(x, pair):
    got = gather_pieces(x, pair)
    return (got[0] + got[1]) + (got[2] + got[3])


def on_device(descriptors, sparse_points, block_weights, block_counts, destinations):
    owners = lax.axis_size("rows")
    groups = lax.axis_size("cols")
    me = lax.axis_index("rows").astype(jnp.int32)
    group = lax.axis_index("cols").astype(jnp.int32)
    slots = block_weights.shape[0]
    per_pair = -(-slots // owners)
    feat = descriptors.shape[1]
    cols, width = sparse_points.shape
    norm = math.sqrt(owners * DST_BLK * BLK)
    pairs = [(1 << i, 2 << i) for i in range(0, owners.bit_length() - 1, 2)]

    first = sparse_points[:PANEL]
    source_parts = share_parts(descriptors)
    if groups == 2:
        moved = lax.ppermute(first, "cols", [(0, 1), (1, 0)])
    else:
        moved = lax.all_gather(first, "cols", axis=0, tiled=False)[0]
    desc_blocks = descriptors.reshape(slots, BLK, feat)
    outgoing = pack(desc_blocks, destinations, block_counts, per_pair)
    received = [lax.all_to_all(outgoing[0], "rows", split_axis=0, concat_axis=0, tiled=True)]

    weights32 = block_weights.astype(jnp.float32)
    gram_part, pw, panel_points = panel_products(
        source_parts, block_counts, weights32, sparse_points, moved
    )
    sent = quarters(column_products(source_parts, pw, sparse_points), pairs[0])

    spare = -(-owners * slots // (PANEL * 8)) * 8
    table = lax.dynamic_update_slice(
        jnp.zeros((spare * PANEL,), jnp.float32), weights32, (me * slots,)
    ).reshape(spare, PANEL)
    if groups == 2:
        gram_part = lax.dynamic_slice_in_dim(gram_part, group * (PANEL // 2), PANEL // 2, 0)
    summed = pair_sum(jnp.concatenate([gram_part, table], 0), pairs[0])
    summed, *sent = lax.optimization_barrier((summed, *sent))
    g = quarter_sum(sent, pairs[0])
    for pair in pairs[1:]:
        summed = pair_sum(summed, pair)
    gram, table = summed[:-spare], summed[-spare:]
    if groups == 2:
        other = lax.ppermute(gram, "cols", [(0, 1), (1, 0)])
        gram = jnp.where(
            group == 0, jnp.concatenate([gram, other], 0), jnp.concatenate([other, gram], 0)
        )
    all_weights = table.reshape(-1)[: owners * slots]

    for pair in pairs[1:]:
        sent = quarters(g, pair)
        if per_pair > 1 and pair == pairs[-1]:
            gram, last, received[0], *sent = lax.optimization_barrier(
                (gram, outgoing[1], received[0], *sent)
            )
        g = quarter_sum(sent, pair)
    if per_pair > 1:
        received.append(lax.all_to_all(last, "rows", split_axis=0, concat_axis=0, tiled=True))
    inverse = factor(gram)
    rt = nt(g, inverse, HIGH).astype(jnp.bfloat16)

    slot_ids = jnp.arange(slots, dtype=jnp.int32)
    toward = ((slot_ids[None, :] < block_counts[:, None]) & (destinations == me)).astype(jnp.int32)
    rank = jnp.cumsum(toward, axis=1) - toward
    flat = toward.reshape(-1)
    place = jnp.cumsum(flat) - flat
    where_from = (jnp.arange(owners, dtype=jnp.int32)[:, None] * per_pair + rank).reshape(-1)
    hit = (flat[None, :] == 1) & (place[None, :] == jnp.arange(DST_BLK, dtype=jnp.int32)[:, None])
    positions = jnp.sum(jnp.where(hit, where_from[None, :], 0), axis=1)
    weights_here = jnp.sum(jnp.where(hit, all_weights[None, :], 0.0), axis=1)
    from_owner = positions // per_pair
    is_second = positions % per_pair == 1
    order = jnp.cumsum(is_second.astype(jnp.int32))
    most = DST_BLK // 2
    pick = is_second[None, :] & (order[None, :] == 1 + jnp.arange(most, dtype=jnp.int32)[:, None])
    places = jnp.sum(jnp.where(pick, jnp.arange(DST_BLK, dtype=jnp.int32)[None, :], 0), axis=1)
    second_owner = jnp.sum(jnp.where(pick, from_owner[None, :], 0), axis=1)
    second_weights = jnp.sum(jnp.where(pick, weights_here[None, :], 0.0), axis=1)

    rt, from_owner = lax.optimization_barrier((rt, from_owner))
    arrived = select(received[:1], [(0, BLK)], from_owner).reshape(DST_BLK * BLK, feat)
    kern, panel, cs, csp = kernel_rows(
        share_parts(arrived), weights_here, panel_points, sparse_points
    )
    for pair in pairs[:0:-1]:
        rt = gather_back(rt, pair)
    pieces = gather_pieces(rt, pairs[0])
    if per_pair > 1:
        rt, kern, second_owner = lax.optimization_barrier((rt, kern, second_owner))
        late = select(received, [(BLK, HEAD), (0, BLK - HEAD)], second_owner)
        late = late.reshape(most * BLK, feat)
        kern, panel = second_rows(
            share_parts(late),
            places,
            order[-1:],
            second_weights,
            panel_points,
            csp,
            sparse_points,
            cs,
            kern,
            panel,
        )
    kern, *pieces = lax.optimization_barrier((kern, *pieces))
    remainder, projected = remainder_rows(
        kern, panel, quarter_of(pairs[0])[None], inverse, jnp.stack(pieces), norm
    )
    return (projected, remainder)


def solution(mesh):
    return jax.shard_map(
        on_device,
        mesh=mesh,
        in_specs=(P("rows", "cols"), P("cols", None), P("rows"), P(), P()),
        out_specs=(P(None, "cols"), P("rows", "cols")),
        check_vma=False,
    )
```

```python
import functools
import math

import jax
import jax.numpy as jnp
from jax import lax
from jax.experimental import pallas as pl
from jax.experimental.pallas import tpu as pltpu
from jax.sharding import PartitionSpec as P

PANEL = 256
BLK = 128
DST_BLK = 13
EPSILON = 1e-06
VMEM_LIMIT = 56 * 1024 * 1024
HIGH = lax.Precision.HIGHEST
ANY = pl.BlockSpec(memory_space=pl.ANY)
VMEM = pl.BlockSpec(memory_space=pltpu.VMEM)
SMEM = pl.BlockSpec(memory_space=pltpu.SMEM)


def params(**kw):
    return pltpu.CompilerParams(vmem_limit_bytes=VMEM_LIMIT, **kw)


def cost(flops, nbytes):
    return pl.CostEstimate(flops=int(flops), bytes_accessed=int(nbytes), transcendentals=0)


def dot(a, b, ca, cb, precision=None):
    return lax.dot_general(
        a, b, (((ca,), (cb,)), ((), ())), preferred_element_type=jnp.float32, precision=precision
    )


def nt(a, b, precision=None):
    return dot(a, b, 1, 1, precision)


def nn(a, b, precision=None):
    return dot(a, b, 1, 0, precision)


def tn(a, b, precision=None):
    return dot(a, b, 0, 0, precision)


def split(x):
    high = x.astype(jnp.bfloat16)
    return high, (x - high.astype(jnp.float32)).astype(jnp.bfloat16)


def pack_kernel(per_pair, dest_ref, cnt_ref, desc_ref, *refs):
    out_refs, (ctr_ref, sems) = refs[:per_pair], refs[per_pair:]
    slots = desc_ref.shape[0]
    owners = ctr_ref.shape[0]
    me = lax.axis_index("rows")
    count = cnt_ref[me]

    def copy(j, d, rank):
        return pltpu.make_async_copy(desc_ref.at[j], out_refs[rank].at[d], sems.at[j])

    @pl.loop(0, owners)
    def _(i):
        ctr_ref[i] = 0

    @pl.loop(0, slots)
    def _(j):
        @pl.when(j < count)
        def _():
            d = dest_ref[me, j]
            rank = ctr_ref[d]
            ctr_ref[d] = rank + 1
            for r in range(per_pair):
                @pl.when(rank == r)
                def _():
                    copy(j, d, r).start()

    @pl.loop(0, slots)
    def _(j):
        @pl.when(j < count)
        def _():
            pltpu.make_async_copy(desc_ref.at[0], out_refs[0].at[0], sems.at[j]).wait()


def pack(desc_blocks, destinations, counts, per_pair):
    slots, blk, feat = desc_blocks.shape
    owners = destinations.shape[0]
    return pl.pallas_call(
        functools.partial(pack_kernel, per_pair),
        out_shape=[jax.ShapeDtypeStruct((owners, blk, feat), desc_blocks.dtype)] * per_pair,
        in_specs=[SMEM, SMEM, VMEM],
        out_specs=[ANY] * per_pair,
        scratch_shapes=[
            pltpu.SMEM((owners,), jnp.int32),
            pltpu.SemaphoreType.DMA((slots,)),
        ],
        compiler_params=params(),
        cost_estimate=cost(0, 4 * slots * blk * feat),
        name="pack",
    )(destinations, counts, desc_blocks)


def select_kernel(owner_ref, recv_ref, out_ref, sems):
    copies = [
        pltpu.make_async_copy(recv_ref.at[owner_ref[p]], out_ref.at[p], sems.at[p])
        for p in range(out_ref.shape[0])
    ]
    for c in copies:
        c.start()
    for c in copies:
        c.wait()


def select(received, from_owner):
    feat = received.shape[-1]
    count = from_owner.shape[0]
    return pl.pallas_call(
        select_kernel,
        out_shape=jax.ShapeDtypeStruct((count, BLK, feat), received.dtype),
        in_specs=[SMEM, ANY],
        out_specs=VMEM,
        scratch_shapes=[pltpu.SemaphoreType.DMA((count,))],
        compiler_params=params(),
        cost_estimate=cost(0, 4 * count * BLK * feat),
        name="select",
    )(from_owner, received)


def small_factor(a):
    n = a.shape[0]
    row = lax.broadcasted_iota(jnp.int32, (n, 1), 0)
    eye = lax.broadcasted_iota(jnp.int32, (n, n), 0) == lax.broadcasted_iota(jnp.int32, (n, n), 1)
    m = jnp.concatenate([a, eye.astype(jnp.float32)], axis=1)
    out = []
    for j in range(0, n, 2):
        r0 = m[j : j + 1, :]
        r1 = m[j + 1 : j + 2, :]
        p = r0[:, j : j + 1]
        q = r0[:, j + 1 : j + 2]
        s = r1[:, j + 1 : j + 2]
        det = p * s - q * q
        out.append(r0[:, n:] * lax.rsqrt(p))
        out.append((r1[:, n:] - (q / p) * r0[:, n:]) * lax.rsqrt(det / p))
        if j + 2 < n:
            inv = 1.0 / det
            g0 = (s * r0 - q * r1) * inv
            g1 = (p * r1 - q * r0) * inv
            c0 = jnp.where(row > j + 1, m[:, j : j + 1], 0.0)
            c1 = jnp.where(row > j + 1, m[:, j + 1 : j + 2], 0.0)
            m = m - c0 * g0 - c1 * g1
    return out


def factor_kernel(leaf, gram_ref, x_ref, a_ref):
    n = gram_ref.shape[0]
    a_ref[...] = gram_ref[...]
    x_ref[...] = jnp.zeros_like(x_ref)
    for k in range(0, n, leaf):
        e = k + leaf
        for i, r in enumerate(small_factor(a_ref[k:e, k:e])):
            x_ref[k + i : k + i + 1, k:e] = r
        xk = x_ref[k:e, k:e]
        if e < n:
            t = nn(xk, a_ref[k:e, e:], HIGH)
            a_ref[k:e, e:] = t
            a_ref[e:, e:] -= tn(t, t, HIGH)
        if k > 0:
            x_ref[k:e, :k] = -nn(xk, tn(a_ref[:k, k:e], x_ref[:k, :k], HIGH), HIGH)


def factor(gram):
    n = gram.shape[0]
    return pl.pallas_call(
        functools.partial(factor_kernel, 64),
        out_shape=jax.ShapeDtypeStruct((n, n), jnp.float32),
        scratch_shapes=[pltpu.VMEM((n, n), jnp.float32)],
        compiler_params=params(),
        cost_estimate=cost(4 * n * n * n, 8 * n * n),
        name="factor",
    )(gram)


def share_parts(x):
    groups = lax.axis_size("cols")
    if groups == 2:
        peer = lax.ppermute(x, "cols", [(0, 1), (1, 0)])
        return [x, peer]
    full = lax.all_gather(x, "cols", axis=0, tiled=False)
    return [full[i] for i in range(groups)]


def part_offset(i, feat):
    if lax.axis_size("cols") == 2:
        c = lax.axis_index("cols")
        return (c if i == 0 else 1 - c) * feat
    return i * feat


def join_copies(parts, x_ref, sems, spans):
    feat = parts[0].shape[1]
    return [
        [
            pltpu.make_async_copy(
                ref.at[pl.ds(start, size)],
                x_ref.at[pl.ds(start, size), pl.ds(pl.multiple_of(part_offset(i, feat), 128), feat)],
                sems.at[t, i],
            )
            for i, ref in enumerate(parts)
        ]
        for t, (start, size) in enumerate(spans)
    ]


def row_scale(x, weight):
    x = x.astype(jnp.float32)
    return weight / (jnp.sum(x * x, axis=1, keepdims=True) / x.shape[1] + EPSILON)


def column_scale(s):
    s = s.astype(jnp.float32)
    width = s.shape[1]
    scale = 1.0 / (width * (jnp.sum(s * s, axis=1, keepdims=True) / width + EPSILON))
    return jnp.broadcast_to(scale, (s.shape[0], 128)).T[:1, :]


def row_tiles(rows):
    blocks = rows // BLK
    per = 5 if blocks % 5 == 0 else 1
    return per, [(i * BLK, per * BLK) for i in range(0, blocks, per)]


def panel_kernel(nparts, cnt_ref, w_ref, *refs):
    parts = refs[:nparts]
    s_ref, moved_ref, gram_ref, pw_ref, sp_ref, x_ref, sems, sp_sem = refs[nparts:]
    per, tiles = row_tiles(x_ref.shape[0])
    count = cnt_ref[lax.axis_index("rows")]
    group = lax.axis_index("cols")
    own = pltpu.make_async_copy(s_ref.at[pl.ds(0, PANEL)], sp_ref, sp_sem)
    other = pltpu.make_async_copy(moved_ref, sp_ref, sp_sem)

    @pl.when(group == 0)
    def _():
        own.start()

    @pl.when(group != 0)
    def _():
        other.start()

    copies = join_copies(parts, x_ref, sems, tiles)
    for moves in copies:
        for c in moves:
            c.start()
    gram_ref[...] = jnp.zeros_like(gram_ref)
    pw_ref[...] = jnp.zeros_like(pw_ref)

    @pl.when(group == 0)
    def _():
        own.wait()

    @pl.when(group != 0)
    def _():
        other.wait()

    points = column_scale(sp_ref[...])
    for t, (start, size) in enumerate(tiles):
        for c in copies[t]:
            c.wait()

        @pl.when(t * per < count)
        def _():
            scales = []
            for b in range(per):
                j = t * per + b
                w = jnp.where(j < count, w_ref[j], 0.0)
                scales.append(row_scale(x_ref[j * BLK : (j + 1) * BLK, :], w))
            scale = jnp.concatenate(scales, axis=0)
            inner = nt(x_ref[start : start + size, :], sp_ref[...])
            panel = (inner * inner * scale * points).astype(jnp.bfloat16)
            gram_ref[...] += tn(panel, panel)
            pw_ref[start : start + size, :] = (panel.astype(jnp.float32) * scale).astype(
                jnp.bfloat16
            )


def panel_products(parts, counts, weights, s, moved):
    rows, feat = parts[0].shape
    width = s.shape[1]
    tiles = len(row_tiles(rows)[1])
    return pl.pallas_call(
        functools.partial(panel_kernel, len(parts)),
        out_shape=(
            jax.ShapeDtypeStruct((PANEL, PANEL), jnp.float32),
            jax.ShapeDtypeStruct((rows, PANEL), jnp.bfloat16),
            jax.ShapeDtypeStruct((PANEL, width), jnp.bfloat16),
        ),
        in_specs=[SMEM, SMEM] + [ANY] * (len(parts) + 2),
        out_specs=(VMEM, VMEM, VMEM),
        scratch_shapes=[
            pltpu.VMEM((rows, width), jnp.bfloat16),
            pltpu.SemaphoreType.DMA((tiles, len(parts))),
            pltpu.SemaphoreType.DMA,
        ],
        compiler_params=params(),
        cost_estimate=cost(2 * rows * PANEL * (width + PANEL), 2 * rows * width),
        name="panel_products",
    )(counts, weights, *parts, s, moved)


def column_kernel(nparts, *refs):
    parts = refs[:nparts]
    pw_ref, s_ref, g_ref, x_ref, sems = refs[nparts:]
    width = x_ref.shape[1]

    @pl.when(pl.program_id(0) == 0)
    def _():
        copies = join_copies(parts, x_ref, sems, row_tiles(x_ref.shape[0])[1])
        for group in copies:
            for c in group:
                c.start()
        for group in copies:
            for c in group:
                c.wait()

    s = s_ref[...]
    inner = nt(s, x_ref[...])
    products = nn((inner * inner).astype(jnp.bfloat16), pw_ref[...])
    wide = s.astype(jnp.float32)
    square = jnp.sum(wide * wide, axis=1, keepdims=True) / width + EPSILON
    g_ref[...] = products / (width * square)


def column_products(parts, pw, s):
    rows, feat = parts[0].shape
    size, width = s.shape
    chunk = min(512, size)
    tiles = len(row_tiles(rows)[1])
    once = pl.Buffered(1)
    return pl.pallas_call(
        functools.partial(column_kernel, len(parts)),
        grid=(size // chunk,),
        out_shape=jax.ShapeDtypeStruct((size, PANEL), jnp.float32),
        in_specs=[ANY] * len(parts)
        + [
            pl.BlockSpec((rows, PANEL), lambda i: (0, 0), pipeline_mode=once),
            pl.BlockSpec((chunk, width), lambda i: (i, 0)),
        ],
        out_specs=pl.BlockSpec((chunk, PANEL), lambda i: (i, 0)),
        scratch_shapes=[
            pltpu.VMEM((rows, width), jnp.bfloat16),
            pltpu.SemaphoreType.DMA((tiles, len(parts))),
        ],
        compiler_params=params(dimension_semantics=("arbitrary",)),
        cost_estimate=cost(2 * rows * (width + PANEL) * size, 2 * rows * width),
        name="column_products",
    )(*parts, pw, s)


def rows_kernel(nparts, w_ref, *refs):
    parts = refs[:nparts]
    sp_ref, s_ref, kern_ref, p_ref, cs_ref, csp_ref, x_ref, rs_ref, sems = refs[nparts:]
    rows_all = x_ref.shape[0]
    chunk = s_ref.shape[0]
    blocks = rows_all // BLK
    bounds = list(range(0, blocks, 7)) + [blocks]
    spans = [(a * BLK, b * BLK) for a, b in zip(bounds, bounds[1:])]

    @pl.when(pl.program_id(0) == 0)
    def _():
        copies = join_copies(parts, x_ref, sems, [(a, b - a) for a, b in spans])
        for moves in copies:
            for c in moves:
                c.start()
        points = column_scale(sp_ref[...])
        csp_ref[...] = points
        for (a, b), moves in zip(spans, copies):
            for c in moves:
                c.wait()
            for j in range(a // BLK, b // BLK):
                scale = row_scale(x_ref[j * BLK : (j + 1) * BLK, :], w_ref[j])
                rs_ref[j * BLK : (j + 1) * BLK, :] = jnp.broadcast_to(scale, (BLK, 128))
            inner = nt(x_ref[a:b, :], sp_ref[...])
            scale = jnp.concatenate([rs_ref[a:b, :]] * (PANEL // 128), axis=1)
            p_ref[a:b, :] = (inner * inner * scale * points).astype(jnp.bfloat16)

    columns = column_scale(s_ref[...])
    cs_ref[...] = columns
    for a, b in spans:
        inner = nt(x_ref[a:b, :], s_ref[...])
        scale = jnp.concatenate([rs_ref[a:b, :]] * (chunk // 128), axis=1)
        kern_ref[a:b, :] = (inner * inner * scale * columns).astype(jnp.bfloat16)


def kernel_rows(parts, weights, sp, s):
    rows, feat = parts[0].shape
    cols, width = s.shape
    chunk = min(512, cols)
    once = pl.Buffered(1)
    return pl.pallas_call(
        functools.partial(rows_kernel, len(parts)),
        grid=(cols // chunk,),
        out_shape=(
            jax.ShapeDtypeStruct((rows, cols), jnp.bfloat16),
            jax.ShapeDtypeStruct((rows, PANEL), jnp.bfloat16),
            jax.ShapeDtypeStruct((1, cols), jnp.float32),
            jax.ShapeDtypeStruct((1, PANEL), jnp.float32),
        ),
        in_specs=[SMEM]
        + [ANY] * len(parts)
        + [
            pl.BlockSpec((PANEL, width), lambda i: (0, 0), pipeline_mode=once),
            pl.BlockSpec((chunk, width), lambda i: (i, 0)),
        ],
        out_specs=(
            pl.BlockSpec((rows, chunk), lambda i: (0, i)),
            pl.BlockSpec((rows, PANEL), lambda i: (0, 0)),
            pl.BlockSpec((1, chunk), lambda i: (0, i)),
            pl.BlockSpec((1, PANEL), lambda i: (0, 0)),
        ),
        scratch_shapes=[
            pltpu.VMEM((rows, width), jnp.bfloat16),
            pltpu.VMEM((rows, 128), jnp.float32),
            pltpu.SemaphoreType.DMA((2, len(parts))),
        ],
        compiler_params=params(dimension_semantics=("arbitrary",)),
        cost_estimate=cost(
            2 * rows * width * (cols + PANEL), 2 * rows * width + 2 * cols * width + 2 * rows * cols
        ),
        name="kernel_rows",
    )(weights, *parts, sp, s)


def seconds_kernel(nparts, place_ref, num_ref, w_ref, *refs):
    parts = refs[:nparts]
    sp_ref, csp_ref, s_ref, cs_ref = refs[nparts : nparts + 4]
    kern_ref, p_ref, x_ref, kbuf_ref, pbuf_ref, sems, out_sems = refs[nparts + 6 :]
    rows_all = x_ref.shape[0]
    blocks = rows_all // BLK
    num = num_ref[0]
    spans = [(a, min(2, blocks - a)) for a in range(0, blocks, 2)]
    copies = join_copies(parts, x_ref, sems, [(a * BLK, n * BLK) for a, n in spans])
    for moves in copies:
        for c in moves:
            c.start()

    def puts(j):
        rows = pl.ds(j * BLK, BLK)
        dst = pl.ds(pl.multiple_of(place_ref[j] * BLK, BLK), BLK)
        return [
            pltpu.make_async_copy(kbuf_ref.at[rows], kern_ref.at[dst], out_sems.at[j, 0]),
            pltpu.make_async_copy(pbuf_ref.at[rows], p_ref.at[dst], out_sems.at[j, 1]),
        ]

    for t, (first, n) in enumerate(spans):
        for c in copies[t]:
            c.wait()

        @pl.when(first < num)
        def _():
            a, b = first * BLK, (first + n) * BLK
            scale = jnp.concatenate(
                [row_scale(x_ref[j * BLK : (j + 1) * BLK, :], w_ref[j]) for j in range(first, first + n)],
                axis=0,
            )
            inner = nt(x_ref[a:b, :], sp_ref[...])
            pbuf_ref[a:b, :] = (inner * inner * scale * csp_ref[...]).astype(jnp.bfloat16)
            inner = nt(x_ref[a:b, :], s_ref[...])
            kbuf_ref[a:b, :] = (inner * inner * scale * cs_ref[...]).astype(jnp.bfloat16)

        for j in range(first, first + n):
            @pl.when(j < num)
            def _():
                for c in puts(j):
                    c.start()

    for j in range(blocks):
        @pl.when(j < num)
        def _():
            for c in puts(j):
                c.wait()


def second_rows(parts, places, num, weights, sp, csp, s, cs, kern, panel):
    rows, feat = parts[0].shape
    cols, width = s.shape
    n = len(parts)
    return pl.pallas_call(
        functools.partial(seconds_kernel, n),
        out_shape=(
            jax.ShapeDtypeStruct(kern.shape, kern.dtype),
            jax.ShapeDtypeStruct(panel.shape, panel.dtype),
        ),
        in_specs=[SMEM] * 3 + [ANY] * n + [VMEM] * 4 + [ANY, ANY],
        out_specs=(ANY, ANY),
        input_output_aliases={n + 7: 0, n + 8: 1},
        scratch_shapes=[
            pltpu.VMEM((rows, width), jnp.bfloat16),
            pltpu.VMEM((rows, cols), jnp.bfloat16),
            pltpu.VMEM((rows, PANEL), jnp.bfloat16),
            pltpu.SemaphoreType.DMA((-(-rows // (2 * BLK)), n)),
            pltpu.SemaphoreType.DMA((rows // BLK, 2)),
        ],
        compiler_params=params(),
        cost_estimate=cost(2 * rows * width * (cols + PANEL), 2 * cols * width),
        name="second_rows",
    )(places, num, weights, *parts, sp, csp, s, cs, kern, panel)


def remainder_kernel(norm, quarter_ref, kern_ref, p_ref, inv_ref, rt_ref, out_ref, proj_ref):
    chunk = kern_ref.shape[1]
    step = pl.program_id(0)
    inv_high, inv_low = split(inv_ref[...])
    rt = rt_ref[0]
    coef = (nn(rt, inv_high) + nn(rt, inv_low)).astype(jnp.bfloat16)
    proj_ref[...] = rt.astype(jnp.float32).T * (1.0 / norm)
    fit = nt(p_ref[...], coef)
    out_ref[...] = (kern_ref[...].astype(jnp.float32) - fit).astype(out_ref.dtype)

    part = min(chunk, PANEL)
    for i in range(PANEL // part):
        @pl.when((step == i) & (lax.axis_index("cols") == 0))
        def _():
            panel = p_ref[...]
            rows = slice(i * part, (i + 1) * part)
            basis = nt(panel, inv_high[rows, :]) + nt(panel, inv_low[rows, :])
            out_ref[:, :part] = (basis * norm).astype(out_ref.dtype)


def remainder_rows(kern, panel, quarter, inverse, rt, norm):
    rows, cols = kern.shape
    chunk = rt.shape[1]
    once = pl.Buffered(1)
    spec = pltpu.PrefetchScalarGridSpec(
        num_scalar_prefetch=1,
        grid=(cols // chunk,),
        in_specs=[
            pl.BlockSpec((rows, chunk), lambda i, q: (0, i)),
            pl.BlockSpec((rows, PANEL), lambda i, q: (0, 0), pipeline_mode=once),
            pl.BlockSpec((PANEL, PANEL), lambda i, q: (0, 0), pipeline_mode=once),
            pl.BlockSpec((1, chunk, PANEL), lambda i, q: (i ^ q[0], 0, 0)),
        ],
        out_specs=(
            pl.BlockSpec((rows, chunk), lambda i, q: (0, i)),
            pl.BlockSpec((PANEL, chunk), lambda i, q: (0, i)),
        ),
    )
    return pl.pallas_call(
        functools.partial(remainder_kernel, norm),
        grid_spec=spec,
        out_shape=(
            jax.ShapeDtypeStruct((rows, cols), jnp.bfloat16),
            jax.ShapeDtypeStruct((PANEL, cols), jnp.float32),
        ),
        compiler_params=params(dimension_semantics=("arbitrary",)),
        cost_estimate=cost(2 * rows * PANEL * cols, 4 * rows * cols),
        name="remainder_rows",
    )(quarter, kern, panel, inverse, rt)


def flips(bit, size):
    return [(i, i ^ bit) for i in range(size)]


def quarter_of(pair):
    me = lax.axis_index("rows").astype(jnp.int32)
    return (me // pair[0]) % 2 + 2 * ((me // pair[1]) % 2)


def trade(x, pair, k):
    bit = pair[0] * (k & 1) + pair[1] * (k >> 1)
    return lax.ppermute(x, "rows", flips(bit, lax.axis_size("rows")))


def quarters(x, pair):
    n = x.shape[0] // 4
    q = quarter_of(pair)
    return [lax.dynamic_slice_in_dim(x, (q ^ k) * n, n, 0) for k in range(4)]


def trades(pieces, pair):
    return [pieces[0]] + [trade(pieces[k], pair, k) for k in range(1, 4)]


def total(got):
    return (got[0] + got[1]) + (got[2] + got[3])


def gather_pieces(x, pair):
    return [x] + [trade(x, pair, k) for k in range(1, 4)]


def gather_back(x, pair):
    q = quarter_of(pair)
    pieces = gather_pieces(x, pair)
    return jnp.concatenate([lax.select_n(q ^ i, *pieces) for i in range(4)], 0)


def pair_sum(x, pair):
    got = gather_pieces(x, pair)
    return (got[0] + got[1]) + (got[2] + got[3])


def on_device(descriptors, sparse_points, block_weights, block_counts, destinations):
    owners = lax.axis_size("rows")
    groups = lax.axis_size("cols")
    me = lax.axis_index("rows").astype(jnp.int32)
    group = lax.axis_index("cols").astype(jnp.int32)
    slots = block_weights.shape[0]
    per_pair = -(-slots // owners)
    feat = descriptors.shape[1]
    cols, width = sparse_points.shape
    norm = math.sqrt(owners * DST_BLK * BLK)
    pairs = [(1 << i, 2 << i) for i in range(0, owners.bit_length() - 1, 2)]

    first = sparse_points[:PANEL]
    source_parts = share_parts(descriptors)
    if groups == 2:
        moved = lax.ppermute(first, "cols", [(0, 1), (1, 0)])
    else:
        moved = lax.all_gather(first, "cols", axis=0, tiled=False)[0]
    desc_blocks = descriptors.reshape(slots, BLK, feat)
    outgoing = pack(desc_blocks, destinations, block_counts, per_pair)
    received = [lax.all_to_all(outgoing[0], "rows", split_axis=0, concat_axis=0, tiled=True)]

    weights32 = block_weights.astype(jnp.float32)
    gram_part, pw, panel_points = panel_products(
        source_parts, block_counts, weights32, sparse_points, moved
    )
    sent = quarters(column_products(source_parts, pw, sparse_points), pairs[0])

    spare = -(-owners * slots // (PANEL * 8)) * 8
    table = lax.dynamic_update_slice(
        jnp.zeros((spare * PANEL,), jnp.float32), weights32, (me * slots,)
    ).reshape(spare, PANEL)
    if groups == 2:
        gram_part = lax.dynamic_slice_in_dim(gram_part, group * (PANEL // 2), PANEL // 2, 0)
    summed = pair_sum(jnp.concatenate([gram_part, table], 0), pairs[0])
    summed, *sent = lax.optimization_barrier((summed, *sent))
    near = trades(sent, pairs[0])
    for pair in pairs[1:]:
        got = gather_pieces(summed, pair)
        if per_pair > 1 and pair == pairs[-1]:
            got, last, received[0] = lax.optimization_barrier((got, outgoing[1], received[0]))
            received.append(
                lax.all_to_all(last, "rows", split_axis=0, concat_axis=0, tiled=True)
            )
        summed = total(got)
    gram, table = summed[:-spare], summed[-spare:]
    if groups == 2:
        other = lax.ppermute(gram, "cols", [(0, 1), (1, 0)])
        gram = jnp.where(
            group == 0, jnp.concatenate([gram, other], 0), jnp.concatenate([other, gram], 0)
        )
    all_weights = table.reshape(-1)[: owners * slots]

    inverse = factor(gram)

    slot_ids = jnp.arange(slots, dtype=jnp.int32)
    toward = ((slot_ids[None, :] < block_counts[:, None]) & (destinations == me)).astype(jnp.int32)
    rank = jnp.cumsum(toward, axis=1) - toward
    flat = toward.reshape(-1)
    place = jnp.cumsum(flat) - flat
    where_from = (jnp.arange(owners, dtype=jnp.int32)[:, None] * per_pair + rank).reshape(-1)
    hit = (flat[None, :] == 1) & (place[None, :] == jnp.arange(DST_BLK, dtype=jnp.int32)[:, None])
    positions = jnp.sum(jnp.where(hit, where_from[None, :], 0), axis=1)
    weights_here = jnp.sum(jnp.where(hit, all_weights[None, :], 0.0), axis=1)
    from_owner = positions // per_pair
    is_second = positions % per_pair == 1
    order = jnp.cumsum(is_second.astype(jnp.int32))
    most = DST_BLK // 2
    pick = is_second[None, :] & (order[None, :] == 1 + jnp.arange(most, dtype=jnp.int32)[:, None])
    places = jnp.sum(jnp.where(pick, jnp.arange(DST_BLK, dtype=jnp.int32)[None, :], 0), axis=1)
    second_owner = jnp.sum(jnp.where(pick, from_owner[None, :], 0), axis=1)
    second_weights = jnp.sum(jnp.where(pick, weights_here[None, :], 0.0), axis=1)

    inverse, *near = lax.optimization_barrier((inverse, *near))
    g = total(near)
    for pair in pairs[1:]:
        sent = quarters(g, pair)
        if pair == pairs[-1]:
            from_owner, *sent = lax.optimization_barrier((from_owner, *sent))
        far = trades(sent, pair)
        g = total(far)
    arrived = select(received[0], from_owner).reshape(DST_BLK * BLK, feat)
    kern, panel, cs, csp = kernel_rows(
        share_parts(arrived), weights_here, panel_points, sparse_points
    )
    kern, *far = lax.optimization_barrier((kern, *far))
    rt = nt(total(far), inverse, HIGH).astype(jnp.bfloat16)
    if per_pair > 1:
        rt, second_owner = lax.optimization_barrier((rt, second_owner))
        late = share_parts(select(received[1], second_owner).reshape(most * BLK, feat))
    for pair in pairs[:0:-1]:
        rt = gather_back(rt, pair)
    rt, kern = lax.optimization_barrier((rt, kern))
    pieces = gather_pieces(rt, pairs[0])
    if per_pair > 1:
        kern, panel = second_rows(
            late,
            places,
            order[-1:],
            second_weights,
            panel_points,
            csp,
            sparse_points,
            cs,
            kern,
            panel,
        )
    kern, *pieces = lax.optimization_barrier((kern, *pieces))
    remainder, projected = remainder_rows(
        kern, panel, quarter_of(pairs[0])[None], inverse, jnp.stack(pieces), norm
    )
    return (projected, remainder)


def solution(mesh):
    return jax.shard_map(
        on_device,
        mesh=mesh,
        in_specs=(P("rows", "cols"), P("cols", None), P("rows"), P(), P()),
        out_specs=(P(None, "cols"), P("rows", "cols")),
        check_vma=False,
    )
```

```python
import functools
import math

import jax
import jax.numpy as jnp
from jax import lax
from jax.experimental import pallas as pl
from jax.experimental.pallas import tpu as pltpu
from jax.sharding import PartitionSpec as P

PANEL = 256
BLK = 128
DST_BLK = 13
EPSILON = 1e-06
VMEM_LIMIT = 56 * 1024 * 1024
HIGH = lax.Precision.HIGHEST
ANY = pl.BlockSpec(memory_space=pl.ANY)
VMEM = pl.BlockSpec(memory_space=pltpu.VMEM)
SMEM = pl.BlockSpec(memory_space=pltpu.SMEM)


def params(**kw):
    return pltpu.CompilerParams(vmem_limit_bytes=VMEM_LIMIT, **kw)


def cost(flops, nbytes):
    return pl.CostEstimate(flops=int(flops), bytes_accessed=int(nbytes), transcendentals=0)


def dot(a, b, ca, cb, precision=None):
    return lax.dot_general(
        a, b, (((ca,), (cb,)), ((), ())), preferred_element_type=jnp.float32, precision=precision
    )


def nt(a, b, precision=None):
    return dot(a, b, 1, 1, precision)


def nn(a, b, precision=None):
    return dot(a, b, 1, 0, precision)


def tn(a, b, precision=None):
    return dot(a, b, 0, 0, precision)


def split(x):
    high = x.astype(jnp.bfloat16)
    return high, (x - high.astype(jnp.float32)).astype(jnp.bfloat16)


HEAD = 32


def block_copies(rank, whole_ref, outer, first_ref, last_ref, sems):
    if rank == 0:
        pairs = [(whole_ref, first_ref.at[outer, pl.ds(0, BLK)])]
    else:
        pairs = [
            (whole_ref.at[pl.ds(0, HEAD)], first_ref.at[outer, pl.ds(BLK, HEAD)]),
            (whole_ref.at[pl.ds(HEAD, BLK - HEAD)], last_ref.at[outer]),
        ]
    return [(a, b, sems.at[i]) for i, (a, b) in enumerate(pairs)]


def pack_kernel(per_pair, dest_ref, cnt_ref, desc_ref, *refs):
    out_refs, (ctr_ref, rank_ref, sems) = refs[:per_pair], refs[per_pair:]
    slots = desc_ref.shape[0]
    owners = ctr_ref.shape[0]
    me = lax.axis_index("rows")
    count = cnt_ref[me]

    def copies(j, d, rank):
        moves = block_copies(rank, desc_ref.at[j], d, out_refs[0], out_refs[-1], sems.at[j])
        return [pltpu.make_async_copy(a, b, sem) for a, b, sem in moves]

    @pl.loop(0, owners)
    def _(i):
        ctr_ref[i] = 0

    @pl.loop(0, slots)
    def _(j):
        @pl.when(j < count)
        def _():
            d = dest_ref[me, j]
            rank = ctr_ref[d]
            ctr_ref[d] = rank + 1
            rank_ref[j] = rank
            for r in range(per_pair):
                @pl.when(rank == r)
                def _():
                    for c in copies(j, d, r):
                        c.start()

    @pl.loop(0, slots)
    def _(j):
        @pl.when(j < count)
        def _():
            for r in range(per_pair):
                @pl.when(rank_ref[j] == r)
                def _():
                    for c in copies(j, 0, r):
                        c.wait()


def pack(desc_blocks, destinations, counts, per_pair):
    slots, blk, feat = desc_blocks.shape
    owners = destinations.shape[0]
    heights = [blk] if per_pair == 1 else [blk + HEAD, blk - HEAD]
    return pl.pallas_call(
        functools.partial(pack_kernel, per_pair),
        out_shape=[
            jax.ShapeDtypeStruct((owners, h, feat), desc_blocks.dtype) for h in heights
        ],
        in_specs=[SMEM, SMEM, VMEM],
        out_specs=[ANY] * per_pair,
        scratch_shapes=[
            pltpu.SMEM((owners,), jnp.int32),
            pltpu.SMEM((slots,), jnp.int32),
            pltpu.SemaphoreType.DMA((slots, 2)),
        ],
        compiler_params=params(),
        cost_estimate=cost(0, 4 * slots * blk * feat),
        name="pack",
    )(destinations, counts, desc_blocks)


def select_kernel(rows, owner_ref, *refs):
    recv_refs, (out_ref, sems) = refs[: len(rows)], refs[len(rows) :]
    copies = []
    for p in range(out_ref.shape[0]):
        at = 0
        for i, (start, size) in enumerate(rows):
            src = recv_refs[i].at[owner_ref[p], pl.ds(start, size)]
            copies.append(pltpu.make_async_copy(src, out_ref.at[p, pl.ds(at, size)], sems.at[p, i]))
            at += size
    for c in copies:
        c.start()
    for c in copies:
        c.wait()


def select(received, rows, from_owner):
    feat = received[0].shape[-1]
    count = from_owner.shape[0]
    return pl.pallas_call(
        functools.partial(select_kernel, rows),
        out_shape=jax.ShapeDtypeStruct((count, BLK, feat), received[0].dtype),
        in_specs=[SMEM] + [ANY] * len(rows),
        out_specs=VMEM,
        scratch_shapes=[pltpu.SemaphoreType.DMA((count, len(rows)))],
        compiler_params=params(),
        cost_estimate=cost(0, 4 * count * BLK * feat),
        name="select",
    )(from_owner, *received)


def small_factor(a):
    n = a.shape[0]
    row = lax.broadcasted_iota(jnp.int32, (n, 1), 0)
    eye = lax.broadcasted_iota(jnp.int32, (n, n), 0) == lax.broadcasted_iota(jnp.int32, (n, n), 1)
    m = jnp.concatenate([a, eye.astype(jnp.float32)], axis=1)
    out = []
    for j in range(0, n, 2):
        r0 = m[j : j + 1, :]
        r1 = m[j + 1 : j + 2, :]
        p = r0[:, j : j + 1]
        q = r0[:, j + 1 : j + 2]
        s = r1[:, j + 1 : j + 2]
        det = p * s - q * q
        out.append(r0[:, n:] * lax.rsqrt(p))
        out.append((r1[:, n:] - (q / p) * r0[:, n:]) * lax.rsqrt(det / p))
        if j + 2 < n:
            inv = 1.0 / det
            g0 = (s * r0 - q * r1) * inv
            g1 = (p * r1 - q * r0) * inv
            c0 = jnp.where(row > j + 1, m[:, j : j + 1], 0.0)
            c1 = jnp.where(row > j + 1, m[:, j + 1 : j + 2], 0.0)
            m = m - c0 * g0 - c1 * g1
    return out


def factor_kernel(leaf, gram_ref, x_ref, a_ref):
    n = gram_ref.shape[0]
    a_ref[...] = gram_ref[...]
    x_ref[...] = jnp.zeros_like(x_ref)
    for k in range(0, n, leaf):
        e = k + leaf
        for i, r in enumerate(small_factor(a_ref[k:e, k:e])):
            x_ref[k + i : k + i + 1, k:e] = r
        xk = x_ref[k:e, k:e]
        if e < n:
            t = nn(xk, a_ref[k:e, e:], HIGH)
            a_ref[k:e, e:] = t
            a_ref[e:, e:] -= tn(t, t, HIGH)
        if k > 0:
            x_ref[k:e, :k] = -nn(xk, tn(a_ref[:k, k:e], x_ref[:k, :k], HIGH), HIGH)


def factor(gram):
    n = gram.shape[0]
    return pl.pallas_call(
        functools.partial(factor_kernel, 64),
        out_shape=jax.ShapeDtypeStruct((n, n), jnp.float32),
        scratch_shapes=[pltpu.VMEM((n, n), jnp.float32)],
        compiler_params=params(),
        cost_estimate=cost(1e11, 8 * n * n),
        name="factor",
    )(gram)


def share_parts(x):
    groups = lax.axis_size("cols")
    if groups == 2:
        peer = lax.ppermute(x, "cols", [(0, 1), (1, 0)])
        return [x, peer]
    full = lax.all_gather(x, "cols", axis=0, tiled=False)
    return [full[i] for i in range(groups)]


def part_offset(i, feat):
    if lax.axis_size("cols") == 2:
        c = lax.axis_index("cols")
        return (c if i == 0 else 1 - c) * feat
    return i * feat


def join_copies(parts, x_ref, sems, spans):
    feat = parts[0].shape[1]
    return [
        [
            pltpu.make_async_copy(
                ref.at[pl.ds(start, size)],
                x_ref.at[pl.ds(start, size), pl.ds(pl.multiple_of(part_offset(i, feat), 128), feat)],
                sems.at[t, i],
            )
            for i, ref in enumerate(parts)
        ]
        for t, (start, size) in enumerate(spans)
    ]


def row_scale(x, weight):
    x = x.astype(jnp.float32)
    return weight / (jnp.sum(x * x, axis=1, keepdims=True) / x.shape[1] + EPSILON)


def column_scale(s):
    s = s.astype(jnp.float32)
    width = s.shape[1]
    scale = 1.0 / (width * (jnp.sum(s * s, axis=1, keepdims=True) / width + EPSILON))
    return jnp.broadcast_to(scale, (s.shape[0], 128)).T[:1, :]


def row_tiles(rows):
    blocks = rows // BLK
    per = 5 if blocks % 5 == 0 else 1
    return per, [(i * BLK, per * BLK) for i in range(0, blocks, per)]


def panel_kernel(nparts, cnt_ref, w_ref, *refs):
    parts = refs[:nparts]
    s_ref, moved_ref, gram_ref, pw_ref, sp_ref, x_ref, sems, sp_sem = refs[nparts:]
    per, tiles = row_tiles(x_ref.shape[0])
    count = cnt_ref[lax.axis_index("rows")]
    group = lax.axis_index("cols")
    own = pltpu.make_async_copy(s_ref.at[pl.ds(0, PANEL)], sp_ref, sp_sem)
    other = pltpu.make_async_copy(moved_ref, sp_ref, sp_sem)

    @pl.when(group == 0)
    def _():
        own.start()

    @pl.when(group != 0)
    def _():
        other.start()

    copies = join_copies(parts, x_ref, sems, tiles)
    for moves in copies:
        for c in moves:
            c.start()
    gram_ref[...] = jnp.zeros_like(gram_ref)
    pw_ref[...] = jnp.zeros_like(pw_ref)

    @pl.when(group == 0)
    def _():
        own.wait()

    @pl.when(group != 0)
    def _():
        other.wait()

    points = column_scale(sp_ref[...])
    for t, (start, size) in enumerate(tiles):
        for c in copies[t]:
            c.wait()

        @pl.when(t * per < count)
        def _():
            scales = []
            for b in range(per):
                j = t * per + b
                w = jnp.where(j < count, w_ref[j], 0.0)
                scales.append(row_scale(x_ref[j * BLK : (j + 1) * BLK, :], w))
            scale = jnp.concatenate(scales, axis=0)
            inner = nt(x_ref[start : start + size, :], sp_ref[...])
            panel = (inner * inner * scale * points).astype(jnp.bfloat16)
            gram_ref[...] += tn(panel, panel)
            pw_ref[start : start + size, :] = (panel.astype(jnp.float32) * scale).astype(
                jnp.bfloat16
            )


def panel_products(parts, counts, weights, s, moved):
    rows, feat = parts[0].shape
    width = s.shape[1]
    tiles = len(row_tiles(rows)[1])
    return pl.pallas_call(
        functools.partial(panel_kernel, len(parts)),
        out_shape=(
            jax.ShapeDtypeStruct((PANEL, PANEL), jnp.float32),
            jax.ShapeDtypeStruct((rows, PANEL), jnp.bfloat16),
            jax.ShapeDtypeStruct((PANEL, width), jnp.bfloat16),
        ),
        in_specs=[SMEM, SMEM] + [ANY] * (len(parts) + 2),
        out_specs=(VMEM, VMEM, VMEM),
        scratch_shapes=[
            pltpu.VMEM((rows, width), jnp.bfloat16),
            pltpu.SemaphoreType.DMA((tiles, len(parts))),
            pltpu.SemaphoreType.DMA,
        ],
        compiler_params=params(),
        cost_estimate=cost(2 * rows * PANEL * (width + PANEL), 2 * rows * width),
        name="panel_products",
    )(counts, weights, *parts, s, moved)


def column_kernel(nparts, *refs):
    parts = refs[:nparts]
    pw_ref, s_ref, g_ref, x_ref, sems = refs[nparts:]
    width = x_ref.shape[1]

    @pl.when(pl.program_id(0) == 0)
    def _():
        copies = join_copies(parts, x_ref, sems, row_tiles(x_ref.shape[0])[1])
        for group in copies:
            for c in group:
                c.start()
        for group in copies:
            for c in group:
                c.wait()

    s = s_ref[...]
    inner = nt(s, x_ref[...])
    products = nn((inner * inner).astype(jnp.bfloat16), pw_ref[...])
    wide = s.astype(jnp.float32)
    square = jnp.sum(wide * wide, axis=1, keepdims=True) / width + EPSILON
    g_ref[...] = products / (width * square)


def column_products(parts, pw, s):
    rows, feat = parts[0].shape
    size, width = s.shape
    chunk = min(512, size)
    tiles = len(row_tiles(rows)[1])
    once = pl.Buffered(1)
    return pl.pallas_call(
        functools.partial(column_kernel, len(parts)),
        grid=(size // chunk,),
        out_shape=jax.ShapeDtypeStruct((size, PANEL), jnp.float32),
        in_specs=[ANY] * len(parts)
        + [
            pl.BlockSpec((rows, PANEL), lambda i: (0, 0), pipeline_mode=once),
            pl.BlockSpec((chunk, width), lambda i: (i, 0)),
        ],
        out_specs=pl.BlockSpec((chunk, PANEL), lambda i: (i, 0)),
        scratch_shapes=[
            pltpu.VMEM((rows, width), jnp.bfloat16),
            pltpu.SemaphoreType.DMA((tiles, len(parts))),
        ],
        compiler_params=params(dimension_semantics=("arbitrary",)),
        cost_estimate=cost(2 * rows * (width + PANEL) * size, 2 * rows * width),
        name="column_products",
    )(*parts, pw, s)


def rows_kernel(nparts, w_ref, *refs):
    parts = refs[:nparts]
    sp_ref, s_ref, kern_ref, p_ref, cs_ref, csp_ref, x_ref, rs_ref, sems = refs[nparts:]
    rows_all = x_ref.shape[0]
    chunk = s_ref.shape[0]
    blocks = rows_all // BLK
    bounds = list(range(0, blocks, 7)) + [blocks]
    spans = [(a * BLK, b * BLK) for a, b in zip(bounds, bounds[1:])]

    @pl.when(pl.program_id(0) == 0)
    def _():
        copies = join_copies(parts, x_ref, sems, [(a, b - a) for a, b in spans])
        for moves in copies:
            for c in moves:
                c.start()
        points = column_scale(sp_ref[...])
        csp_ref[...] = points
        for (a, b), moves in zip(spans, copies):
            for c in moves:
                c.wait()
            for j in range(a // BLK, b // BLK):
                scale = row_scale(x_ref[j * BLK : (j + 1) * BLK, :], w_ref[j])
                rs_ref[j * BLK : (j + 1) * BLK, :] = jnp.broadcast_to(scale, (BLK, 128))
            inner = nt(x_ref[a:b, :], sp_ref[...])
            scale = jnp.concatenate([rs_ref[a:b, :]] * (PANEL // 128), axis=1)
            p_ref[a:b, :] = (inner * inner * scale * points).astype(jnp.bfloat16)

    columns = column_scale(s_ref[...])
    cs_ref[...] = columns
    for a, b in spans:
        inner = nt(x_ref[a:b, :], s_ref[...])
        scale = jnp.concatenate([rs_ref[a:b, :]] * (chunk // 128), axis=1)
        kern_ref[a:b, :] = (inner * inner * scale * columns).astype(jnp.bfloat16)


def kernel_rows(parts, weights, sp, s):
    rows, feat = parts[0].shape
    cols, width = s.shape
    chunk = min(512, cols)
    once = pl.Buffered(1)
    return pl.pallas_call(
        functools.partial(rows_kernel, len(parts)),
        grid=(cols // chunk,),
        out_shape=(
            jax.ShapeDtypeStruct((rows, cols), jnp.bfloat16),
            jax.ShapeDtypeStruct((rows, PANEL), jnp.bfloat16),
            jax.ShapeDtypeStruct((1, cols), jnp.float32),
            jax.ShapeDtypeStruct((1, PANEL), jnp.float32),
        ),
        in_specs=[SMEM]
        + [ANY] * len(parts)
        + [
            pl.BlockSpec((PANEL, width), lambda i: (0, 0), pipeline_mode=once),
            pl.BlockSpec((chunk, width), lambda i: (i, 0)),
        ],
        out_specs=(
            pl.BlockSpec((rows, chunk), lambda i: (0, i)),
            pl.BlockSpec((rows, PANEL), lambda i: (0, 0)),
            pl.BlockSpec((1, chunk), lambda i: (0, i)),
            pl.BlockSpec((1, PANEL), lambda i: (0, 0)),
        ),
        scratch_shapes=[
            pltpu.VMEM((rows, width), jnp.bfloat16),
            pltpu.VMEM((rows, 128), jnp.float32),
            pltpu.SemaphoreType.DMA((2, len(parts))),
        ],
        compiler_params=params(dimension_semantics=("arbitrary",)),
        cost_estimate=cost(
            2 * rows * width * (cols + PANEL), 2 * rows * width + 2 * cols * width + 2 * rows * cols
        ),
        name="kernel_rows",
    )(weights, *parts, sp, s)


def seconds_kernel(nparts, place_ref, num_ref, w_ref, *refs):
    parts = refs[:nparts]
    sp_ref, csp_ref, s_ref, cs_ref = refs[nparts : nparts + 4]
    kern_ref, p_ref, x_ref, kbuf_ref, pbuf_ref, sems, out_sems = refs[nparts + 6 :]
    rows_all = x_ref.shape[0]
    blocks = rows_all // BLK
    num = num_ref[0]
    spans = [(a, min(2, blocks - a)) for a in range(0, blocks, 2)]
    copies = join_copies(parts, x_ref, sems, [(a * BLK, n * BLK) for a, n in spans])
    for moves in copies:
        for c in moves:
            c.start()

    def puts(j):
        rows = pl.ds(j * BLK, BLK)
        dst = pl.ds(pl.multiple_of(place_ref[j] * BLK, BLK), BLK)
        return [
            pltpu.make_async_copy(kbuf_ref.at[rows], kern_ref.at[dst], out_sems.at[j, 0]),
            pltpu.make_async_copy(pbuf_ref.at[rows], p_ref.at[dst], out_sems.at[j, 1]),
        ]

    for t, (first, n) in enumerate(spans):
        for c in copies[t]:
            c.wait()

        @pl.when(first < num)
        def _():
            a, b = first * BLK, (first + n) * BLK
            scale = jnp.concatenate(
                [row_scale(x_ref[j * BLK : (j + 1) * BLK, :], w_ref[j]) for j in range(first, first + n)],
                axis=0,
            )
            inner = nt(x_ref[a:b, :], sp_ref[...])
            pbuf_ref[a:b, :] = (inner * inner * scale * csp_ref[...]).astype(jnp.bfloat16)
            inner = nt(x_ref[a:b, :], s_ref[...])
            kbuf_ref[a:b, :] = (inner * inner * scale * cs_ref[...]).astype(jnp.bfloat16)

        for j in range(first, first + n):
            @pl.when(j < num)
            def _():
                for c in puts(j):
                    c.start()

    for j in range(blocks):
        @pl.when(j < num)
        def _():
            for c in puts(j):
                c.wait()


def second_rows(parts, places, num, weights, sp, csp, s, cs, kern, panel):
    rows, feat = parts[0].shape
    cols, width = s.shape
    n = len(parts)
    return pl.pallas_call(
        functools.partial(seconds_kernel, n),
        out_shape=(
            jax.ShapeDtypeStruct(kern.shape, kern.dtype),
            jax.ShapeDtypeStruct(panel.shape, panel.dtype),
        ),
        in_specs=[SMEM] * 3 + [ANY] * n + [VMEM] * 4 + [ANY, ANY],
        out_specs=(ANY, ANY),
        input_output_aliases={n + 7: 0, n + 8: 1},
        scratch_shapes=[
            pltpu.VMEM((rows, width), jnp.bfloat16),
            pltpu.VMEM((rows, cols), jnp.bfloat16),
            pltpu.VMEM((rows, PANEL), jnp.bfloat16),
            pltpu.SemaphoreType.DMA((-(-rows // (2 * BLK)), n)),
            pltpu.SemaphoreType.DMA((rows // BLK, 2)),
        ],
        compiler_params=params(),
        cost_estimate=cost(2 * rows * width * (cols + PANEL), 2 * cols * width),
        name="second_rows",
    )(places, num, weights, *parts, sp, csp, s, cs, kern, panel)


def remainder_kernel(norm, quarter_ref, kern_ref, p_ref, inv_ref, rt_ref, out_ref, proj_ref):
    chunk = kern_ref.shape[1]
    step = pl.program_id(0)
    inv_high, inv_low = split(inv_ref[...])
    rt = rt_ref[0]
    coef = (nn(rt, inv_high) + nn(rt, inv_low)).astype(jnp.bfloat16)
    proj_ref[...] = rt.astype(jnp.float32).T * (1.0 / norm)
    fit = nt(p_ref[...], coef)
    out_ref[...] = (kern_ref[...].astype(jnp.float32) - fit).astype(out_ref.dtype)

    part = min(chunk, PANEL)
    for i in range(PANEL // part):
        @pl.when((step == i) & (lax.axis_index("cols") == 0))
        def _():
            panel = p_ref[...]
            rows = slice(i * part, (i + 1) * part)
            basis = nt(panel, inv_high[rows, :]) + nt(panel, inv_low[rows, :])
            out_ref[:, :part] = (basis * norm).astype(out_ref.dtype)


def remainder_rows(kern, panel, quarter, inverse, rt, norm):
    rows, cols = kern.shape
    chunk = rt.shape[1]
    once = pl.Buffered(1)
    spec = pltpu.PrefetchScalarGridSpec(
        num_scalar_prefetch=1,
        grid=(cols // chunk,),
        in_specs=[
            pl.BlockSpec((rows, chunk), lambda i, q: (0, i)),
            pl.BlockSpec((rows, PANEL), lambda i, q: (0, 0), pipeline_mode=once),
            pl.BlockSpec((PANEL, PANEL), lambda i, q: (0, 0), pipeline_mode=once),
            pl.BlockSpec((1, chunk, PANEL), lambda i, q: (i ^ q[0], 0, 0)),
        ],
        out_specs=(
            pl.BlockSpec((rows, chunk), lambda i, q: (0, i)),
            pl.BlockSpec((PANEL, chunk), lambda i, q: (0, i)),
        ),
    )
    return pl.pallas_call(
        functools.partial(remainder_kernel, norm),
        grid_spec=spec,
        out_shape=(
            jax.ShapeDtypeStruct((rows, cols), jnp.bfloat16),
            jax.ShapeDtypeStruct((PANEL, cols), jnp.float32),
        ),
        compiler_params=params(dimension_semantics=("arbitrary",)),
        cost_estimate=cost(2 * rows * PANEL * cols, 4 * rows * cols),
        name="remainder_rows",
    )(quarter, kern, panel, inverse, rt)


def flips(bit, size):
    return [(i, i ^ bit) for i in range(size)]


def quarter_of(pair):
    me = lax.axis_index("rows").astype(jnp.int32)
    return (me // pair[0]) % 2 + 2 * ((me // pair[1]) % 2)


def trade(x, pair, k):
    bit = pair[0] * (k & 1) + pair[1] * (k >> 1)
    return lax.ppermute(x, "rows", flips(bit, lax.axis_size("rows")))


def quarters(x, pair):
    n = x.shape[0] // 4
    q = quarter_of(pair)
    return [lax.dynamic_slice_in_dim(x, (q ^ k) * n, n, 0) for k in range(4)]


def trades(pieces, pair):
    return [pieces[0]] + [trade(pieces[k], pair, k) for k in range(1, 4)]


def total(got):
    return (got[0] + got[1]) + (got[2] + got[3])


def gather_pieces(x, pair):
    return [x] + [trade(x, pair, k) for k in range(1, 4)]


def gather_back(x, pair):
    q = quarter_of(pair)
    pieces = gather_pieces(x, pair)
    return jnp.concatenate([lax.select_n(q ^ i, *pieces) for i in range(4)], 0)


def pair_sum(x, pair):
    got = gather_pieces(x, pair)
    return (got[0] + got[1]) + (got[2] + got[3])


def on_device(descriptors, sparse_points, block_weights, block_counts, destinations):
    owners = lax.axis_size("rows")
    groups = lax.axis_size("cols")
    me = lax.axis_index("rows").astype(jnp.int32)
    group = lax.axis_index("cols").astype(jnp.int32)
    slots = block_weights.shape[0]
    per_pair = -(-slots // owners)
    feat = descriptors.shape[1]
    cols, width = sparse_points.shape
    norm = math.sqrt(owners * DST_BLK * BLK)
    pairs = [(1 << i, 2 << i) for i in range(0, owners.bit_length() - 1, 2)]

    first = sparse_points[:PANEL]
    source_parts = share_parts(descriptors)
    if groups == 2:
        moved = lax.ppermute(first, "cols", [(0, 1), (1, 0)])
    else:
        moved = lax.all_gather(first, "cols", axis=0, tiled=False)[0]
    desc_blocks = descriptors.reshape(slots, BLK, feat)
    outgoing = list(pack(desc_blocks, destinations, block_counts, per_pair))

    weights32 = block_weights.astype(jnp.float32)
    spare = -(-owners * slots // (PANEL * 8)) * 8
    table = lax.dynamic_update_slice(
        jnp.zeros((spare * PANEL,), jnp.float32), weights32, (me * slots,)
    ).reshape(spare, PANEL)
    for pair in pairs[::-1]:
        table = pair_sum(table, pair)
    table, outgoing[0], source_parts = lax.optimization_barrier(
        (table, outgoing[0], source_parts)
    )
    all_weights = table.reshape(-1)[: owners * slots]
    received = [lax.all_to_all(outgoing[0], "rows", split_axis=0, concat_axis=0, tiled=True)]

    gram_part, pw, panel_points = panel_products(
        source_parts, block_counts, weights32, sparse_points, moved
    )
    sent = quarters(column_products(source_parts, pw, sparse_points), pairs[0])

    slot_ids = jnp.arange(slots, dtype=jnp.int32)
    toward = ((slot_ids[None, :] < block_counts[:, None]) & (destinations == me)).astype(jnp.int32)
    rank = jnp.cumsum(toward, axis=1) - toward
    flat = toward.reshape(-1)
    place = jnp.cumsum(flat) - flat
    where_from = (jnp.arange(owners, dtype=jnp.int32)[:, None] * per_pair + rank).reshape(-1)
    hit = (flat[None, :] == 1) & (place[None, :] == jnp.arange(DST_BLK, dtype=jnp.int32)[:, None])
    positions = jnp.sum(jnp.where(hit, where_from[None, :], 0), axis=1)
    weights_here = jnp.sum(jnp.where(hit, all_weights[None, :], 0.0), axis=1)
    from_owner = positions // per_pair
    is_second = positions % per_pair == 1
    order = jnp.cumsum(is_second.astype(jnp.int32))
    most = DST_BLK // 2
    pick = is_second[None, :] & (order[None, :] == 1 + jnp.arange(most, dtype=jnp.int32)[:, None])
    places = jnp.sum(jnp.where(pick, jnp.arange(DST_BLK, dtype=jnp.int32)[None, :], 0), axis=1)
    second_owner = jnp.sum(jnp.where(pick, from_owner[None, :], 0), axis=1)
    second_weights = jnp.sum(jnp.where(pick, weights_here[None, :], 0.0), axis=1)

    if groups == 2:
        gram_part = lax.dynamic_slice_in_dim(gram_part, group * (PANEL // 2), PANEL // 2, 0)
    gram = pair_sum(gram_part, pairs[0])
    gram, from_owner, *sent = lax.optimization_barrier((gram, from_owner, *sent))
    for pair in pairs[1:-1]:
        gram = pair_sum(gram, pair)
    far = gather_pieces(gram, pairs[-1])
    near = trades(sent, pairs[0])

    arrived = select(received[:1], [(0, BLK)], from_owner).reshape(DST_BLK * BLK, feat)
    kern, panel, cs, csp = kernel_rows(
        share_parts(arrived), weights_here, panel_points, sparse_points
    )
    kern, far, near = lax.optimization_barrier((kern, far, near))
    gram = total(far)
    if groups == 2:
        other = lax.ppermute(gram, "cols", [(0, 1), (1, 0)])
        gram = jnp.where(
            group == 0, jnp.concatenate([gram, other], 0), jnp.concatenate([other, gram], 0)
        )
    g = total(near)
    for pair in pairs[1:]:
        sent = quarters(g, pair)
        if per_pair > 1 and pair == pairs[-1]:
            gram, last, received[0], *sent = lax.optimization_barrier(
                (gram, outgoing[1], received[0], *sent)
            )
        far = trades(sent, pair)
    if per_pair > 1:
        received.append(lax.all_to_all(last, "rows", split_axis=0, concat_axis=0, tiled=True))
    inverse = factor(gram)
    inverse, *far = lax.optimization_barrier((inverse, *far))
    rt = nt(total(far), inverse, HIGH).astype(jnp.bfloat16)
    for pair in pairs[:0:-1]:
        rt = gather_back(rt, pair)
    if per_pair > 1:
        rt, kern, second_owner = lax.optimization_barrier((rt, kern, second_owner))
    pieces = gather_pieces(rt, pairs[0])
    if per_pair > 1:
        late = select(received, [(BLK, HEAD), (0, BLK - HEAD)], second_owner)
        kern, panel = second_rows(
            share_parts(late.reshape(most * BLK, feat)),
            places,
            order[-1:],
            second_weights,
            panel_points,
            csp,
            sparse_points,
            cs,
            kern,
            panel,
        )
    kern, *pieces = lax.optimization_barrier((kern, *pieces))
    remainder, projected = remainder_rows(
        kern, panel, quarter_of(pairs[0])[None], inverse, jnp.stack(pieces), norm
    )
    return (projected, remainder)


def solution(mesh):
    return jax.shard_map(
        on_device,
        mesh=mesh,
        in_specs=(P("rows", "cols"), P("cols", None), P("rows"), P(), P()),
        out_specs=(P(None, "cols"), P("rows", "cols")),
        check_vma=False,
    )
```

```python
import functools
import math

import jax
import jax.numpy as jnp
from jax import lax
from jax.experimental import pallas as pl
from jax.experimental.pallas import tpu as pltpu
from jax.sharding import PartitionSpec as P

PANEL = 256
BLK = 128
DST_BLK = 13
EPSILON = 1e-06
VMEM_LIMIT = 56 * 1024 * 1024
HIGH = lax.Precision.HIGHEST
ANY = pl.BlockSpec(memory_space=pl.ANY)
VMEM = pl.BlockSpec(memory_space=pltpu.VMEM)
SMEM = pl.BlockSpec(memory_space=pltpu.SMEM)


def params(**kw):
    return pltpu.CompilerParams(vmem_limit_bytes=VMEM_LIMIT, **kw)


def cost(flops, nbytes):
    return pl.CostEstimate(flops=int(flops), bytes_accessed=int(nbytes), transcendentals=0)


def dot(a, b, ca, cb, precision=None):
    return lax.dot_general(
        a, b, (((ca,), (cb,)), ((), ())), preferred_element_type=jnp.float32, precision=precision
    )


def nt(a, b, precision=None):
    return dot(a, b, 1, 1, precision)


def nn(a, b, precision=None):
    return dot(a, b, 1, 0, precision)


def tn(a, b, precision=None):
    return dot(a, b, 0, 0, precision)


def split(x):
    high = x.astype(jnp.bfloat16)
    return high, (x - high.astype(jnp.float32)).astype(jnp.bfloat16)


HEAD = 48


def block_copies(rank, whole_ref, outer, first_ref, last_ref, sems):
    if rank == 0:
        pairs = [(whole_ref, first_ref.at[outer, pl.ds(0, BLK)])]
    else:
        pairs = [
            (whole_ref.at[pl.ds(0, HEAD)], first_ref.at[outer, pl.ds(BLK, HEAD)]),
            (whole_ref.at[pl.ds(HEAD, BLK - HEAD)], last_ref.at[outer]),
        ]
    return [(a, b, sems.at[i]) for i, (a, b) in enumerate(pairs)]


def pack_kernel(per_pair, dest_ref, cnt_ref, desc_ref, *refs):
    out_refs, (ctr_ref, rank_ref, sems) = refs[:per_pair], refs[per_pair:]
    slots = desc_ref.shape[0]
    owners = ctr_ref.shape[0]
    me = lax.axis_index("rows")
    count = cnt_ref[me]

    def copies(j, d, rank):
        moves = block_copies(rank, desc_ref.at[j], d, out_refs[0], out_refs[-1], sems.at[j])
        return [pltpu.make_async_copy(a, b, sem) for a, b, sem in moves]

    @pl.loop(0, owners)
    def _(i):
        ctr_ref[i] = 0

    @pl.loop(0, slots)
    def _(j):
        @pl.when(j < count)
        def _():
            d = dest_ref[me, j]
            rank = ctr_ref[d]
            ctr_ref[d] = rank + 1
            rank_ref[j] = rank
            for r in range(per_pair):
                @pl.when(rank == r)
                def _():
                    for c in copies(j, d, r):
                        c.start()

    @pl.loop(0, slots)
    def _(j):
        @pl.when(j < count)
        def _():
            for r in range(per_pair):
                @pl.when(rank_ref[j] == r)
                def _():
                    for c in copies(j, 0, r):
                        c.wait()


def pack(desc_blocks, destinations, counts, per_pair):
    slots, blk, feat = desc_blocks.shape
    owners = destinations.shape[0]
    heights = [blk] if per_pair == 1 else [blk + HEAD, blk - HEAD]
    return pl.pallas_call(
        functools.partial(pack_kernel, per_pair),
        out_shape=[
            jax.ShapeDtypeStruct((owners, h, feat), desc_blocks.dtype) for h in heights
        ],
        in_specs=[SMEM, SMEM, VMEM],
        out_specs=[ANY] * per_pair,
        scratch_shapes=[
            pltpu.SMEM((owners,), jnp.int32),
            pltpu.SMEM((slots,), jnp.int32),
            pltpu.SemaphoreType.DMA((slots, 2)),
        ],
        compiler_params=params(),
        cost_estimate=cost(0, 4 * slots * blk * feat),
        name="pack",
    )(destinations, counts, desc_blocks)


def select_kernel(per_pair, pos_ref, *refs):
    recv_refs, (out_ref, sems) = refs[:per_pair], refs[per_pair:]

    def copies(p, rank):
        owner = pos_ref[p] // per_pair
        moves = block_copies(rank, out_ref.at[p], owner, recv_refs[0], recv_refs[-1], sems.at[p])
        return [pltpu.make_async_copy(b, a, sem) for a, b, sem in moves]

    for act in ("start", "wait"):
        for p in range(DST_BLK):
            for r in range(per_pair):
                @pl.when(pos_ref[p] % per_pair == r)
                def _():
                    for c in copies(p, r):
                        getattr(c, act)()


def select(received, positions):
    feat = received[0].shape[-1]
    return pl.pallas_call(
        functools.partial(select_kernel, len(received)),
        out_shape=jax.ShapeDtypeStruct((DST_BLK, BLK, feat), received[0].dtype),
        in_specs=[SMEM] + [ANY] * len(received),
        out_specs=VMEM,
        scratch_shapes=[pltpu.SemaphoreType.DMA((DST_BLK, 2))],
        compiler_params=params(),
        cost_estimate=cost(0, 4 * DST_BLK * BLK * feat),
        name="select",
    )(positions, *received)


def small_factor(a):
    n = a.shape[0]
    row = lax.broadcasted_iota(jnp.int32, (n, 1), 0)
    eye = lax.broadcasted_iota(jnp.int32, (n, n), 0) == lax.broadcasted_iota(jnp.int32, (n, n), 1)
    m = jnp.concatenate([a, eye.astype(jnp.float32)], axis=1)
    out = []
    for j in range(0, n, 2):
        r0 = m[j : j + 1, :]
        r1 = m[j + 1 : j + 2, :]
        p = r0[:, j : j + 1]
        q = r0[:, j + 1 : j + 2]
        s = r1[:, j + 1 : j + 2]
        det = p * s - q * q
        out.append(r0[:, n:] * lax.rsqrt(p))
        out.append((r1[:, n:] - (q / p) * r0[:, n:]) * lax.rsqrt(det / p))
        if j + 2 < n:
            inv = 1.0 / det
            g0 = (s * r0 - q * r1) * inv
            g1 = (p * r1 - q * r0) * inv
            c0 = jnp.where(row > j + 1, m[:, j : j + 1], 0.0)
            c1 = jnp.where(row > j + 1, m[:, j + 1 : j + 2], 0.0)
            m = m - c0 * g0 - c1 * g1
    return out


def factor_kernel(leaf, gram_ref, x_ref, a_ref):
    n = gram_ref.shape[0]
    a_ref[...] = gram_ref[...]
    x_ref[...] = jnp.zeros_like(x_ref)
    for k in range(0, n, leaf):
        e = k + leaf
        for i, r in enumerate(small_factor(a_ref[k:e, k:e])):
            x_ref[k + i : k + i + 1, k:e] = r
        xk = x_ref[k:e, k:e]
        if e < n:
            t = nn(xk, a_ref[k:e, e:], HIGH)
            a_ref[k:e, e:] = t
            a_ref[e:, e:] -= tn(t, t, HIGH)
        if k > 0:
            x_ref[k:e, :k] = -nn(xk, tn(a_ref[:k, k:e], x_ref[:k, :k], HIGH), HIGH)


def factor(gram):
    n = gram.shape[0]
    return pl.pallas_call(
        functools.partial(factor_kernel, 64),
        out_shape=jax.ShapeDtypeStruct((n, n), jnp.float32),
        scratch_shapes=[pltpu.VMEM((n, n), jnp.float32)],
        compiler_params=params(),
        cost_estimate=cost(2e10, 8 * n * n),
        name="factor",
    )(gram)


def share_parts(x):
    groups = lax.axis_size("cols")
    if groups == 2:
        peer = lax.ppermute(x, "cols", [(0, 1), (1, 0)])
        return [x, peer]
    full = lax.all_gather(x, "cols", axis=0, tiled=False)
    return [full[i] for i in range(groups)]


def part_offset(i, feat):
    if lax.axis_size("cols") == 2:
        c = lax.axis_index("cols")
        return (c if i == 0 else 1 - c) * feat
    return i * feat


def join_copies(parts, x_ref, sems, spans):
    feat = parts[0].shape[1]
    return [
        [
            pltpu.make_async_copy(
                ref.at[pl.ds(start, size)],
                x_ref.at[pl.ds(start, size), pl.ds(pl.multiple_of(part_offset(i, feat), 128), feat)],
                sems.at[t, i],
            )
            for i, ref in enumerate(parts)
        ]
        for t, (start, size) in enumerate(spans)
    ]


def row_scale(x, weight):
    x = x.astype(jnp.float32)
    return weight / (jnp.sum(x * x, axis=1, keepdims=True) / x.shape[1] + EPSILON)


def column_scale(s):
    s = s.astype(jnp.float32)
    width = s.shape[1]
    scale = 1.0 / (width * (jnp.sum(s * s, axis=1, keepdims=True) / width + EPSILON))
    return jnp.broadcast_to(scale, (s.shape[0], 128)).T[:1, :]


def row_tiles(rows):
    blocks = rows // BLK
    per = 5 if blocks % 5 == 0 else 1
    return per, [(i * BLK, per * BLK) for i in range(0, blocks, per)]


def panel_kernel(nparts, cnt_ref, w_ref, *refs):
    parts = refs[:nparts]
    s_ref, moved_ref, gram_ref, pw_ref, sp_ref, x_ref, sems, sp_sem = refs[nparts:]
    per, tiles = row_tiles(x_ref.shape[0])
    count = cnt_ref[lax.axis_index("rows")]
    group = lax.axis_index("cols")
    own = pltpu.make_async_copy(s_ref.at[pl.ds(0, PANEL)], sp_ref, sp_sem)
    other = pltpu.make_async_copy(moved_ref, sp_ref, sp_sem)

    @pl.when(group == 0)
    def _():
        own.start()

    @pl.when(group != 0)
    def _():
        other.start()

    copies = join_copies(parts, x_ref, sems, tiles)
    for moves in copies:
        for c in moves:
            c.start()
    gram_ref[...] = jnp.zeros_like(gram_ref)
    pw_ref[...] = jnp.zeros_like(pw_ref)

    @pl.when(group == 0)
    def _():
        own.wait()

    @pl.when(group != 0)
    def _():
        other.wait()

    points = column_scale(sp_ref[...])
    for t, (start, size) in enumerate(tiles):
        for c in copies[t]:
            c.wait()

        @pl.when(t * per < count)
        def _():
            scales = []
            for b in range(per):
                j = t * per + b
                w = jnp.where(j < count, w_ref[j], 0.0)
                scales.append(row_scale(x_ref[j * BLK : (j + 1) * BLK, :], w))
            scale = jnp.concatenate(scales, axis=0)
            inner = nt(x_ref[start : start + size, :], sp_ref[...])
            panel = (inner * inner * scale * points).astype(jnp.bfloat16)
            gram_ref[...] += tn(panel, panel)
            pw_ref[start : start + size, :] = (panel.astype(jnp.float32) * scale).astype(
                jnp.bfloat16
            )


def panel_products(parts, counts, weights, s, moved):
    rows, feat = parts[0].shape
    width = s.shape[1]
    tiles = len(row_tiles(rows)[1])
    return pl.pallas_call(
        functools.partial(panel_kernel, len(parts)),
        out_shape=(
            jax.ShapeDtypeStruct((PANEL, PANEL), jnp.float32),
            jax.ShapeDtypeStruct((rows, PANEL), jnp.bfloat16),
            jax.ShapeDtypeStruct((PANEL, width), jnp.bfloat16),
        ),
        in_specs=[SMEM, SMEM] + [ANY] * (len(parts) + 2),
        out_specs=(VMEM, VMEM, VMEM),
        scratch_shapes=[
            pltpu.VMEM((rows, width), jnp.bfloat16),
            pltpu.SemaphoreType.DMA((tiles, len(parts))),
            pltpu.SemaphoreType.DMA,
        ],
        compiler_params=params(),
        cost_estimate=cost(2 * rows * PANEL * (width + PANEL), 2 * rows * width),
        name="panel_products",
    )(counts, weights, *parts, s, moved)


def column_kernel(nparts, *refs):
    parts = refs[:nparts]
    pw_ref, s_ref, g_ref, x_ref, sems = refs[nparts:]
    width = x_ref.shape[1]

    @pl.when(pl.program_id(0) == 0)
    def _():
        copies = join_copies(parts, x_ref, sems, row_tiles(x_ref.shape[0])[1])
        for group in copies:
            for c in group:
                c.start()
        for group in copies:
            for c in group:
                c.wait()

    s = s_ref[...]
    inner = nt(s, x_ref[...])
    products = nn((inner * inner).astype(jnp.bfloat16), pw_ref[...])
    wide = s.astype(jnp.float32)
    square = jnp.sum(wide * wide, axis=1, keepdims=True) / width + EPSILON
    g_ref[...] = products / (width * square)


def column_products(parts, pw, s):
    rows, feat = parts[0].shape
    size, width = s.shape
    chunk = min(512, size)
    tiles = len(row_tiles(rows)[1])
    once = pl.Buffered(1)
    return pl.pallas_call(
        functools.partial(column_kernel, len(parts)),
        grid=(size // chunk,),
        out_shape=jax.ShapeDtypeStruct((size, PANEL), jnp.float32),
        in_specs=[ANY] * len(parts)
        + [
            pl.BlockSpec((rows, PANEL), lambda i: (0, 0), pipeline_mode=once),
            pl.BlockSpec((chunk, width), lambda i: (i, 0)),
        ],
        out_specs=pl.BlockSpec((chunk, PANEL), lambda i: (i, 0)),
        scratch_shapes=[
            pltpu.VMEM((rows, width), jnp.bfloat16),
            pltpu.SemaphoreType.DMA((tiles, len(parts))),
        ],
        compiler_params=params(dimension_semantics=("arbitrary",)),
        cost_estimate=cost(2 * rows * (width + PANEL) * size, 2 * rows * width),
        name="column_products",
    )(*parts, pw, s)


def rows_kernel(nparts, w_ref, *refs):
    parts = refs[:nparts]
    sp_ref, s_ref, kern_ref, p_ref, x_ref, rs_ref, sems = refs[nparts:]
    rows_all = x_ref.shape[0]
    chunk = s_ref.shape[0]
    blocks = rows_all // BLK
    bounds = list(range(0, blocks, 7)) + [blocks]
    spans = [(a * BLK, b * BLK) for a, b in zip(bounds, bounds[1:])]

    @pl.when(pl.program_id(0) == 0)
    def _():
        copies = join_copies(parts, x_ref, sems, [(a, b - a) for a, b in spans])
        for moves in copies:
            for c in moves:
                c.start()
        points = column_scale(sp_ref[...])
        for (a, b), moves in zip(spans, copies):
            for c in moves:
                c.wait()
            for j in range(a // BLK, b // BLK):
                scale = row_scale(x_ref[j * BLK : (j + 1) * BLK, :], w_ref[j])
                rs_ref[j * BLK : (j + 1) * BLK, :] = jnp.broadcast_to(scale, (BLK, 128))
            inner = nt(x_ref[a:b, :], sp_ref[...])
            scale = jnp.concatenate([rs_ref[a:b, :]] * (PANEL // 128), axis=1)
            p_ref[a:b, :] = (inner * inner * scale * points).astype(jnp.bfloat16)

    columns = column_scale(s_ref[...])
    for a, b in spans:
        inner = nt(x_ref[a:b, :], s_ref[...])
        scale = jnp.concatenate([rs_ref[a:b, :]] * (chunk // 128), axis=1)
        kern_ref[a:b, :] = (inner * inner * scale * columns).astype(jnp.bfloat16)


def kernel_rows(parts, weights, sp, s):
    rows, feat = parts[0].shape
    cols, width = s.shape
    chunk = min(512, cols)
    once = pl.Buffered(1)
    return pl.pallas_call(
        functools.partial(rows_kernel, len(parts)),
        grid=(cols // chunk,),
        out_shape=(
            jax.ShapeDtypeStruct((rows, cols), jnp.bfloat16),
            jax.ShapeDtypeStruct((rows, PANEL), jnp.bfloat16),
        ),
        in_specs=[SMEM]
        + [ANY] * len(parts)
        + [
            pl.BlockSpec((PANEL, width), lambda i: (0, 0), pipeline_mode=once),
            pl.BlockSpec((chunk, width), lambda i: (i, 0)),
        ],
        out_specs=(
            pl.BlockSpec((rows, chunk), lambda i: (0, i)),
            pl.BlockSpec((rows, PANEL), lambda i: (0, 0)),
        ),
        scratch_shapes=[
            pltpu.VMEM((rows, width), jnp.bfloat16),
            pltpu.VMEM((rows, 128), jnp.float32),
            pltpu.SemaphoreType.DMA((2, len(parts))),
        ],
        compiler_params=params(dimension_semantics=("arbitrary",)),
        cost_estimate=cost(
            2 * rows * width * (cols + PANEL), 2 * rows * width + 2 * cols * width + 2 * rows * cols
        ),
        name="kernel_rows",
    )(weights, *parts, sp, s)


def remainder_kernel(norm, quarter_ref, kern_ref, p_ref, inv_ref, rt_ref, out_ref, proj_ref):
    chunk = kern_ref.shape[1]
    step = pl.program_id(0)
    inv_high, inv_low = split(inv_ref[...])
    rt = rt_ref[0]
    coef = (nn(rt, inv_high) + nn(rt, inv_low)).astype(jnp.bfloat16)
    proj_ref[...] = rt.astype(jnp.float32).T * (1.0 / norm)
    fit = nt(p_ref[...], coef)
    out_ref[...] = (kern_ref[...].astype(jnp.float32) - fit).astype(out_ref.dtype)

    part = min(chunk, PANEL)
    for i in range(PANEL // part):
        @pl.when((step == i) & (lax.axis_index("cols") == 0))
        def _():
            panel = p_ref[...]
            rows = slice(i * part, (i + 1) * part)
            basis = nt(panel, inv_high[rows, :]) + nt(panel, inv_low[rows, :])
            out_ref[:, :part] = (basis * norm).astype(out_ref.dtype)


def remainder_rows(kern, panel, quarter, inverse, rt, norm):
    rows, cols = kern.shape
    chunk = rt.shape[1]
    once = pl.Buffered(1)
    spec = pltpu.PrefetchScalarGridSpec(
        num_scalar_prefetch=1,
        grid=(cols // chunk,),
        in_specs=[
            pl.BlockSpec((rows, chunk), lambda i, q: (0, i)),
            pl.BlockSpec((rows, PANEL), lambda i, q: (0, 0), pipeline_mode=once),
            pl.BlockSpec((PANEL, PANEL), lambda i, q: (0, 0), pipeline_mode=once),
            pl.BlockSpec((1, chunk, PANEL), lambda i, q: (i ^ q[0], 0, 0)),
        ],
        out_specs=(
            pl.BlockSpec((rows, chunk), lambda i, q: (0, i)),
            pl.BlockSpec((PANEL, chunk), lambda i, q: (0, i)),
        ),
    )
    return pl.pallas_call(
        functools.partial(remainder_kernel, norm),
        grid_spec=spec,
        out_shape=(
            jax.ShapeDtypeStruct((rows, cols), jnp.bfloat16),
            jax.ShapeDtypeStruct((PANEL, cols), jnp.float32),
        ),
        compiler_params=params(dimension_semantics=("arbitrary",)),
        cost_estimate=cost(2 * rows * PANEL * cols, 4 * rows * cols),
        name="remainder_rows",
    )(quarter, kern, panel, inverse, rt)


def flips(bit, size):
    return [(i, i ^ bit) for i in range(size)]


def quarter_of(pair):
    me = lax.axis_index("rows").astype(jnp.int32)
    return (me // pair[0]) % 2 + 2 * ((me // pair[1]) % 2)


def trade(x, pair, k):
    bit = pair[0] * (k & 1) + pair[1] * (k >> 1)
    return lax.ppermute(x, "rows", flips(bit, lax.axis_size("rows")))


def scatter_sum(x, pair):
    n = x.shape[0] // 4
    q = quarter_of(pair)
    pieces = [lax.dynamic_slice_in_dim(x, (q ^ k) * n, n, 0) for k in range(4)]
    got = [pieces[0]] + [trade(pieces[k], pair, k) for k in range(1, 4)]
    return (got[0] + got[1]) + (got[2] + got[3])


def gather_pieces(x, pair):
    return [x] + [trade(x, pair, k) for k in range(1, 4)]


def gather_back(x, pair):
    n = x.shape[0]
    q = quarter_of(pair)
    pieces = gather_pieces(x, pair)
    return jnp.concatenate(
        [lax.select_n(q ^ i, *pieces) for i in range(4)], 0
    )


def pair_sum(x, pair):
    got = gather_pieces(x, pair)
    return (got[0] + got[1]) + (got[2] + got[3])


def on_device(descriptors, sparse_points, block_weights, block_counts, destinations):
    owners = lax.axis_size("rows")
    groups = lax.axis_size("cols")
    me = lax.axis_index("rows").astype(jnp.int32)
    group = lax.axis_index("cols").astype(jnp.int32)
    slots = block_weights.shape[0]
    per_pair = -(-slots // owners)
    feat = descriptors.shape[1]
    cols, width = sparse_points.shape
    norm = math.sqrt(owners * DST_BLK * BLK)
    pairs = [(1 << i, 2 << i) for i in range(0, owners.bit_length() - 1, 2)]

    first = sparse_points[:PANEL]
    source_parts = share_parts(descriptors)
    if groups == 2:
        moved = lax.ppermute(first, "cols", [(0, 1), (1, 0)])
    else:
        moved = lax.all_gather(first, "cols", axis=0, tiled=False)[0]
    desc_blocks = descriptors.reshape(slots, BLK, feat)
    outgoing = pack(desc_blocks, destinations, block_counts, per_pair)
    received = [lax.all_to_all(outgoing[0], "rows", split_axis=0, concat_axis=0, tiled=True)]

    weights32 = block_weights.astype(jnp.float32)
    gram_part, pw, panel_points = panel_products(
        source_parts, block_counts, weights32, sparse_points, moved
    )
    g = column_products(source_parts, pw, sparse_points)

    spare = -(-owners * slots // (PANEL * 8)) * 8
    table = lax.dynamic_update_slice(
        jnp.zeros((spare * PANEL,), jnp.float32), weights32, (me * slots,)
    ).reshape(spare, PANEL)
    if groups == 2:
        gram_part = lax.dynamic_slice_in_dim(gram_part, group * (PANEL // 2), PANEL // 2, 0)
    summed = pair_sum(jnp.concatenate([gram_part, table], 0), pairs[0])
    summed, g = lax.optimization_barrier((summed, g))
    for pair in pairs[1:]:
        summed = pair_sum(summed, pair)
    gram, table = summed[:-spare], summed[-spare:]
    if groups == 2:
        other = lax.ppermute(gram, "cols", [(0, 1), (1, 0)])
        gram = jnp.where(
            group == 0, jnp.concatenate([gram, other], 0), jnp.concatenate([other, gram], 0)
        )
    all_weights = table.reshape(-1)[: owners * slots]

    g = scatter_sum(g, pairs[0])
    if per_pair > 1:
        g, gram, last = lax.optimization_barrier((g, gram, outgoing[1]))
    for pair in pairs[1:]:
        g = scatter_sum(g, pair)
    if per_pair > 1:
        received.append(lax.all_to_all(last, "rows", split_axis=0, concat_axis=0, tiled=True))
    inverse = factor(gram)
    rt = nt(g, inverse, HIGH).astype(jnp.bfloat16)
    for pair in pairs[:0:-1]:
        rt = gather_back(rt, pair)

    slot_ids = jnp.arange(slots, dtype=jnp.int32)
    toward = ((slot_ids[None, :] < block_counts[:, None]) & (destinations == me)).astype(jnp.int32)
    rank = jnp.cumsum(toward, axis=1) - toward
    flat = toward.reshape(-1)
    place = jnp.cumsum(flat) - flat
    where_from = (jnp.arange(owners, dtype=jnp.int32)[:, None] * per_pair + rank).reshape(-1)
    hit = (flat[None, :] == 1) & (place[None, :] == jnp.arange(DST_BLK, dtype=jnp.int32)[:, None])
    positions = jnp.sum(jnp.where(hit, where_from[None, :], 0), axis=1)
    weights_here = jnp.sum(jnp.where(hit, all_weights[None, :], 0.0), axis=1)

    rt, positions = lax.optimization_barrier((rt, positions))
    arrived = select(received, positions).reshape(DST_BLK * BLK, feat)
    kern, panel = kernel_rows(share_parts(arrived), weights_here, panel_points, sparse_points)
    pieces = gather_pieces(rt, pairs[0])
    kern, *pieces = lax.optimization_barrier((kern, *pieces))
    rt = jnp.stack(pieces)
    remainder, projected = remainder_rows(
        kern, panel, quarter_of(pairs[0])[None], inverse, rt, norm
    )
    return (projected, remainder)


def solution(mesh):
    return jax.shard_map(
        on_device,
        mesh=mesh,
        in_specs=(P("rows", "cols"), P("cols", None), P("rows"), P(), P()),
        out_specs=(P(None, "cols"), P("rows", "cols")),
        check_vma=False,
    )
```

```python
import functools
import math

import jax
import jax.numpy as jnp
from jax import lax
from jax.experimental import pallas as pl
from jax.experimental.pallas import tpu as pltpu
from jax.sharding import PartitionSpec as P

PANEL = 256
BLK = 128
DST_BLK = 13
EPSILON = 1e-06
VMEM_LIMIT = 56 * 1024 * 1024
HIGH = lax.Precision.HIGHEST
ANY = pl.BlockSpec(memory_space=pl.ANY)
VMEM = pl.BlockSpec(memory_space=pltpu.VMEM)
SMEM = pl.BlockSpec(memory_space=pltpu.SMEM)


def params(**kw):
    return pltpu.CompilerParams(vmem_limit_bytes=VMEM_LIMIT, **kw)


def cost(flops, nbytes):
    return pl.CostEstimate(flops=int(flops), bytes_accessed=int(nbytes), transcendentals=0)


def dot(a, b, ca, cb, precision=None):
    return lax.dot_general(
        a, b, (((ca,), (cb,)), ((), ())), preferred_element_type=jnp.float32, precision=precision
    )


def nt(a, b, precision=None):
    return dot(a, b, 1, 1, precision)


def nn(a, b, precision=None):
    return dot(a, b, 1, 0, precision)


def tn(a, b, precision=None):
    return dot(a, b, 0, 0, precision)


def split(x):
    high = x.astype(jnp.bfloat16)
    return high, (x - high.astype(jnp.float32)).astype(jnp.bfloat16)


HEAD = 48


def block_copies(rank, whole_ref, outer, first_ref, last_ref, sems):
    if rank == 0:
        pairs = [(whole_ref, first_ref.at[outer, pl.ds(0, BLK)])]
    else:
        pairs = [
            (whole_ref.at[pl.ds(0, HEAD)], first_ref.at[outer, pl.ds(BLK, HEAD)]),
            (whole_ref.at[pl.ds(HEAD, BLK - HEAD)], last_ref.at[outer]),
        ]
    return [(a, b, sems.at[i]) for i, (a, b) in enumerate(pairs)]


def pack_kernel(per_pair, dest_ref, cnt_ref, desc_ref, *refs):
    out_refs, (ctr_ref, rank_ref, sems) = refs[:per_pair], refs[per_pair:]
    slots = desc_ref.shape[0]
    owners = ctr_ref.shape[0]
    me = lax.axis_index("rows")
    count = cnt_ref[me]

    def copies(j, d, rank):
        moves = block_copies(rank, desc_ref.at[j], d, out_refs[0], out_refs[-1], sems.at[j])
        return [pltpu.make_async_copy(a, b, sem) for a, b, sem in moves]

    @pl.loop(0, owners)
    def _(i):
        ctr_ref[i] = 0

    @pl.loop(0, slots)
    def _(j):
        @pl.when(j < count)
        def _():
            d = dest_ref[me, j]
            rank = ctr_ref[d]
            ctr_ref[d] = rank + 1
            rank_ref[j] = rank
            for r in range(per_pair):
                @pl.when(rank == r)
                def _():
                    for c in copies(j, d, r):
                        c.start()

    @pl.loop(0, slots)
    def _(j):
        @pl.when(j < count)
        def _():
            for r in range(per_pair):
                @pl.when(rank_ref[j] == r)
                def _():
                    for c in copies(j, 0, r):
                        c.wait()


def pack(desc_blocks, destinations, counts, per_pair):
    slots, blk, feat = desc_blocks.shape
    owners = destinations.shape[0]
    heights = [blk] if per_pair == 1 else [blk + HEAD, blk - HEAD]
    return pl.pallas_call(
        functools.partial(pack_kernel, per_pair),
        out_shape=[
            jax.ShapeDtypeStruct((owners, h, feat), desc_blocks.dtype) for h in heights
        ],
        in_specs=[SMEM, SMEM, VMEM],
        out_specs=[ANY] * per_pair,
        scratch_shapes=[
            pltpu.SMEM((owners,), jnp.int32),
            pltpu.SMEM((slots,), jnp.int32),
            pltpu.SemaphoreType.DMA((slots, 2)),
        ],
        compiler_params=params(),
        cost_estimate=cost(0, 4 * slots * blk * feat),
        name="pack",
    )(destinations, counts, desc_blocks)


def select_kernel(per_pair, pos_ref, *refs):
    recv_refs, (out_ref, sems) = refs[:per_pair], refs[per_pair:]

    def copies(p, rank):
        owner = pos_ref[p] // per_pair
        moves = block_copies(rank, out_ref.at[p], owner, recv_refs[0], recv_refs[-1], sems.at[p])
        return [pltpu.make_async_copy(b, a, sem) for a, b, sem in moves]

    for act in ("start", "wait"):
        for p in range(DST_BLK):
            for r in range(per_pair):
                @pl.when(pos_ref[p] % per_pair == r)
                def _():
                    for c in copies(p, r):
                        getattr(c, act)()


def select(received, positions):
    feat = received[0].shape[-1]
    return pl.pallas_call(
        functools.partial(select_kernel, len(received)),
        out_shape=jax.ShapeDtypeStruct((DST_BLK, BLK, feat), received[0].dtype),
        in_specs=[SMEM] + [ANY] * len(received),
        out_specs=VMEM,
        scratch_shapes=[pltpu.SemaphoreType.DMA((DST_BLK, 2))],
        compiler_params=params(),
        cost_estimate=cost(0, 4 * DST_BLK * BLK * feat),
        name="select",
    )(positions, *received)


def small_factor(a):
    n = a.shape[0]
    row = lax.broadcasted_iota(jnp.int32, (n, 1), 0)
    eye = lax.broadcasted_iota(jnp.int32, (n, n), 0) == lax.broadcasted_iota(jnp.int32, (n, n), 1)
    m = jnp.concatenate([a, eye.astype(jnp.float32)], axis=1)
    out = []
    for j in range(0, n, 2):
        r0 = m[j : j + 1, :]
        r1 = m[j + 1 : j + 2, :]
        p = r0[:, j : j + 1]
        q = r0[:, j + 1 : j + 2]
        s = r1[:, j + 1 : j + 2]
        det = p * s - q * q
        out.append(r0[:, n:] * lax.rsqrt(p))
        out.append((r1[:, n:] - (q / p) * r0[:, n:]) * lax.rsqrt(det / p))
        if j + 2 < n:
            inv = 1.0 / det
            g0 = (s * r0 - q * r1) * inv
            g1 = (p * r1 - q * r0) * inv
            c0 = jnp.where(row > j + 1, m[:, j : j + 1], 0.0)
            c1 = jnp.where(row > j + 1, m[:, j + 1 : j + 2], 0.0)
            m = m - c0 * g0 - c1 * g1
    return out


def factor_kernel(leaf, gram_ref, x_ref, a_ref):
    n = gram_ref.shape[0]
    a_ref[...] = gram_ref[...]
    x_ref[...] = jnp.zeros_like(x_ref)
    for k in range(0, n, leaf):
        e = k + leaf
        for i, r in enumerate(small_factor(a_ref[k:e, k:e])):
            x_ref[k + i : k + i + 1, k:e] = r
        xk = x_ref[k:e, k:e]
        if e < n:
            t = nn(xk, a_ref[k:e, e:], HIGH)
            a_ref[k:e, e:] = t
            a_ref[e:, e:] -= tn(t, t, HIGH)
        if k > 0:
            x_ref[k:e, :k] = -nn(xk, tn(a_ref[:k, k:e], x_ref[:k, :k], HIGH), HIGH)


def factor(gram):
    n = gram.shape[0]
    return pl.pallas_call(
        functools.partial(factor_kernel, 64),
        out_shape=jax.ShapeDtypeStruct((n, n), jnp.float32),
        scratch_shapes=[pltpu.VMEM((n, n), jnp.float32)],
        compiler_params=params(),
        cost_estimate=cost(2e10, 8 * n * n),
        name="factor",
    )(gram)


def share_parts(x):
    groups = lax.axis_size("cols")
    if groups == 2:
        peer = lax.ppermute(x, "cols", [(0, 1), (1, 0)])
        return [x, peer]
    full = lax.all_gather(x, "cols", axis=0, tiled=False)
    return [full[i] for i in range(groups)]


def part_offset(i, feat):
    if lax.axis_size("cols") == 2:
        c = lax.axis_index("cols")
        return (c if i == 0 else 1 - c) * feat
    return i * feat


def join_copies(parts, x_ref, sems, spans):
    feat = parts[0].shape[1]
    return [
        [
            pltpu.make_async_copy(
                ref.at[pl.ds(start, size)],
                x_ref.at[pl.ds(start, size), pl.ds(pl.multiple_of(part_offset(i, feat), 128), feat)],
                sems.at[t, i],
            )
            for i, ref in enumerate(parts)
        ]
        for t, (start, size) in enumerate(spans)
    ]


def row_scale(x, weight):
    x = x.astype(jnp.float32)
    return weight / (jnp.sum(x * x, axis=1, keepdims=True) / x.shape[1] + EPSILON)


def column_scale(s):
    s = s.astype(jnp.float32)
    width = s.shape[1]
    scale = 1.0 / (width * (jnp.sum(s * s, axis=1, keepdims=True) / width + EPSILON))
    return jnp.broadcast_to(scale, (s.shape[0], 128)).T[:1, :]


def row_tiles(rows):
    blocks = rows // BLK
    per = 5 if blocks % 5 == 0 else 1
    return per, [(i * BLK, per * BLK) for i in range(0, blocks, per)]


def panel_kernel(nparts, cnt_ref, w_ref, *refs):
    parts = refs[:nparts]
    s_ref, moved_ref, gram_ref, pw_ref, sp_ref, x_ref, sems, sp_sem = refs[nparts:]
    per, tiles = row_tiles(x_ref.shape[0])
    count = cnt_ref[lax.axis_index("rows")]
    group = lax.axis_index("cols")
    own = pltpu.make_async_copy(s_ref.at[pl.ds(0, PANEL)], sp_ref, sp_sem)
    other = pltpu.make_async_copy(moved_ref, sp_ref, sp_sem)

    @pl.when(group == 0)
    def _():
        own.start()

    @pl.when(group != 0)
    def _():
        other.start()

    copies = join_copies(parts, x_ref, sems, tiles)
    for moves in copies:
        for c in moves:
            c.start()
    gram_ref[...] = jnp.zeros_like(gram_ref)
    pw_ref[...] = jnp.zeros_like(pw_ref)

    @pl.when(group == 0)
    def _():
        own.wait()

    @pl.when(group != 0)
    def _():
        other.wait()

    points = column_scale(sp_ref[...])
    for t, (start, size) in enumerate(tiles):
        for c in copies[t]:
            c.wait()

        @pl.when(t * per < count)
        def _():
            scales = []
            for b in range(per):
                j = t * per + b
                w = jnp.where(j < count, w_ref[j], 0.0)
                scales.append(row_scale(x_ref[j * BLK : (j + 1) * BLK, :], w))
            scale = jnp.concatenate(scales, axis=0)
            inner = nt(x_ref[start : start + size, :], sp_ref[...])
            panel = (inner * inner * scale * points).astype(jnp.bfloat16)
            gram_ref[...] += tn(panel, panel)
            pw_ref[start : start + size, :] = (panel.astype(jnp.float32) * scale).astype(
                jnp.bfloat16
            )


def panel_products(parts, counts, weights, s, moved):
    rows, feat = parts[0].shape
    width = s.shape[1]
    tiles = len(row_tiles(rows)[1])
    return pl.pallas_call(
        functools.partial(panel_kernel, len(parts)),
        out_shape=(
            jax.ShapeDtypeStruct((PANEL, PANEL), jnp.float32),
            jax.ShapeDtypeStruct((rows, PANEL), jnp.bfloat16),
            jax.ShapeDtypeStruct((PANEL, width), jnp.bfloat16),
        ),
        in_specs=[SMEM, SMEM] + [ANY] * (len(parts) + 2),
        out_specs=(VMEM, VMEM, VMEM),
        scratch_shapes=[
            pltpu.VMEM((rows, width), jnp.bfloat16),
            pltpu.SemaphoreType.DMA((tiles, len(parts))),
            pltpu.SemaphoreType.DMA,
        ],
        compiler_params=params(),
        cost_estimate=cost(2 * rows * PANEL * (width + PANEL), 2 * rows * width),
        name="panel_products",
    )(counts, weights, *parts, s, moved)


def column_kernel(nparts, *refs):
    parts = refs[:nparts]
    pw_ref, s_ref, g_ref, x_ref, sems = refs[nparts:]
    width = x_ref.shape[1]

    @pl.when(pl.program_id(0) == 0)
    def _():
        copies = join_copies(parts, x_ref, sems, row_tiles(x_ref.shape[0])[1])
        for group in copies:
            for c in group:
                c.start()
        for group in copies:
            for c in group:
                c.wait()

    s = s_ref[...]
    inner = nt(s, x_ref[...])
    products = nn((inner * inner).astype(jnp.bfloat16), pw_ref[...])
    wide = s.astype(jnp.float32)
    square = jnp.sum(wide * wide, axis=1, keepdims=True) / width + EPSILON
    g_ref[...] = products / (width * square)


def column_products(parts, pw, s):
    rows, feat = parts[0].shape
    size, width = s.shape
    chunk = min(512, size)
    tiles = len(row_tiles(rows)[1])
    once = pl.Buffered(1)
    return pl.pallas_call(
        functools.partial(column_kernel, len(parts)),
        grid=(size // chunk,),
        out_shape=jax.ShapeDtypeStruct((size, PANEL), jnp.float32),
        in_specs=[ANY] * len(parts)
        + [
            pl.BlockSpec((rows, PANEL), lambda i: (0, 0), pipeline_mode=once),
            pl.BlockSpec((chunk, width), lambda i: (i, 0)),
        ],
        out_specs=pl.BlockSpec((chunk, PANEL), lambda i: (i, 0)),
        scratch_shapes=[
            pltpu.VMEM((rows, width), jnp.bfloat16),
            pltpu.SemaphoreType.DMA((tiles, len(parts))),
        ],
        compiler_params=params(dimension_semantics=("arbitrary",)),
        cost_estimate=cost(2 * rows * (width + PANEL) * size, 2 * rows * width),
        name="column_products",
    )(*parts, pw, s)


def rows_kernel(nparts, w_ref, *refs):
    parts = refs[:nparts]
    sp_ref, s_ref, kern_ref, p_ref, x_ref, rs_ref, sems = refs[nparts:]
    rows_all = x_ref.shape[0]
    chunk = s_ref.shape[0]
    blocks = rows_all // BLK
    bounds = list(range(0, blocks, 7)) + [blocks]
    spans = [(a * BLK, b * BLK) for a, b in zip(bounds, bounds[1:])]

    @pl.when(pl.program_id(0) == 0)
    def _():
        copies = join_copies(parts, x_ref, sems, [(a, b - a) for a, b in spans])
        for moves in copies:
            for c in moves:
                c.start()
        points = column_scale(sp_ref[...])
        for (a, b), moves in zip(spans, copies):
            for c in moves:
                c.wait()
            for j in range(a // BLK, b // BLK):
                scale = row_scale(x_ref[j * BLK : (j + 1) * BLK, :], w_ref[j])
                rs_ref[j * BLK : (j + 1) * BLK, :] = jnp.broadcast_to(scale, (BLK, 128))
            inner = nt(x_ref[a:b, :], sp_ref[...])
            scale = jnp.concatenate([rs_ref[a:b, :]] * (PANEL // 128), axis=1)
            p_ref[a:b, :] = (inner * inner * scale * points).astype(jnp.bfloat16)

    columns = column_scale(s_ref[...])
    for a, b in spans:
        inner = nt(x_ref[a:b, :], s_ref[...])
        scale = jnp.concatenate([rs_ref[a:b, :]] * (chunk // 128), axis=1)
        kern_ref[a:b, :] = (inner * inner * scale * columns).astype(jnp.bfloat16)


def kernel_rows(parts, weights, sp, s):
    rows, feat = parts[0].shape
    cols, width = s.shape
    chunk = min(512, cols)
    once = pl.Buffered(1)
    return pl.pallas_call(
        functools.partial(rows_kernel, len(parts)),
        grid=(cols // chunk,),
        out_shape=(
            jax.ShapeDtypeStruct((rows, cols), jnp.bfloat16),
            jax.ShapeDtypeStruct((rows, PANEL), jnp.bfloat16),
        ),
        in_specs=[SMEM]
        + [ANY] * len(parts)
        + [
            pl.BlockSpec((PANEL, width), lambda i: (0, 0), pipeline_mode=once),
            pl.BlockSpec((chunk, width), lambda i: (i, 0)),
        ],
        out_specs=(
            pl.BlockSpec((rows, chunk), lambda i: (0, i)),
            pl.BlockSpec((rows, PANEL), lambda i: (0, 0)),
        ),
        scratch_shapes=[
            pltpu.VMEM((rows, width), jnp.bfloat16),
            pltpu.VMEM((rows, 128), jnp.float32),
            pltpu.SemaphoreType.DMA((2, len(parts))),
        ],
        compiler_params=params(dimension_semantics=("arbitrary",)),
        cost_estimate=cost(
            2 * rows * width * (cols + PANEL), 2 * rows * width + 2 * cols * width + 2 * rows * cols
        ),
        name="kernel_rows",
    )(weights, *parts, sp, s)


def remainder_kernel(norm, quarter_ref, kern_ref, p_ref, inv_ref, rt_ref, out_ref, proj_ref):
    chunk = kern_ref.shape[1]
    step = pl.program_id(0)
    inv_high, inv_low = split(inv_ref[...])
    rt = rt_ref[0]
    coef = (nn(rt, inv_high) + nn(rt, inv_low)).astype(jnp.bfloat16)
    proj_ref[...] = rt.astype(jnp.float32).T * (1.0 / norm)
    fit = nt(p_ref[...], coef)
    out_ref[...] = (kern_ref[...].astype(jnp.float32) - fit).astype(out_ref.dtype)

    part = min(chunk, PANEL)
    for i in range(PANEL // part):
        @pl.when((step == i) & (lax.axis_index("cols") == 0))
        def _():
            panel = p_ref[...]
            rows = slice(i * part, (i + 1) * part)
            basis = nt(panel, inv_high[rows, :]) + nt(panel, inv_low[rows, :])
            out_ref[:, :part] = (basis * norm).astype(out_ref.dtype)


def remainder_rows(kern, panel, quarter, inverse, rt, norm):
    rows, cols = kern.shape
    chunk = rt.shape[1]
    once = pl.Buffered(1)
    spec = pltpu.PrefetchScalarGridSpec(
        num_scalar_prefetch=1,
        grid=(cols // chunk,),
        in_specs=[
            pl.BlockSpec((rows, chunk), lambda i, q: (0, i)),
            pl.BlockSpec((rows, PANEL), lambda i, q: (0, 0), pipeline_mode=once),
            pl.BlockSpec((PANEL, PANEL), lambda i, q: (0, 0), pipeline_mode=once),
            pl.BlockSpec((1, chunk, PANEL), lambda i, q: (i ^ q[0], 0, 0)),
        ],
        out_specs=(
            pl.BlockSpec((rows, chunk), lambda i, q: (0, i)),
            pl.BlockSpec((PANEL, chunk), lambda i, q: (0, i)),
        ),
    )
    return pl.pallas_call(
        functools.partial(remainder_kernel, norm),
        grid_spec=spec,
        out_shape=(
            jax.ShapeDtypeStruct((rows, cols), jnp.bfloat16),
            jax.ShapeDtypeStruct((PANEL, cols), jnp.float32),
        ),
        compiler_params=params(dimension_semantics=("arbitrary",)),
        cost_estimate=cost(2 * rows * PANEL * cols, 4 * rows * cols),
        name="remainder_rows",
    )(quarter, kern, panel, inverse, rt)


def flips(bit, size):
    return [(i, i ^ bit) for i in range(size)]


def quarter_of(pair):
    me = lax.axis_index("rows").astype(jnp.int32)
    return (me // pair[0]) % 2 + 2 * ((me // pair[1]) % 2)


def trade(x, pair, k):
    bit = pair[0] * (k & 1) + pair[1] * (k >> 1)
    return lax.ppermute(x, "rows", flips(bit, lax.axis_size("rows")))


def scatter_sum(x, pair):
    n = x.shape[0] // 4
    q = quarter_of(pair)
    pieces = [lax.dynamic_slice_in_dim(x, (q ^ k) * n, n, 0) for k in range(4)]
    got = [pieces[0]] + [trade(pieces[k], pair, k) for k in range(1, 4)]
    return (got[0] + got[1]) + (got[2] + got[3])


def gather_pieces(x, pair):
    return [x] + [trade(x, pair, k) for k in range(1, 4)]


def gather_back(x, pair):
    n = x.shape[0]
    q = quarter_of(pair)
    pieces = gather_pieces(x, pair)
    return jnp.concatenate(
        [lax.select_n(q ^ i, *pieces) for i in range(4)], 0
    )


def pair_sum(x, pair):
    got = gather_pieces(x, pair)
    return (got[0] + got[1]) + (got[2] + got[3])


def on_device(descriptors, sparse_points, block_weights, block_counts, destinations):
    owners = lax.axis_size("rows")
    groups = lax.axis_size("cols")
    me = lax.axis_index("rows").astype(jnp.int32)
    group = lax.axis_index("cols").astype(jnp.int32)
    slots = block_weights.shape[0]
    per_pair = -(-slots // owners)
    feat = descriptors.shape[1]
    cols, width = sparse_points.shape
    norm = math.sqrt(owners * DST_BLK * BLK)
    pairs = [(1 << i, 2 << i) for i in range(0, owners.bit_length() - 1, 2)]

    first = sparse_points[:PANEL]
    source_parts = share_parts(descriptors)
    if groups == 2:
        moved = lax.ppermute(first, "cols", [(0, 1), (1, 0)])
    else:
        moved = lax.all_gather(first, "cols", axis=0, tiled=False)[0]
    desc_blocks = descriptors.reshape(slots, BLK, feat)
    outgoing = pack(desc_blocks, destinations, block_counts, per_pair)
    received = [lax.all_to_all(outgoing[0], "rows", split_axis=0, concat_axis=0, tiled=True)]

    weights32 = block_weights.astype(jnp.float32)
    gram_part, pw, panel_points = panel_products(
        source_parts, block_counts, weights32, sparse_points, moved
    )
    g = column_products(source_parts, pw, sparse_points)

    spare = -(-owners * slots // (PANEL * 8)) * 8
    table = lax.dynamic_update_slice(
        jnp.zeros((spare * PANEL,), jnp.float32), weights32, (me * slots,)
    ).reshape(spare, PANEL)
    if groups == 2:
        gram_part = lax.dynamic_slice_in_dim(gram_part, group * (PANEL // 2), PANEL // 2, 0)
    summed = pair_sum(jnp.concatenate([gram_part, table], 0), pairs[0])
    summed, g = lax.optimization_barrier((summed, g))
    for pair in pairs[1:]:
        summed = pair_sum(summed, pair)
    gram, table = summed[:-spare], summed[-spare:]
    if groups == 2:
        other = lax.ppermute(gram, "cols", [(0, 1), (1, 0)])
        gram = jnp.where(
            group == 0, jnp.concatenate([gram, other], 0), jnp.concatenate([other, gram], 0)
        )
    all_weights = table.reshape(-1)[: owners * slots]

    g = scatter_sum(g, pairs[0])
    if per_pair > 1:
        g, gram, last = lax.optimization_barrier((g, gram, outgoing[1]))
    for pair in pairs[1:]:
        n = g.shape[0] // 4
        q = quarter_of(pair)
        far = [lax.dynamic_slice_in_dim(g, (q ^ k) * n, n, 0) for k in range(4)]
        far = [far[0]] + [trade(far[k], pair, k) for k in range(1, 4)]
        if pair != pairs[-1]:
            g = (far[0] + far[1]) + (far[2] + far[3])
    if per_pair > 1:
        received.append(lax.all_to_all(last, "rows", split_axis=0, concat_axis=0, tiled=True))
    inverse = factor(gram)

    slot_ids = jnp.arange(slots, dtype=jnp.int32)
    toward = ((slot_ids[None, :] < block_counts[:, None]) & (destinations == me)).astype(jnp.int32)
    rank = jnp.cumsum(toward, axis=1) - toward
    flat = toward.reshape(-1)
    place = jnp.cumsum(flat) - flat
    where_from = (jnp.arange(owners, dtype=jnp.int32)[:, None] * per_pair + rank).reshape(-1)
    hit = (flat[None, :] == 1) & (place[None, :] == jnp.arange(DST_BLK, dtype=jnp.int32)[:, None])
    positions = jnp.sum(jnp.where(hit, where_from[None, :], 0), axis=1)
    weights_here = jnp.sum(jnp.where(hit, all_weights[None, :], 0.0), axis=1)

    inverse, positions = lax.optimization_barrier((inverse, positions))
    arrived = select(received, positions).reshape(DST_BLK * BLK, feat)
    kern, panel = kernel_rows(share_parts(arrived), weights_here, panel_points, sparse_points)
    kern, *far = lax.optimization_barrier((kern, *far))
    g = (far[0] + far[1]) + (far[2] + far[3])
    rt = nt(g, inverse, HIGH).astype(jnp.bfloat16)
    for pair in pairs[:0:-1]:
        rt = gather_back(rt, pair)
    pieces = gather_pieces(rt, pairs[0])
    kern, *pieces = lax.optimization_barrier((kern, *pieces))
    rt = jnp.stack(pieces)
    remainder, projected = remainder_rows(
        kern, panel, quarter_of(pairs[0])[None], inverse, rt, norm
    )
    return (projected, remainder)


def solution(mesh):
    return jax.shard_map(
        on_device,
        mesh=mesh,
        in_specs=(P("rows", "cols"), P("cols", None), P("rows"), P(), P()),
        out_specs=(P(None, "cols"), P("rows", "cols")),
        check_vma=False,
    )
```

```python
import functools
import math

import jax
import jax.numpy as jnp
from jax import lax
from jax.experimental import pallas as pl
from jax.experimental.pallas import tpu as pltpu
from jax.sharding import PartitionSpec as P

PANEL = 256
BLK = 128
DST_BLK = 13
EPSILON = 1e-06
VMEM_LIMIT = 56 * 1024 * 1024
HIGH = lax.Precision.HIGHEST
ANY = pl.BlockSpec(memory_space=pl.ANY)
VMEM = pl.BlockSpec(memory_space=pltpu.VMEM)
SMEM = pl.BlockSpec(memory_space=pltpu.SMEM)


def params(**kw):
    return pltpu.CompilerParams(vmem_limit_bytes=VMEM_LIMIT, **kw)


def cost(flops, nbytes):
    return pl.CostEstimate(flops=int(flops), bytes_accessed=int(nbytes), transcendentals=0)


def dot(a, b, ca, cb, precision=None):
    return lax.dot_general(
        a, b, (((ca,), (cb,)), ((), ())), preferred_element_type=jnp.float32, precision=precision
    )


def nt(a, b, precision=None):
    return dot(a, b, 1, 1, precision)


def nn(a, b, precision=None):
    return dot(a, b, 1, 0, precision)


def tn(a, b, precision=None):
    return dot(a, b, 0, 0, precision)


def split(x):
    high = x.astype(jnp.bfloat16)
    return high, (x - high.astype(jnp.float32)).astype(jnp.bfloat16)


HEAD = 48


def block_copies(rank, whole_ref, outer, first_ref, last_ref, sems):
    if rank == 0:
        pairs = [(whole_ref, first_ref.at[outer, pl.ds(0, BLK)])]
    else:
        pairs = [
            (whole_ref.at[pl.ds(0, HEAD)], first_ref.at[outer, pl.ds(BLK, HEAD)]),
            (whole_ref.at[pl.ds(HEAD, BLK - HEAD)], last_ref.at[outer]),
        ]
    return [(a, b, sems.at[i]) for i, (a, b) in enumerate(pairs)]


def pack_kernel(per_pair, dest_ref, cnt_ref, desc_ref, *refs):
    out_refs, (ctr_ref, rank_ref, sems) = refs[:per_pair], refs[per_pair:]
    slots = desc_ref.shape[0]
    owners = ctr_ref.shape[0]
    me = lax.axis_index("rows")
    count = cnt_ref[me]

    def copies(j, d, rank):
        moves = block_copies(rank, desc_ref.at[j], d, out_refs[0], out_refs[-1], sems.at[j])
        return [pltpu.make_async_copy(a, b, sem) for a, b, sem in moves]

    @pl.loop(0, owners)
    def _(i):
        ctr_ref[i] = 0

    @pl.loop(0, slots)
    def _(j):
        @pl.when(j < count)
        def _():
            d = dest_ref[me, j]
            rank = ctr_ref[d]
            ctr_ref[d] = rank + 1
            rank_ref[j] = rank
            for r in range(per_pair):
                @pl.when(rank == r)
                def _():
                    for c in copies(j, d, r):
                        c.start()

    @pl.loop(0, slots)
    def _(j):
        @pl.when(j < count)
        def _():
            for r in range(per_pair):
                @pl.when(rank_ref[j] == r)
                def _():
                    for c in copies(j, 0, r):
                        c.wait()


def pack(desc_blocks, destinations, counts, per_pair):
    slots, blk, feat = desc_blocks.shape
    owners = destinations.shape[0]
    heights = [blk] if per_pair == 1 else [blk + HEAD, blk - HEAD]
    return pl.pallas_call(
        functools.partial(pack_kernel, per_pair),
        out_shape=[
            jax.ShapeDtypeStruct((owners, h, feat), desc_blocks.dtype) for h in heights
        ],
        in_specs=[SMEM, SMEM, VMEM],
        out_specs=[ANY] * per_pair,
        scratch_shapes=[
            pltpu.SMEM((owners,), jnp.int32),
            pltpu.SMEM((slots,), jnp.int32),
            pltpu.SemaphoreType.DMA((slots, 2)),
        ],
        compiler_params=params(),
        cost_estimate=cost(0, 4 * slots * blk * feat),
        name="pack",
    )(destinations, counts, desc_blocks)


def select_kernel(per_pair, pos_ref, *refs):
    recv_refs, (out_ref, sems) = refs[:per_pair], refs[per_pair:]

    def copies(p, rank):
        owner = pos_ref[p] // per_pair
        moves = block_copies(rank, out_ref.at[p], owner, recv_refs[0], recv_refs[-1], sems.at[p])
        return [pltpu.make_async_copy(b, a, sem) for a, b, sem in moves]

    for act in ("start", "wait"):
        for p in range(DST_BLK):
            for r in range(per_pair):
                @pl.when(pos_ref[p] % per_pair == r)
                def _():
                    for c in copies(p, r):
                        getattr(c, act)()


def select(received, positions):
    feat = received[0].shape[-1]
    return pl.pallas_call(
        functools.partial(select_kernel, len(received)),
        out_shape=jax.ShapeDtypeStruct((DST_BLK, BLK, feat), received[0].dtype),
        in_specs=[SMEM] + [ANY] * len(received),
        out_specs=VMEM,
        scratch_shapes=[pltpu.SemaphoreType.DMA((DST_BLK, 2))],
        compiler_params=params(),
        cost_estimate=cost(0, 4 * DST_BLK * BLK * feat),
        name="select",
    )(positions, *received)


def small_factor(a):
    n = a.shape[0]
    row = lax.broadcasted_iota(jnp.int32, (n, 1), 0)
    eye = lax.broadcasted_iota(jnp.int32, (n, n), 0) == lax.broadcasted_iota(jnp.int32, (n, n), 1)
    m = jnp.concatenate([a, eye.astype(jnp.float32)], axis=1)
    out = []
    for j in range(0, n, 2):
        r0 = m[j : j + 1, :]
        r1 = m[j + 1 : j + 2, :]
        p = r0[:, j : j + 1]
        q = r0[:, j + 1 : j + 2]
        s = r1[:, j + 1 : j + 2]
        det = p * s - q * q
        out.append(r0[:, n:] * lax.rsqrt(p))
        out.append((r1[:, n:] - (q / p) * r0[:, n:]) * lax.rsqrt(det / p))
        if j + 2 < n:
            inv = 1.0 / det
            g0 = (s * r0 - q * r1) * inv
            g1 = (p * r1 - q * r0) * inv
            c0 = jnp.where(row > j + 1, m[:, j : j + 1], 0.0)
            c1 = jnp.where(row > j + 1, m[:, j + 1 : j + 2], 0.0)
            m = m - c0 * g0 - c1 * g1
    return out


def factor_kernel(leaf, gram_ref, x_ref, a_ref):
    n = gram_ref.shape[0]
    a_ref[...] = gram_ref[...]
    x_ref[...] = jnp.zeros_like(x_ref)
    for k in range(0, n, leaf):
        e = k + leaf
        for i, r in enumerate(small_factor(a_ref[k:e, k:e])):
            x_ref[k + i : k + i + 1, k:e] = r
        xk = x_ref[k:e, k:e]
        if e < n:
            t = nn(xk, a_ref[k:e, e:], HIGH)
            a_ref[k:e, e:] = t
            a_ref[e:, e:] -= tn(t, t, HIGH)
        if k > 0:
            x_ref[k:e, :k] = -nn(xk, tn(a_ref[:k, k:e], x_ref[:k, :k], HIGH), HIGH)


def factor(gram):
    n = gram.shape[0]
    return pl.pallas_call(
        functools.partial(factor_kernel, 64),
        out_shape=jax.ShapeDtypeStruct((n, n), jnp.float32),
        scratch_shapes=[pltpu.VMEM((n, n), jnp.float32)],
        compiler_params=params(),
        cost_estimate=cost(2e10, 8 * n * n),
        name="factor",
    )(gram)


def share_parts(x):
    groups = lax.axis_size("cols")
    if groups == 2:
        peer = lax.ppermute(x, "cols", [(0, 1), (1, 0)])
        return [x, peer]
    full = lax.all_gather(x, "cols", axis=0, tiled=False)
    return [full[i] for i in range(groups)]


def part_offset(i, feat):
    if lax.axis_size("cols") == 2:
        c = lax.axis_index("cols")
        return (c if i == 0 else 1 - c) * feat
    return i * feat


def join_copies(parts, x_ref, sems, spans):
    feat = parts[0].shape[1]
    return [
        [
            pltpu.make_async_copy(
                ref.at[pl.ds(start, size)],
                x_ref.at[pl.ds(start, size), pl.ds(pl.multiple_of(part_offset(i, feat), 128), feat)],
                sems.at[t, i],
            )
            for i, ref in enumerate(parts)
        ]
        for t, (start, size) in enumerate(spans)
    ]


def row_scale(x, weight):
    x = x.astype(jnp.float32)
    return weight / (jnp.sum(x * x, axis=1, keepdims=True) / x.shape[1] + EPSILON)


def column_scale(s):
    s = s.astype(jnp.float32)
    width = s.shape[1]
    scale = 1.0 / (width * (jnp.sum(s * s, axis=1, keepdims=True) / width + EPSILON))
    return jnp.broadcast_to(scale, (s.shape[0], 128)).T[:1, :]


def row_tiles(rows):
    blocks = rows // BLK
    per = 5 if blocks % 5 == 0 else 1
    return per, [(i * BLK, per * BLK) for i in range(0, blocks, per)]


def panel_kernel(nparts, cnt_ref, w_ref, *refs):
    parts = refs[:nparts]
    s_ref, moved_ref, gram_ref, pw_ref, sp_ref, x_ref, sems, sp_sem = refs[nparts:]
    per, tiles = row_tiles(x_ref.shape[0])
    count = cnt_ref[lax.axis_index("rows")]
    group = lax.axis_index("cols")
    own = pltpu.make_async_copy(s_ref.at[pl.ds(0, PANEL)], sp_ref, sp_sem)
    other = pltpu.make_async_copy(moved_ref, sp_ref, sp_sem)

    @pl.when(group == 0)
    def _():
        own.start()

    @pl.when(group != 0)
    def _():
        other.start()

    copies = join_copies(parts, x_ref, sems, tiles)
    for moves in copies:
        for c in moves:
            c.start()
    gram_ref[...] = jnp.zeros_like(gram_ref)
    pw_ref[...] = jnp.zeros_like(pw_ref)

    @pl.when(group == 0)
    def _():
        own.wait()

    @pl.when(group != 0)
    def _():
        other.wait()

    points = column_scale(sp_ref[...])
    for t, (start, size) in enumerate(tiles):
        for c in copies[t]:
            c.wait()

        @pl.when(t * per < count)
        def _():
            scales = []
            for b in range(per):
                j = t * per + b
                w = jnp.where(j < count, w_ref[j], 0.0)
                scales.append(row_scale(x_ref[j * BLK : (j + 1) * BLK, :], w))
            scale = jnp.concatenate(scales, axis=0)
            inner = nt(x_ref[start : start + size, :], sp_ref[...])
            panel = (inner * inner * scale * points).astype(jnp.bfloat16)
            gram_ref[...] += tn(panel, panel)
            pw_ref[start : start + size, :] = (panel.astype(jnp.float32) * scale).astype(
                jnp.bfloat16
            )


def panel_products(parts, counts, weights, s, moved):
    rows, feat = parts[0].shape
    width = s.shape[1]
    tiles = len(row_tiles(rows)[1])
    return pl.pallas_call(
        functools.partial(panel_kernel, len(parts)),
        out_shape=(
            jax.ShapeDtypeStruct((PANEL, PANEL), jnp.float32),
            jax.ShapeDtypeStruct((rows, PANEL), jnp.bfloat16),
            jax.ShapeDtypeStruct((PANEL, width), jnp.bfloat16),
        ),
        in_specs=[SMEM, SMEM] + [ANY] * (len(parts) + 2),
        out_specs=(VMEM, VMEM, VMEM),
        scratch_shapes=[
            pltpu.VMEM((rows, width), jnp.bfloat16),
            pltpu.SemaphoreType.DMA((tiles, len(parts))),
            pltpu.SemaphoreType.DMA,
        ],
        compiler_params=params(),
        cost_estimate=cost(2 * rows * PANEL * (width + PANEL), 2 * rows * width),
        name="panel_products",
    )(counts, weights, *parts, s, moved)


def column_kernel(nparts, *refs):
    parts = refs[:nparts]
    pw_ref, s_ref, g_ref, x_ref, sems = refs[nparts:]
    width = x_ref.shape[1]

    @pl.when(pl.program_id(0) == 0)
    def _():
        copies = join_copies(parts, x_ref, sems, row_tiles(x_ref.shape[0])[1])
        for group in copies:
            for c in group:
                c.start()
        for group in copies:
            for c in group:
                c.wait()

    s = s_ref[...]
    inner = nt(s, x_ref[...])
    products = nn((inner * inner).astype(jnp.bfloat16), pw_ref[...])
    wide = s.astype(jnp.float32)
    square = jnp.sum(wide * wide, axis=1, keepdims=True) / width + EPSILON
    g_ref[...] = products / (width * square)


def column_products(parts, pw, s):
    rows, feat = parts[0].shape
    size, width = s.shape
    chunk = min(512, size)
    tiles = len(row_tiles(rows)[1])
    once = pl.Buffered(1)
    return pl.pallas_call(
        functools.partial(column_kernel, len(parts)),
        grid=(size // chunk,),
        out_shape=jax.ShapeDtypeStruct((size, PANEL), jnp.float32),
        in_specs=[ANY] * len(parts)
        + [
            pl.BlockSpec((rows, PANEL), lambda i: (0, 0), pipeline_mode=once),
            pl.BlockSpec((chunk, width), lambda i: (i, 0)),
        ],
        out_specs=pl.BlockSpec((chunk, PANEL), lambda i: (i, 0)),
        scratch_shapes=[
            pltpu.VMEM((rows, width), jnp.bfloat16),
            pltpu.SemaphoreType.DMA((tiles, len(parts))),
        ],
        compiler_params=params(dimension_semantics=("arbitrary",)),
        cost_estimate=cost(2 * rows * (width + PANEL) * size, 2 * rows * width),
        name="column_products",
    )(*parts, pw, s)


def rows_kernel(nparts, w_ref, *refs):
    parts = refs[:nparts]
    sp_ref, s_ref, kern_ref, p_ref, x_ref, rs_ref, sems = refs[nparts:]
    rows_all = x_ref.shape[0]
    chunk = s_ref.shape[0]
    blocks = rows_all // BLK
    bounds = list(range(0, blocks, 7)) + [blocks]
    spans = [(a * BLK, b * BLK) for a, b in zip(bounds, bounds[1:])]

    @pl.when(pl.program_id(0) == 0)
    def _():
        copies = join_copies(parts, x_ref, sems, [(a, b - a) for a, b in spans])
        for moves in copies:
            for c in moves:
                c.start()
        points = column_scale(sp_ref[...])
        for (a, b), moves in zip(spans, copies):
            for c in moves:
                c.wait()
            for j in range(a // BLK, b // BLK):
                scale = row_scale(x_ref[j * BLK : (j + 1) * BLK, :], w_ref[j])
                rs_ref[j * BLK : (j + 1) * BLK, :] = jnp.broadcast_to(scale, (BLK, 128))
            inner = nt(x_ref[a:b, :], sp_ref[...])
            scale = jnp.concatenate([rs_ref[a:b, :]] * (PANEL // 128), axis=1)
            p_ref[a:b, :] = (inner * inner * scale * points).astype(jnp.bfloat16)

    columns = column_scale(s_ref[...])
    for a, b in spans:
        inner = nt(x_ref[a:b, :], s_ref[...])
        scale = jnp.concatenate([rs_ref[a:b, :]] * (chunk // 128), axis=1)
        kern_ref[a:b, :] = (inner * inner * scale * columns).astype(jnp.bfloat16)


def kernel_rows(parts, weights, sp, s):
    rows, feat = parts[0].shape
    cols, width = s.shape
    chunk = min(512, cols)
    once = pl.Buffered(1)
    return pl.pallas_call(
        functools.partial(rows_kernel, len(parts)),
        grid=(cols // chunk,),
        out_shape=(
            jax.ShapeDtypeStruct((rows, cols), jnp.bfloat16),
            jax.ShapeDtypeStruct((rows, PANEL), jnp.bfloat16),
        ),
        in_specs=[SMEM]
        + [ANY] * len(parts)
        + [
            pl.BlockSpec((PANEL, width), lambda i: (0, 0), pipeline_mode=once),
            pl.BlockSpec((chunk, width), lambda i: (i, 0)),
        ],
        out_specs=(
            pl.BlockSpec((rows, chunk), lambda i: (0, i)),
            pl.BlockSpec((rows, PANEL), lambda i: (0, 0)),
        ),
        scratch_shapes=[
            pltpu.VMEM((rows, width), jnp.bfloat16),
            pltpu.VMEM((rows, 128), jnp.float32),
            pltpu.SemaphoreType.DMA((2, len(parts))),
        ],
        compiler_params=params(dimension_semantics=("arbitrary",)),
        cost_estimate=cost(
            2 * rows * width * (cols + PANEL), 2 * rows * width + 2 * cols * width + 2 * rows * cols
        ),
        name="kernel_rows",
    )(weights, *parts, sp, s)


def remainder_kernel(norm, quarter_ref, kern_ref, p_ref, inv_ref, *refs):
    pieces, (out_ref, proj_ref, rt_ref) = refs[:4], refs[4:]
    chunk = kern_ref.shape[1]
    step = pl.program_id(0)
    inv_high, inv_low = split(inv_ref[...])
    for k in range(4):
        @pl.when((step ^ quarter_ref[0]) == k)
        def _():
            rt_ref[...] = pieces[k][...]

    rt = rt_ref[...]
    coef = (nn(rt, inv_high) + nn(rt, inv_low)).astype(jnp.bfloat16)
    proj_ref[...] = rt.astype(jnp.float32).T * (1.0 / norm)
    fit = nt(p_ref[...], coef)
    out_ref[...] = (kern_ref[...].astype(jnp.float32) - fit).astype(out_ref.dtype)

    part = min(chunk, PANEL)
    for i in range(PANEL // part):
        @pl.when((step == i) & (lax.axis_index("cols") == 0))
        def _():
            panel = p_ref[...]
            rows = slice(i * part, (i + 1) * part)
            basis = nt(panel, inv_high[rows, :]) + nt(panel, inv_low[rows, :])
            out_ref[:, :part] = (basis * norm).astype(out_ref.dtype)


def remainder_rows(kern, panel, quarter, inverse, pieces, norm):
    rows, cols = kern.shape
    chunk = pieces[0].shape[0]
    once = pl.Buffered(1)
    spec = pltpu.PrefetchScalarGridSpec(
        num_scalar_prefetch=1,
        grid=(cols // chunk,),
        in_specs=[
            pl.BlockSpec((rows, chunk), lambda i, q: (0, i)),
            pl.BlockSpec((rows, PANEL), lambda i, q: (0, 0), pipeline_mode=once),
            pl.BlockSpec((PANEL, PANEL), lambda i, q: (0, 0), pipeline_mode=once),
        ]
        + [pl.BlockSpec((chunk, PANEL), lambda i, q: (0, 0), pipeline_mode=once)] * 4,
        out_specs=(
            pl.BlockSpec((rows, chunk), lambda i, q: (0, i)),
            pl.BlockSpec((PANEL, chunk), lambda i, q: (0, i)),
        ),
        scratch_shapes=[pltpu.VMEM((chunk, PANEL), jnp.bfloat16)],
    )
    return pl.pallas_call(
        functools.partial(remainder_kernel, norm),
        grid_spec=spec,
        out_shape=(
            jax.ShapeDtypeStruct((rows, cols), jnp.bfloat16),
            jax.ShapeDtypeStruct((PANEL, cols), jnp.float32),
        ),
        compiler_params=params(dimension_semantics=("arbitrary",)),
        cost_estimate=cost(2 * rows * PANEL * cols, 4 * rows * cols),
        name="remainder_rows",
    )(quarter, kern, panel, inverse, *pieces)


def flips(bit, size):
    return [(i, i ^ bit) for i in range(size)]


def quarter_of(pair):
    me = lax.axis_index("rows").astype(jnp.int32)
    return (me // pair[0]) % 2 + 2 * ((me // pair[1]) % 2)


def trade(x, pair, k):
    bit = pair[0] * (k & 1) + pair[1] * (k >> 1)
    return lax.ppermute(x, "rows", flips(bit, lax.axis_size("rows")))


def scatter_sum(x, pair):
    n = x.shape[0] // 4
    q = quarter_of(pair)
    pieces = [lax.dynamic_slice_in_dim(x, (q ^ k) * n, n, 0) for k in range(4)]
    got = [pieces[0]] + [trade(pieces[k], pair, k) for k in range(1, 4)]
    return (got[0] + got[1]) + (got[2] + got[3])


def gather_pieces(x, pair):
    return [x] + [trade(x, pair, k) for k in range(1, 4)]


def gather_back(x, pair):
    n = x.shape[0]
    q = quarter_of(pair)
    pieces = gather_pieces(x, pair)
    return jnp.concatenate(
        [lax.select_n(q ^ i, *pieces) for i in range(4)], 0
    )


def pair_sum(x, pair):
    got = gather_pieces(x, pair)
    return (got[0] + got[1]) + (got[2] + got[3])


def on_device(descriptors, sparse_points, block_weights, block_counts, destinations):
    owners = lax.axis_size("rows")
    groups = lax.axis_size("cols")
    me = lax.axis_index("rows").astype(jnp.int32)
    group = lax.axis_index("cols").astype(jnp.int32)
    slots = block_weights.shape[0]
    per_pair = -(-slots // owners)
    feat = descriptors.shape[1]
    cols, width = sparse_points.shape
    norm = math.sqrt(owners * DST_BLK * BLK)
    pairs = [(1 << i, 2 << i) for i in range(0, owners.bit_length() - 1, 2)]

    first = sparse_points[:PANEL]
    source_parts = share_parts(descriptors)
    if groups == 2:
        moved = lax.ppermute(first, "cols", [(0, 1), (1, 0)])
    else:
        moved = lax.all_gather(first, "cols", axis=0, tiled=False)[0]
    desc_blocks = descriptors.reshape(slots, BLK, feat)
    outgoing = pack(desc_blocks, destinations, block_counts, per_pair)
    received = [lax.all_to_all(outgoing[0], "rows", split_axis=0, concat_axis=0, tiled=True)]

    weights32 = block_weights.astype(jnp.float32)
    gram_part, pw, panel_points = panel_products(
        source_parts, block_counts, weights32, sparse_points, moved
    )
    g = column_products(source_parts, pw, sparse_points)

    spare = -(-owners * slots // (PANEL * 8)) * 8
    table = lax.dynamic_update_slice(
        jnp.zeros((spare * PANEL,), jnp.float32), weights32, (me * slots,)
    ).reshape(spare, PANEL)
    if groups == 2:
        gram_part = lax.dynamic_slice_in_dim(gram_part, group * (PANEL // 2), PANEL // 2, 0)
    summed = pair_sum(jnp.concatenate([gram_part, table], 0), pairs[0])
    summed, g = lax.optimization_barrier((summed, g))
    for pair in pairs[1:]:
        summed = pair_sum(summed, pair)
    gram, table = summed[:-spare], summed[-spare:]
    if groups == 2:
        other = lax.ppermute(gram, "cols", [(0, 1), (1, 0)])
        gram = jnp.where(
            group == 0, jnp.concatenate([gram, other], 0), jnp.concatenate([other, gram], 0)
        )
    all_weights = table.reshape(-1)[: owners * slots]

    g = scatter_sum(g, pairs[0])
    if per_pair > 1:
        g, gram, last = lax.optimization_barrier((g, gram, outgoing[1]))
    for pair in pairs[1:]:
        g = scatter_sum(g, pair)
    if per_pair > 1:
        received.append(lax.all_to_all(last, "rows", split_axis=0, concat_axis=0, tiled=True))
    inverse = factor(gram)
    rt = nt(g, inverse, HIGH).astype(jnp.bfloat16)
    for pair in pairs[:0:-1]:
        rt = gather_back(rt, pair)

    slot_ids = jnp.arange(slots, dtype=jnp.int32)
    toward = ((slot_ids[None, :] < block_counts[:, None]) & (destinations == me)).astype(jnp.int32)
    rank = jnp.cumsum(toward, axis=1) - toward
    flat = toward.reshape(-1)
    place = jnp.cumsum(flat) - flat
    where_from = (jnp.arange(owners, dtype=jnp.int32)[:, None] * per_pair + rank).reshape(-1)
    hit = (flat[None, :] == 1) & (place[None, :] == jnp.arange(DST_BLK, dtype=jnp.int32)[:, None])
    positions = jnp.sum(jnp.where(hit, where_from[None, :], 0), axis=1)
    weights_here = jnp.sum(jnp.where(hit, all_weights[None, :], 0.0), axis=1)

    rt, positions = lax.optimization_barrier((rt, positions))
    arrived = select(received, positions).reshape(DST_BLK * BLK, feat)
    kern, panel = kernel_rows(share_parts(arrived), weights_here, panel_points, sparse_points)
    pieces = gather_pieces(rt, pairs[0])
    kern, *pieces = lax.optimization_barrier((kern, *pieces))
    remainder, projected = remainder_rows(
        kern, panel, quarter_of(pairs[0])[None], inverse, pieces, norm
    )
    return (projected, remainder)


def solution(mesh):
    return jax.shard_map(
        on_device,
        mesh=mesh,
        in_specs=(P("rows", "cols"), P("cols", None), P("rows"), P(), P()),
        out_specs=(P(None, "cols"), P("rows", "cols")),
        check_vma=False,
    )
```
